128 devices in a mesh: dp: 32 (over y, x_hi, z), mp: 4 (over x_lo, core).
Axes of the slice: x: 4 (x_hi: 2, x_lo: 2; x = x_hi * 2 + x_lo), y: 4, z: 4, core: 2. Of those that a mesh axis runs over, the one named last changes fastest.
Arguments:
- tokens: bfloat16 [32, 224, 768], P('dp'), may hold values from -6 to 6
- lengths: int32 [32, 3], P('dp'), may hold values from 9 to 128, as said below
- partner: int32 [32], replicated, may hold values from 0 to 31, each once
- mix_coef: float32 [32], replicated, may hold values from 0.3 to 0.7
- norm_gain: float32 [4, 2, 768], replicated, may hold values from 0.5 to 1.5
- norm_bias: float32 [4, 2, 768], replicated, may hold values from -1.8 to 1.8
- w_qkv: bfloat16 [4, 768, 3, 768], P(None, None, None, 'mp'), may hold values from -0.21875 to 0.21875
- b_qv: float32 [4, 2, 768], P(None, None, 'mp'), may hold values from -1.8 to 1.8
- w_out: bfloat16 [4, 768, 768], P(None, 'mp'), may hold values from -1.25 to 1.25
- b_out: float32 [4, 768], replicated, may hold values from -1.8 to 1.8
- w_up: bfloat16 [4, 768, 3072], P(None, None, 'mp'), may hold values from -0.21875 to 0.21875
- b_up: float32 [4, 3072], P(None, 'mp'), may hold values from -1.8 to 1.8
- w_down: bfloat16 [4, 3072, 768], P(None, 'mp'), may hold values from -0.109375 to 0.109375
- b_down: float32 [4, 768], replicated, may hold values from -1.8 to 1.8
- cot_tokens: bfloat16 [32, 224, 768], P('dp'), may hold values from -6 to 6
- cot_global: bfloat16 [32, 3, 768], P('dp'), may hold values from -6 to 6
Outputs:
- out_tokens: bfloat16 [32, 224, 768], P('dp')
- out_global: bfloat16 [32, 3, 768], P('dp')
- grad_tokens: bfloat16 [32, 224, 768], P('dp')
- grad_norm_gain: float32 [4, 2, 768], P(None, None, 'mp')
- grad_norm_bias: float32 [4, 2, 768], P(None, None, 'mp')
- grad_w_qkv: float32 [4, 768, 3, 768], P(None, None, None, 'mp')
- grad_b_qv: float32 [4, 2, 768], P(None, None, 'mp')
- grad_w_out: float32 [4, 768, 768], P(None, 'mp')
- grad_b_out: float32 [4, 768], P(None, 'mp')
- grad_w_up: float32 [4, 768, 3072], P(None, None, 'mp')
- grad_b_up: float32 [4, 3072], P(None, 'mp')
- grad_w_down: float32 [4, 3072, 768], P(None, 'mp')
- grad_b_down: float32 [4, 768], P(None, 'mp')
The draws below stay inside these ranges and needn't reach their ends.
Inputs may be any that keep to these rules, and one draw needn't show every extreme that they name: lengths[c, v] counts the valid tokens of view v of clip c (class token included): view 0 from 33 to 128, view 1 from 17 to 64, view 2 from 9 to 32; in every draw at least one clip has all three views full.
All inputs are finite; a program needn't handle non-finite values.
Results may differ from the reference program's by a relative error of at most 0.028.
Values may be sent and summed in bfloat16 or wider, within the bound.
A program may use at most 192 MiB of HBM per device.

```python
import jax
import jax.numpy as jnp
from jax import lax

D = 768
HD = 64
FF = 3072
L1 = 128
L2 = 64
L3 = 32
CLIPS = 32
LT = 224


def draw_lengths(key, part):
    key = jax.random.fold_in(key, 11)
    first, second = jax.random.split(key)
    tops = jnp.array([L1, L2, L3], dtype=jnp.int32)
    lows = tops // 4 + 1
    raw = jax.random.randint(first, (CLIPS, 3), 0, 1 << 20, dtype=jnp.int32)
    picked = lows[None, :] + raw % (tops - lows + 1)[None, :]
    full = jax.random.randint(second, (), 0, CLIPS, dtype=jnp.int32)
    rows = jnp.arange(CLIPS, dtype=jnp.int32)[:, None]
    return jnp.where(rows == full, tops[None, :], picked).astype(jnp.int32)


def level_of(stream_key, extent, cuts, smallest, largest):
    def one(axis_at, blocks):
        heights = jax.random.uniform(jax.random.fold_in(jax.random.fold_in(stream_key, 6), axis_at), (blocks,), jnp.float32, smallest / len(cuts), largest / len(cuts))
        return jnp.repeat(jnp.exp(heights), extent[axis_at] // blocks).reshape((-1,) + (1,) * (len(extent) - axis_at - 1))

    loudness = one(*cuts[0])
    for cut in cuts[1:]:
        loudness = loudness * one(*cut)
    return loudness


def gaussian(rng, dims, deviation, limit, shards=(), kind=jnp.bfloat16):
    values = jax.random.normal(rng, dims, jnp.float32) * deviation
    if len(shards) > 0:
        values = level_of(rng, dims, shards, -0.22, 0.18) * values
    return jnp.clip(values, min=-limit, max=limit).astype(kind)


def setup_inputs(seed: int = 0) -> dict:
    key_of = jax.random.split(jax.random.key(seed), 17)
    tokens = gaussian(key_of[0], (CLIPS, LT, D), 1.0, 6.0, ((0, 32),))
    lengths = draw_lengths(jax.random.fold_in(key_of[16], 71), 0)
    partner = jax.random.permutation(key_of[2], CLIPS).astype(jnp.int32)
    mix_coef = jnp.clip(jax.random.uniform(key_of[3], (CLIPS,), jnp.float32, 0.3, 0.7), 0.3, 0.7)
    norm_gain = jnp.clip(1.0 + 0.1 * jax.random.normal(key_of[4], (4, 2, D), jnp.float32), 0.5, 1.5)
    norm_bias = gaussian(key_of[5], (4, 2, D), 0.3, 1.8, (), jnp.float32)
    w_qkv = gaussian(key_of[6], (4, D, 3, D), D ** -0.5, 0.21875, ((3, 4),))
    b_qv = gaussian(key_of[7], (4, 2, D), 0.3, 1.8, ((2, 4),), jnp.float32)
    w_out = gaussian(key_of[8], (4, D, D), (D // 32) ** -0.5, 1.25, ((1, 4),))
    b_out = gaussian(key_of[9], (4, D), 0.3, 1.8, (), jnp.float32)
    w_up = gaussian(key_of[10], (4, D, FF), D ** -0.5, 0.21875, ((2, 4),))
    b_up = gaussian(key_of[11], (4, FF), 0.3, 1.8, ((1, 4),), jnp.float32)
    w_down = gaussian(key_of[12], (4, FF, D), FF ** -0.5, 0.109375, ((1, 4),))
    b_down = gaussian(key_of[13], (4, D), 0.3, 1.8, (), jnp.float32)
    cot_tokens = gaussian(key_of[14], (CLIPS, LT, D), 1.0, 6.0, ((0, 32),))
    cot_global = gaussian(key_of[15], (CLIPS, 3, D), 1.0, 6.0, ((0, 32),))
    return {"tokens": tokens, "lengths": lengths, "partner": partner, "mix_coef": mix_coef, "norm_gain": norm_gain, "norm_bias": norm_bias, "w_qkv": w_qkv, "b_qv": b_qv, "w_out": w_out, "b_out": b_out, "w_up": w_up, "b_up": b_up, "w_down": w_down, "b_down": b_down, "cot_tokens": cot_tokens, "cot_global": cot_global}


@jax.custom_vjp
def low(v):
    return lax.optimization_barrier(v.astype(jnp.bfloat16)).astype(jnp.float32)

@jax.custom_vjp
def low_back(v):
    return v

def low_keep(v):
    return (low(v), None)

def low_pass(kept, grad):
    return (grad,)

def back_keep(v):
    return (v, None)

def back_low(kept, grad):
    return (low(grad),)
low.defvjp(low_keep, low_pass)
low_back.defvjp(back_keep, back_low)
EPS = 1e-06
NEG = -1000000000.0
HIGH = lax.Precision.HIGHEST

def layer_norm(x, gain, shift):
    center = x - lax.optimization_barrier(jnp.mean(x, -1, keepdims=True))
    spread = lax.optimization_barrier(jnp.mean(center * center, -1, keepdims=True))
    return center * lax.rsqrt(spread + EPS) * gain + shift

def softmax_rows(scores):
    top = lax.optimization_barrier(jnp.max(scores, -1, keepdims=True))
    expo = jnp.exp(scores - top)
    return expo / lax.optimization_barrier(jnp.sum(expo, -1, keepdims=True))

def block(x, valid, params):
    gain, shift, wqkv, bqv, wout, bout, wup, bup, wdown, bdown = params
    batch, span = valid.shape
    heads = wqkv.shape[-1] // HD
    scale = HD ** (-0.5)
    normed = low(layer_norm(x, gain[0], shift[0]))
    proj = jnp.einsum('bsd,dtk->bstk', normed, wqkv, precision=HIGH)
    query = low(low_back(proj[:, :, 0] + bqv[0])).reshape(batch, span, heads, HD)
    keys = low(low_back(proj[:, :, 1])).reshape(batch, span, heads, HD)
    values = low(low_back(proj[:, :, 2] + bqv[1])).reshape(batch, span, heads, HD)
    scores = low_back(jnp.einsum('bqhe,bkhe->bhqk', query, keys, precision=HIGH) * scale)
    scores = jnp.where(valid[:, None, None, :], scores, NEG)
    light = low(softmax_rows(scores))
    mixed_heads = jnp.einsum('bhqk,bkhe->bqhe', light, values, precision=HIGH)
    heads_out = low(low_back(mixed_heads.reshape(batch, span, heads * HD)))
    after = x + low_back(jnp.einsum('bsk,kd->bsd', heads_out, wout, precision=HIGH)) + bout
    normed2 = low(layer_norm(after, gain[1], shift[1]))
    inner = low_back(jnp.einsum('bsd,df->bsf', normed2, wup, precision=HIGH) + bup)
    active = low(jax.nn.gelu(inner))
    return after + low_back(jnp.einsum('bsf,fd->bsd', active, wdown, precision=HIGH)) + bdown

def reference(tokens, lengths, partner, mix_coef, norm_gain, norm_bias, w_qkv, b_qv, w_out, b_out, w_up, b_up, w_down, b_down, cot_tokens, cot_global):
    weights = tuple((w.astype(jnp.float32) for w in (norm_gain, norm_bias, w_qkv, b_qv, w_out, b_out, w_up, b_up, w_down, b_down)))
    spans = (L1, L2, L3)

    def forward(x, stack):
        lam = mix_coef.astype(jnp.float32)[:, None, None]
        mixed = lam * x + (1.0 - lam) * x[partner]
        pieces = []
        classes = []
        start = 0
        for view in range(3):
            width = spans[view]
            rows = mixed[:, start:start + width]
            valid = jnp.arange(width, dtype=jnp.int32)[None, :] < lengths[:, view:view + 1]
            result = block(rows, valid, tuple((p[view] for p in stack)))
            pieces.append(result)
            classes.append(result[:, 0])
            start = start + width
        view_out = jnp.concatenate(pieces, 1)
        gin = jnp.stack(classes, 1).reshape(1, CLIPS * 3, D)
        every = jnp.ones((1, CLIPS * 3), dtype=bool)
        glob = block(gin, every, tuple((p[3] for p in stack))).reshape(CLIPS, 3, D)
        return (view_out, glob)
    outs, pull = jax.vjp(forward, tokens.astype(jnp.float32), weights)
    dtokens, grads = pull((cot_tokens.astype(jnp.float32), cot_global.astype(jnp.float32)))
    return (outs[0].astype(jnp.bfloat16), outs[1].astype(jnp.bfloat16), dtokens.astype(jnp.bfloat16), grads[0], grads[1], grads[2], grads[3], grads[4], grads[5], grads[6], grads[7], grads[8], grads[9])
```

```python
import functools

import jax
import jax.numpy as jnp
from jax import lax
from jax.experimental import pallas as pl
from jax.experimental.pallas import tpu as pltpu
from jax.sharding import PartitionSpec as P

HD = 64
D = 768
KD = 192
SPANS = (128, 64, 32, 96)
SLABS = (32, 16, 8, 24)
OFFS = (0, 128, 192)
CLIPS = 32
PIECES = 21
EPS = 1e-06
NEG = -1000000000.0
MESH = pl.DeviceIdType.MESH
BF = jnp.bfloat16
F32 = jnp.float32
UNITS = (
    ("down", 0, "yz"),
    ("up", 0, "xyz"),
    ("down", 1, "zy"),
    ("up", 1, "xzy"),
    ("down", 2, "yz"),
    ("up", 2, "xyz"),
    ("qo", 0, "zy"),
    ("qo", 1, "xzy"),
    ("qo", 2, "yz"),
)
UNIT_OF = {(name, view): place for place, (name, view, _) in enumerate(UNITS)}
FLAT = [place for place, unit in enumerate(UNITS) if len(unit[2]) == 2]
SPLIT = [place for place, unit in enumerate(UNITS) if len(unit[2]) == 3]
OUT_OF = {"qo": 0, "up": 1, "down": 2}


def nn(a, b):
    return lax.dot_general(a, b, (((1,), (0,)), ((), ())), preferred_element_type=F32)


def nt(a, b):
    return lax.dot_general(a, b, (((1,), (1,)), ((), ())), preferred_element_type=F32)


def tn(a, b):
    return lax.dot_general(a, b, (((0,), (0,)), ((), ())), preferred_element_type=F32)


def layer_stats(x):
    center = x - jnp.mean(x, -1, keepdims=True)
    spread = jnp.mean(center * center, -1, keepdims=True)
    inv = lax.rsqrt(spread + EPS)
    return center * inv, inv


def scratch_plan():
    plan = {}
    for i in range(4):
        span, slab = SPANS[i], SLABS[i]
        for name in ("n1", "s1", "n2", "s2", "zo", "s3", "da", "s4"):
            plan[name, i] = pltpu.VMEM((4, slab, D), BF)
        for name in ("r1", "r2", "r3", "r4"):
            plan[name, i] = pltpu.VMEM((3, slab, D), BF)
        for name in ("x", "af", "daf"):
            plan[name, i] = pltpu.VMEM((slab, D), F32)
        plan["dz", i] = pltpu.VMEM((4, slab, D), F32)
        for name in ("q", "k", "v", "ho"):
            plan[name, i] = pltpu.VMEM((span, KD), BF)
        plan["pr", i] = pltpu.VMEM((3 * span, span), F32)
        plan["dg", i] = pltpu.VMEM((span, D), F32)
        plan["ac", i] = pltpu.VMEM((span, D), BF)
        plan["wq", i] = pltpu.VMEM((3 * KD, D), BF)
        plan["wo", i] = pltpu.VMEM((KD, D), BF)
        plan["wu", i] = pltpu.VMEM((D, D), BF)
        plan["wd", i] = pltpu.VMEM((D, D), BF)
        if i < 3:
            plan["gt", i] = pltpu.VMEM((4, slab, D), BF)
    for turn in range(2):
        plan["pa", turn] = pltpu.VMEM((CLIPS, 8, 256), BF)
        plan["pb", turn] = pltpu.VMEM((CLIPS, 8, 256), BF)
        plan["pc", turn] = pltpu.VMEM((PIECES, 8, 256), BF)
    plan["ts"] = pltpu.VMEM((7, 8, D), BF)
    plan["mx"] = pltpu.VMEM((7, 8, D), F32)
    plan["cl"] = pltpu.VMEM((8, D), BF)
    plan["cg"] = pltpu.VMEM((CLIPS, 8, D), BF)
    plan["ct"] = pltpu.VMEM((CLIPS, 8, D), BF)
    plan["gin"] = pltpu.VMEM((4, 24, D), F32)
    plan["gdx"] = pltpu.VMEM((4, 24, D), BF)
    plan["go"] = pltpu.VMEM((3, 16, 48, D), BF)
    plan["g"] = pltpu.VMEM((len(FLAT), 16, 48, D), BF)
    plan["g1"] = pltpu.VMEM((len(FLAT), 3, 4, 48, D), BF)
    plan["g2"] = pltpu.VMEM((len(FLAT), 3, 48, D), BF)
    plan["gx"] = pltpu.VMEM((len(FLAT), 2, 48, D), BF)
    plan["ga"] = pltpu.VMEM((len(FLAT), 4, 48, D), BF)
    plan["h"] = pltpu.VMEM((len(SPLIT), 2, 16, 48, 384), BF)
    plan["hx"] = pltpu.VMEM((len(SPLIT), 16, 48, 384), BF)
    plan["h1"] = pltpu.VMEM((len(SPLIT), 3, 4, 48, 384), BF)
    plan["h2"] = pltpu.VMEM((len(SPLIT), 3, 48, 384), BF)
    plan["ha"] = pltpu.VMEM((len(SPLIT), 16, 48, 384), BF)
    plan["sva"] = pltpu.VMEM((16, D), F32)
    plan["svb"] = pltpu.VMEM((16, D), F32)
    plan["svr"] = pltpu.VMEM((3, 16, D), F32)
    for step in range(3):
        plan["svs", step] = pltpu.VMEM((32, D), BF)
        plan["svt", step] = pltpu.VMEM((3, 32, D), BF)
    plan["ssem"] = pltpu.SemaphoreType.DMA((160,))
    plan["rsem"] = pltpu.SemaphoreType.DMA((160,))
    plan["lsem"] = pltpu.SemaphoreType.DMA((48,))
    return plan


def kernel(names, *refs):
    (
        partner,
        inverse,
        mix,
        lengths,
        tok,
        cot,
        cotg,
        gain,
        shift,
        b_out,
        b_down,
        b_up,
        b_qv,
        wq_all,
        wo_all,
        wu_all,
        wd_all,
        out_tok,
        out_glob,
        out_grad,
        out_small,
        out_qo,
        out_up,
        out_down,
    ) = refs[:24]
    b = dict(zip(names, refs[24:]))
    ssem, rsem, lsem = b["ssem"], b["rsem"], b["lsem"]
    outs = {"qo": out_qo, "up": out_up, "down": out_down}
    me = lax.axis_index("dp")
    m = lax.axis_index("mp")
    place = {"y": lax.div(me, 8), "x": lax.rem(lax.div(me, 4), 2), "z": lax.rem(me, 4)}

    def at(**moved):
        p = dict(place)
        p.update(moved)
        return ((p["y"] * 2 + p["x"]) * 4 + p["z"], m)

    count = {"s": 0, "l": 0}
    drains = []

    def new(kind):
        count[kind] += 1
        return count[kind] - 1

    def send(src, dst, s, dev):
        pltpu.make_async_remote_copy(
            src_ref=src,
            dst_ref=dst,
            send_sem=ssem.at[s],
            recv_sem=rsem.at[s],
            device_id=dev,
            device_id_type=MESH,
        ).start()

    def wait(like, sem):
        pltpu.make_async_copy(like, like, sem).wait()

    def landed(like, s):
        wait(like, rsem.at[s])
        drains.append((like, s))

    barrier = pltpu.get_barrier_semaphore()

    def greet(k, _):
        pl.semaphore_signal(
            barrier, inc=1, device_id=(lax.rem(me + k, CLIPS), m), device_id_type=MESH
        )
        return 0

    lax.fori_loop(1, CLIPS, greet, 0)
    for k in (1, 2, 3):
        pl.semaphore_signal(barrier, inc=1, device_id=(me, lax.rem(m + k, 4)), device_id_type=MESH)

    fetch = {}
    for i in range(4):
        for name, src in (("wq", wq_all), ("wo", wo_all), ("wu", wu_all), ("wd", wd_all)):
            copy = pltpu.make_async_copy(src.at[i], b[name, i], lsem.at[new("l")])
            copy.start()
            fetch[name, i] = copy

    def weight(name, i):
        if (name, i) in fetch:
            fetch.pop((name, i)).wait()
        return b[name, i]

    pl.semaphore_wait(barrier, CLIPS - 1 + 3)

    def gather_start(buf):
        s = new("s")
        for k in (2, 1, 3):
            send(buf.at[m], buf.at[m], s, (me, lax.rem(m + k, 4)))
        return buf.at[pl.ds(0, 3)], s

    def scatter_start(src, dst):
        s = new("s")
        for k in (2, 1, 3):
            t = lax.rem(m + k, 4)
            send(src.at[t], dst.at[k - 1], s, (me, t))
        return dst, s

    def dp_gather_start(src, dst):
        s = new("s")

        def step(k, _):
            send(src, dst.at[me], s, (lax.rem(me + k, CLIPS), m))
            return 0

        lax.fori_loop(1, CLIPS, step, 0)
        dst[me] = src[...]
        return dst.at[pl.ds(0, CLIPS - 1)], s

    def rows_of(buf, i):
        span, slab = SPANS[i], SLABS[i]
        if slab % 16 == 0:
            return buf[...].reshape(span, D)
        return buf[...].astype(F32).reshape(span, D).astype(BF)

    groups = [m * 4 + r for r in range(4)] + [16 + m * 2 + r for r in range(2)] + [24 + m]

    def deal_start(turn, src_at):
        keep = b["pa", turn]
        s = new("s")
        for j in range(PIECES):

            @pl.when(me != j)
            def _():
                send(src_at(j // 3).at[:, pl.ds((j % 3) * 256, 256)], keep.at[me], s, (j, m))

            @pl.when(me == j)
            def _():
                keep[me] = src_at(j // 3)[:, (j % 3) * 256 : (j % 3) * 256 + 256]

        return s

    def few_or_all(buf, sem):
        @pl.when(me < PIECES)
        def _():
            wait(buf.at[pl.ds(0, PIECES - 1)], sem)

        @pl.when(me >= PIECES)
        def _():
            wait(buf, sem)

    def deal_turn(turn, s, index):
        keep, stage, got = b["pa", turn], b["pb", turn], b["pc", turn]
        t = new("s")

        @pl.when(me < PIECES)
        def _():
            wait(keep.at[pl.ds(0, CLIPS - 1)], rsem.at[s])
            for d in range(CLIPS):
                stage[d] = keep[index[d]]
            got[me] = stage[me]

            def step(k, _):
                d = lax.rem(me + k, CLIPS)
                send(stage.at[d], got.at[me], t, (d, m))
                return 0

            lax.fori_loop(1, CLIPS, step, 0)

        few_or_all(got, ssem.at[s])
        return t

    def deal_end(turn, t):
        stage, got = b["pb", turn], b["pc", turn]
        few_or_all(got, rsem.at[t])

        @pl.when(me < PIECES)
        def _():
            wait(stage.at[pl.ds(0, CLIPS - 1)], ssem.at[t])

        return [
            jnp.concatenate([got[3 * r + c].astype(F32) for c in range(3)], 1) for r in range(7)
        ]

    lam = mix[me]
    s = deal_start(0, lambda r: tok.at[groups[r]])
    cot_ticket = dp_gather_start(cotg, b["ct"])
    t = deal_turn(0, s, partner)
    taken = deal_end(0, t)
    for r in range(7):
        value = lam * tok[groups[r]].astype(F32) + (1.0 - lam) * taken[r]
        if r < 4:
            b["x", 0][8 * r : 8 * r + 8] = value
        elif r < 6:
            b["x", 1][8 * (r - 4) : 8 * (r - 4) + 8] = value
        else:
            b["x", 2][...] = value

    def vec(ref, row):
        return ref[row : row + 1, :]

    def norm(x, i, j):
        hat, _ = layer_stats(x)
        return hat * vec(gain, 2 * i + j) + vec(shift, 2 * i + j)

    def head_mask(h):
        lane = lax.broadcasted_iota(jnp.int32, (1, KD), 1)
        return (lane >= h * HD) & (lane < h * HD + HD)

    masks = [head_mask(h) for h in range(3)]
    zero = jnp.zeros((), BF)

    def stacked(a):
        return jnp.concatenate(
            [jnp.where(masks[h], a.astype(F32), 0.0) for h in range(3)], 0
        ).astype(BF)

    def folded(a, span):
        total = None
        for h in range(3):
            part = jnp.where(masks[h], a[h * span : (h + 1) * span], 0.0)
            total = part if total is None else total + part
        return total

    scale = HD ** (-0.5)

    def attend(i):
        span = SPANS[i]
        normed = rows_of(b["n1", i], i)
        wq = weight("wq", i)
        query = (nt(normed, wq[0:KD]) + vec(b_qv, 2 * i)).astype(BF)
        keys = nt(normed, wq[KD : 2 * KD]).astype(BF)
        values = (nt(normed, wq[2 * KD : 3 * KD]) + vec(b_qv, 2 * i + 1)).astype(BF)
        b["q", i][...] = query
        b["k", i][...] = keys
        b["v", i][...] = values
        scores = nt(stacked(query), keys) * scale
        if i < 3:
            col = lax.broadcasted_iota(jnp.int32, (1, span), 1)
            scores = jnp.where(col < lengths[0, i], scores, NEG)
        expo = jnp.exp(scores - jnp.max(scores, -1, keepdims=True))
        probs = expo / jnp.sum(expo, -1, keepdims=True)
        b["pr", i][...] = probs
        heads_out = folded(nn(probs.astype(BF), values), span).astype(BF)
        b["ho", i][...] = heads_out
        part = nn(heads_out, weight("wo", i)[...])
        b["s1", i][...] = part.astype(BF).reshape(4, SLABS[i], D) if SLABS[i] % 16 == 0 else (
            part.reshape(4, SLABS[i], D).astype(BF)
        )
        return scatter_start(b["s1", i], b["r1", i])

    def put_slabs(name, i, value):
        b[name, i][...] = value.reshape(4, SLABS[i], D).astype(BF)

    def summed(send_name, recv_name, i, ticket):
        landed(*ticket)
        got = b[recv_name, i]
        total = b[send_name, i][m].astype(F32)
        for k in range(3):
            total = total + got[k].astype(F32)
        return total

    def middle(i, ticket):
        after = b["x", i][...] + summed("s1", "r1", i, ticket) + vec(b_out, i)
        b["af", i][...] = after
        b["n2", i][m] = norm(after, i, 1).astype(BF)
        return gather_start(b["n2", i])

    def feed(i, ticket):
        landed(*ticket)
        normed2 = rows_of(b["n2", i], i)
        inner = nn(normed2, weight("wu", i)[...]) + vec(b_up, i)
        c0, c1 = 0.7978845608028654, 0.044715
        square = inner * inner
        th = jnp.tanh(c0 * inner * (1.0 + c1 * square))
        half = 0.5 * (1.0 + th)
        active = (inner * half).astype(BF)
        b["dg", i][...] = half + 0.5 * inner * (1.0 - th * th) * c0 * (1.0 + 3.0 * c1 * square)
        b["ac", i][...] = active
        put_slabs("s2", i, nn(active, weight("wd", i)[...]))
        return scatter_start(b["s2", i], b["r2", i])

    def finish(i, ticket):
        total = b["af", i][...] + summed("s2", "r2", i, ticket) + vec(b_down, i)
        b["zo", i][m] = total.astype(BF)
        return gather_start(b["zo", i])

    tickets = [None] * 3
    for i in range(3):
        b["n1", i][m] = norm(b["x", i][...], i, 0).astype(BF)
        tickets[i] = gather_start(b["n1", i])
    for i in range(3):
        landed(*tickets[i])
        tickets[i] = attend(i)
    for i in range(3):
        tickets[i] = middle(i, tickets[i])
    for i in range(3):
        tickets[i] = feed(i, tickets[i])
    for i in range(3):
        tickets[i] = finish(i, tickets[i])
    row8 = lax.broadcasted_iota(jnp.int32, (8, 1), 0)
    classes = jnp.zeros((8, D), F32)
    for i in range(3):
        landed(*tickets[i])
        first = b["zo", i][0].astype(F32)[0:1]
        classes = jnp.where(row8 == i, first, classes)
    b["cl"][...] = classes.astype(BF)
    ticket = dp_gather_start(b["cl"], b["cg"])
    for i in range(3):
        out_tok[OFFS[i] : OFFS[i] + SPANS[i]] = rows_of(b["zo", i], i)

    r_at = lax.broadcasted_iota(jnp.int32, (96, 256), 0)
    k_at = lax.broadcasted_iota(jnp.int32, (96, 256), 1)
    pick = (k_at == lax.rem(r_at, 32) * 8 + lax.div(r_at, 32)).astype(F32).astype(BF)

    def class_rows(buf):
        return nn(pick, buf[...].astype(F32).reshape(256, D).astype(BF))

    landed(*ticket)
    gin = class_rows(b["cg"])
    b["gin"][...] = gin.reshape(4, 24, D)
    b["x", 3][...] = b["gin"][m]
    put_slabs("n1", 3, norm(gin, 3, 0))
    ticket = attend(3)
    ticket = middle(3, ticket)
    ticket = feed(3, ticket)
    glob_ticket = finish(3, ticket)
    landed(*cot_ticket)
    b["dz", 3][...] = class_rows(b["ct"]).reshape(4, 24, D)

    def put_unit(name, i, row, value):
        value = value.astype(BF)
        chunks = value.shape[0] // 48
        lo = row // 48
        if i == 3:
            b["go"][OUT_OF[name], lo : lo + chunks] = value.reshape(chunks, 48, D)
            return
        u = UNIT_OF[name, i]
        if u in FLAT:
            b["g"][FLAT.index(u), lo : lo + chunks] = value.reshape(chunks, 48, D)
        else:
            for half in range(2):
                b["h"][SPLIT.index(u), half, lo : lo + chunks] = value[
                    :, half * 384 : half * 384 + 384
                ].reshape(chunks, 48, 384)

    def back_feed(i):
        span = SPANS[i]
        dz = b["dz", i][...].reshape(span, D)
        b["svb"][4 * i : 4 * i + 1] = jnp.sum(dz, 0, keepdims=True)
        dm = dz.astype(BF)
        for part in range(2):
            cols = slice(part * 384, part * 384 + 384)
            put_unit("down", i, part * 384, tn(b["ac", i][:, cols], dm))
        start_unit("down", i)
        dact = nt(dm, weight("wd", i)[...])
        dinner = (b["dg", i][...] * dact).astype(BF)
        put_slabs("s3", i, nt(dinner, weight("wu", i)[...]))
        ticket = scatter_start(b["s3", i], b["r3", i])
        b["svb"][4 * i + 2 : 4 * i + 3] = jnp.sum(dinner.astype(F32), 0, keepdims=True)
        normed2 = rows_of(b["n2", i], i)
        for part in range(2):
            cols = slice(part * 384, part * 384 + 384)
            put_unit("up", i, part * 384, tn(normed2[:, cols], dinner))
        start_unit("up", i)
        return ticket

    def norm_back(x, dy, i, j):
        hat, inv = layer_stats(x)
        b["sva"][4 * i + 2 * j : 4 * i + 2 * j + 1] = jnp.sum(dy * hat, 0, keepdims=True)
        b["sva"][4 * i + 2 * j + 1 : 4 * i + 2 * j + 2] = jnp.sum(dy, 0, keepdims=True)
        g = dy * vec(gain, 2 * i + j)
        return inv * (
            g - jnp.mean(g, -1, keepdims=True) - hat * jnp.mean(g * hat, -1, keepdims=True)
        )

    def back_middle(i, ticket):
        dn2 = summed("s3", "r3", i, ticket)
        dafter = b["dz", i][m] + norm_back(b["af", i][...], dn2, i, 1)
        b["daf", i][...] = dafter
        b["da", i][m] = dafter.astype(BF)
        return gather_start(b["da", i])

    def back_attend(i, ticket):
        span = SPANS[i]
        landed(*ticket)
        da = rows_of(b["da", i], i)
        b["svb"][4 * i + 1 : 4 * i + 2] = jnp.sum(da.astype(F32), 0, keepdims=True)
        dheads = nt(da, weight("wo", i)[...]).astype(BF)
        query, keys, values = b["q", i][...], b["k", i][...], b["v", i][...]
        probs = b["pr", i][...]
        d3 = stacked(dheads)
        dprob = nt(d3, values)
        dscore = probs * (dprob - jnp.sum(dprob * probs, -1, keepdims=True))
        dscore = dscore.astype(BF)
        dquery = (folded(nn(dscore, keys), span) * scale).astype(BF)
        dkeys = (tn(dscore, stacked(query)) * scale).astype(BF)
        dvalues = tn(probs.astype(BF), d3).astype(BF)
        wq = weight("wq", i)
        part = nn(dquery, wq[0:KD]) + nn(dkeys, wq[KD : 2 * KD]) + nn(dvalues, wq[2 * KD : 3 * KD])
        put_slabs("s4", i, part)
        ticket = scatter_start(b["s4", i], b["r4", i])
        b["svb"][4 * i + 3 : 4 * i + 4, 0:KD] = jnp.sum(dquery.astype(F32), 0, keepdims=True)
        b["svb"][4 * i + 3 : 4 * i + 4, 256 : 256 + KD] = jnp.sum(
            dvalues.astype(F32), 0, keepdims=True
        )
        normed = rows_of(b["n1", i], i)
        put_unit("qo", i, 0, tn(dquery, normed))
        put_unit("qo", i, KD, tn(dkeys, normed))
        put_unit("qo", i, 2 * KD, tn(dvalues, normed))
        put_unit("qo", i, 3 * KD, tn(b["ho", i][...], da))
        start_unit("qo", i)
        return ticket

    def back_finish(i, ticket):
        dn1 = summed("s4", "r4", i, ticket)
        return b["daf", i][...] + norm_back(b["x", i][...], dn1, i, 0)

    def flat_unit(u):
        name, view, axes = UNITS[u]
        f = FLAT.index(u)
        g, g1, g2, gx = b["g"].at[f], b["g1"].at[f], b["g2"].at[f], b["gx"].at[f]
        one, two = axes
        p1, p2 = place[one], place[two]
        s = new("s")
        for k in (1, 3, 2):
            t = lax.rem(p1 + k, 4)
            send(g.at[pl.ds(t * 4, 4)], g1.at[k - 1], s, at(**{one: t}))
        yield
        landed(g1, s)
        for c in range(4):
            total = g[p1 * 4 + c].astype(F32)
            for k in range(3):
                total = total + g1[k, c].astype(F32)
            g[p1 * 4 + c] = total.astype(BF)
        s = new("s")
        for k in (1, 3, 2):
            t = lax.rem(p2 + k, 4)
            send(g.at[p1 * 4 + t], g2.at[k - 1], s, at(**{two: t}))
        yield
        landed(g2, s)
        total = g[p1 * 4 + p2].astype(F32)
        for k in range(3):
            total = total + g2[k].astype(F32)
        gx[0] = total.astype(BF)
        s = new("s")
        send(gx.at[0], gx.at[1], s, at(x=1 - place["x"]))
        yield
        landed(gx.at[1], s)
        ga, out = b["ga"].at[f], outs[name].at[view]
        ga[p2] = (gx[0].astype(F32) + gx[1].astype(F32)).astype(BF)
        s = new("s")
        for k in (1, 3, 2):
            send(ga.at[p2], ga.at[p2], s, at(**{two: lax.rem(p2 + k, 4)}))
        yield
        landed(ga.at[pl.ds(0, 3)], s)
        s = new("s")
        own = out.at[pl.ds(p1 * 4, 4)]
        for k in (1, 3, 2):
            send(ga, own, s, at(**{one: lax.rem(p1 + k, 4)}))
        store(ga, own)
        yield
        landed(out.at[pl.ds(0, 12)], s)

    def split_unit(u):
        name, view, axes = UNITS[u]
        f = SPLIT.index(u)
        h, hx, h1, h2 = b["h"].at[f], b["hx"].at[f], b["h1"].at[f], b["h2"].at[f]
        one, two = axes[1:]
        p1, p2, px = place[one], place[two], place["x"]
        s = new("s")
        send(h.at[1 - px], hx, s, at(x=1 - px))
        yield
        landed(hx, s)
        for c in range(16):
            h[px, c] = (h[px, c].astype(F32) + hx[c].astype(F32)).astype(BF)
        g = h.at[px]
        s = new("s")
        for k in (1, 3, 2):
            t = lax.rem(p1 + k, 4)
            send(g.at[pl.ds(t * 4, 4)], h1.at[k - 1], s, at(**{one: t}))
        yield
        landed(h1, s)
        for c in range(4):
            total = h[px, p1 * 4 + c].astype(F32)
            for k in range(3):
                total = total + h1[k, c].astype(F32)
            h[px, p1 * 4 + c] = total.astype(BF)
        s = new("s")
        for k in (1, 3, 2):
            t = lax.rem(p2 + k, 4)
            send(g.at[p1 * 4 + t], h2.at[k - 1], s, at(**{two: t}))
        yield
        landed(h2, s)
        mine = p1 * 4 + p2
        total = h[px, mine].astype(F32)
        for k in range(3):
            total = total + h2[k].astype(F32)
        ha, out = b["ha"].at[f], outs[name].at[view, :, :, pl.ds(px * 384, 384)]
        ha[mine] = total.astype(BF)
        s = new("s")
        for k in (1, 3, 2):
            send(ha.at[mine], ha.at[mine], s, at(**{two: lax.rem(p2 + k, 4)}))
        yield
        landed(ha.at[pl.ds(0, 3)], s)
        s = new("s")
        own = ha.at[pl.ds(p1 * 4, 4)]
        for k in (1, 3, 2):
            send(own, own, s, at(**{one: lax.rem(p1 + k, 4)}))
        yield
        landed(ha.at[pl.ds(0, 12)], s)
        s = new("s")
        send(ha, out, s, at(x=1 - px))
        store(ha, out)
        yield
        landed(out, s)

    stores = []

    def store(src, dst):
        copy = pltpu.make_async_copy(src, dst, lsem.at[new("l")])
        copy.start()
        stores.append(copy)

    running = []

    def start_unit(name, i):
        if i == 3:
            store(b["go"].at[OUT_OF[name]], outs[name].at[3])
            return
        u = UNIT_OF[name, i]
        unit = flat_unit(u) if u in FLAT else split_unit(u)
        next(unit)
        running.append(unit)

    def advance(some):
        for unit in some:
            if unit in running and next(unit, "end") == "end":
                running.remove(unit)

    ticket = back_feed(3)
    ticket = back_middle(3, ticket)
    ticket = back_attend(3, ticket)
    dx = back_finish(3, ticket)
    b["gdx"][m] = dx.astype(BF)
    ticket = gather_start(b["gdx"])
    landed(*glob_ticket)
    o_at = lax.broadcasted_iota(jnp.int32, (8, 96), 0)
    w_at = lax.broadcasted_iota(jnp.int32, (8, 96), 1)
    mine = ((w_at == o_at * 32 + me) & (o_at < 3)).astype(F32).astype(BF)
    out_glob[...] = nn(mine, rows_of(b["zo", 3], 3)).astype(BF)
    landed(*ticket)
    dgin = nn(mine, rows_of(b["gdx"], 3))

    for i in range(3):
        dz = cot[OFFS[i] : OFFS[i] + SPANS[i]].astype(F32)
        row = lax.broadcasted_iota(jnp.int32, (SPANS[i], 1), 0)
        dz = dz + jnp.where(row == 0, dgin[i : i + 1], 0.0)
        b["dz", i][...] = dz.reshape(4, SLABS[i], D)
        tickets[i] = back_feed(i)
    for i in range(3):
        tickets[i] = back_middle(i, tickets[i])
    for i in range(3):
        tickets[i] = back_attend(i, tickets[i])
    for i in range(3):
        dx = back_finish(i, tickets[i])
        base = (0, 4, 6)[i]
        for r in range(SLABS[i] // 8):
            rows = dx[8 * r : 8 * r + 8]
            b["mx"][base + r] = lam * rows
            b["ts"][base + r] = ((1.0 - lam) * rows).astype(BF)
    order = list(running)
    s = deal_start(1, lambda r: b["ts"].at[r])

    s_mp = new("s")
    for k in (2, 1, 3):
        send(b["sva"], b["svr"].at[k - 1], s_mp, (me, lax.rem(m + k, 4)))
    advance(order[:3])
    t = deal_turn(1, s, inverse)
    advance(order[3:6])
    landed(b["svr"], s_mp)
    sva = b["sva"][...] + b["svr"][0] + b["svr"][1] + b["svr"][2]
    svb = b["svb"][...]
    b["svs", 0][...] = jnp.concatenate([sva, svb], 0).astype(BF)

    def small_start(step, axis):
        s = new("s")
        far = (1, 3, 2) if axis != "x" else (1,)
        size = 4 if axis != "x" else 2
        for k in far:
            dev = at(**{axis: lax.rem(place[axis] + k, size)})
            send(b["svs", step], b["svt", step].at[k - 1], s, dev)
        return b["svt", step].at[pl.ds(0, len(far))], s

    def small_end(step, ticket, axis):
        landed(*ticket)
        total = b["svs", step][...].astype(F32)
        for k in range(3 if axis != "x" else 1):
            total = total + b["svt", step][k].astype(F32)
        return total

    ticket = small_start(0, "y")
    taken = deal_end(1, t)
    for i in range(3):
        base = (0, 4, 6)[i]
        for r in range(SLABS[i] // 8):
            rows = b["mx"][base + r] + taken[base + r]
            b["gt", i][m, 8 * r : 8 * r + 8] = rows.astype(BF)
        tickets[i] = gather_start(b["gt", i])
    advance(order[:3])
    b["svs", 1][...] = small_end(0, ticket, "y").astype(BF)
    ticket = small_start(1, "z")
    advance(order[3:6])
    for i in range(3):
        landed(*tickets[i])
        out_grad[OFFS[i] : OFFS[i] + SPANS[i]] = rows_of(b["gt", i], i)
    b["svs", 2][...] = small_end(1, ticket, "z").astype(BF)
    ticket = small_start(2, "x")
    advance(order)
    total = small_end(2, ticket, "x")
    out_small[0:12] = total[0:12]
    out_small[12:16] = sva[12:16]
    out_small[16:28] = total[16:28]
    out_small[28:32] = svb[12:16]
    while running:
        advance(list(running))
    for like, s in drains:
        wait(like, ssem.at[s])
    for copy in stores:
        copy.wait()


def shards(
    tokens,
    lengths,
    partner,
    mix_coef,
    norm_gain,
    norm_bias,
    w_qkv,
    b_qv,
    w_out,
    b_out,
    w_up,
    b_up,
    w_down,
    b_down,
    cot_tokens,
    cot_global,
):
    ids = jnp.arange(CLIPS, dtype=jnp.int32)
    inverse = jnp.sum(jnp.where(partner[:, None] == ids[None, :], ids[:, None], 0), 0)
    wq = jnp.transpose(w_qkv, (0, 2, 3, 1)).reshape(4, 3 * KD, D)
    cotg = jnp.pad(cot_global[0], ((0, 5), (0, 0)))
    plan = scratch_plan()
    names = list(plan)
    smem = pl.BlockSpec(memory_space=pltpu.SMEM)
    vmem = pl.BlockSpec(memory_space=pltpu.VMEM)
    hbm = pl.BlockSpec(memory_space=pl.ANY)
    unit = jax.ShapeDtypeStruct((4, 16, 48, D), BF)
    out_tok, out_glob, out_grad, small, qo, up, down = pl.pallas_call(
        functools.partial(kernel, names),
        out_shape=(
            jax.ShapeDtypeStruct((224, D), BF),
            jax.ShapeDtypeStruct((8, D), BF),
            jax.ShapeDtypeStruct((224, D), BF),
            jax.ShapeDtypeStruct((32, D), F32),
            unit,
            unit,
            unit,
        ),
        in_specs=[smem] * 4 + [vmem] * 9 + [hbm] * 4,
        out_specs=(vmem,) * 4 + (hbm,) * 3,
        scratch_shapes=list(plan.values()),
        compiler_params=pltpu.CompilerParams(
            collective_id=0, has_side_effects=True, vmem_limit_bytes=60 * 2**20
        ),
    )(
        partner,
        inverse,
        mix_coef,
        lengths,
        tokens.reshape(28, 8, D),
        cot_tokens[0],
        cotg,
        norm_gain.reshape(8, D),
        norm_bias.reshape(8, D),
        b_out,
        b_down,
        b_up,
        b_qv.reshape(8, KD),
        wq,
        w_out,
        w_up,
        w_down,
    )
    qo = qo.reshape(4, D, D)
    sva = small[0:16].reshape(4, 4, D)
    svb = small[16:32].reshape(4, 4, D)
    offset = lax.axis_index("mp") * KD
    mine = lax.dynamic_slice_in_dim(sva, offset, KD, 2)
    mine_b = lax.dynamic_slice_in_dim(svb, offset, KD, 2)
    return (
        out_tok[None],
        out_glob[None, 0:3],
        out_grad[None],
        mine[:, 0::2],
        mine[:, 1::2],
        jnp.transpose(qo[:, : 3 * KD].astype(F32).reshape(4, 3, KD, D), (0, 3, 1, 2)),
        jnp.stack([svb[:, 3, 0:KD], svb[:, 3, 256 : 256 + KD]], 1),
        qo[:, 3 * KD :].astype(F32),
        mine_b[:, 1],
        up.reshape(4, D, D).astype(F32),
        svb[:, 2],
        down.reshape(4, D, D).astype(F32),
        mine_b[:, 0],
    )


def solution(mesh):
    placed = (
        P("dp", None, None),
        P("dp", None),
        P(),
        P(),
        P(),
        P(),
        P(None, None, None, "mp"),
        P(None, None, "mp"),
        P(None, "mp", None),
        P(),
        P(None, None, "mp"),
        P(None, "mp"),
        P(None, "mp", None),
        P(),
        P("dp", None, None),
        P("dp", None, None),
    )
    return jax.shard_map(
        shards,
        mesh=mesh,
        in_specs=placed,
        out_specs=(
            P("dp", None, None),
            P("dp", None, None),
            P("dp", None, None),
            P(None, None, "mp"),
            P(None, None, "mp"),
            P(None, None, None, "mp"),
            P(None, None, "mp"),
            P(None, "mp", None),
            P(None, "mp"),
            P(None, None, "mp"),
            P(None, "mp"),
            P(None, "mp", None),
            P(None, "mp"),
        ),
        check_vma=False,
    )
```

```python
import functools

import jax
import jax.numpy as jnp
from jax import lax
from jax.experimental import pallas as pl
from jax.experimental.pallas import tpu as pltpu
from jax.sharding import PartitionSpec as P

HD = 64
D = 768
KD = 192
SPANS = (128, 64, 32, 96)
SLABS = (32, 16, 8, 24)
OFFS = (0, 128, 192)
CLIPS = 32
PIECES = 21
EPS = 1e-06
NEG = -1000000000.0
MESH = pl.DeviceIdType.MESH
BF = jnp.bfloat16
F32 = jnp.float32
UNITS = (
    ("down", 0, "yz"),
    ("up", 0, "zy"),
    ("down", 1, "yz"),
    ("up", 1, "zy"),
    ("down", 2, "yz"),
    ("up", 2, "zy"),
    ("qo", 0, "yz"),
    ("qo", 1, "zy"),
    ("qo", 2, "yz"),
)
UNIT_OF = {(name, view): place for place, (name, view, _) in enumerate(UNITS)}
OUT_OF = {"qo": 0, "up": 1, "down": 2}


def nn(a, b):
    return lax.dot_general(a, b, (((1,), (0,)), ((), ())), preferred_element_type=F32)


def nt(a, b):
    return lax.dot_general(a, b, (((1,), (1,)), ((), ())), preferred_element_type=F32)


def tn(a, b):
    return lax.dot_general(a, b, (((0,), (0,)), ((), ())), preferred_element_type=F32)


def layer_stats(x):
    center = x - jnp.mean(x, -1, keepdims=True)
    spread = jnp.mean(center * center, -1, keepdims=True)
    inv = lax.rsqrt(spread + EPS)
    return center * inv, inv


def scratch_plan():
    plan = {}
    for i in range(4):
        span, slab = SPANS[i], SLABS[i]
        for name in ("n1", "s1", "n2", "s2", "zo", "s3", "da", "s4"):
            plan[name, i] = pltpu.VMEM((4, slab, D), BF)
        for name in ("r1", "r2", "r3", "r4"):
            plan[name, i] = pltpu.VMEM((3, slab, D), BF)
        for name in ("x", "af", "daf"):
            plan[name, i] = pltpu.VMEM((slab, D), F32)
        plan["dz", i] = pltpu.VMEM((4, slab, D), F32)
        for name in ("q", "k", "v", "ho"):
            plan[name, i] = pltpu.VMEM((span, KD), BF)
        plan["pr", i] = pltpu.VMEM((3 * span, span), F32)
        plan["dg", i] = pltpu.VMEM((span, D), F32)
        plan["ac", i] = pltpu.VMEM((span, D), BF)
        plan["wq", i] = pltpu.VMEM((3 * KD, D), BF)
        plan["wo", i] = pltpu.VMEM((KD, D), BF)
        plan["wu", i] = pltpu.VMEM((D, D), BF)
        plan["wd", i] = pltpu.VMEM((D, D), BF)
        if i < 3:
            plan["gt", i] = pltpu.VMEM((4, slab, D), BF)
    for turn in range(2):
        plan["pa", turn] = pltpu.VMEM((CLIPS, 8, 256), BF)
        plan["pb", turn] = pltpu.VMEM((CLIPS, 8, 256), BF)
        plan["pc", turn] = pltpu.VMEM((PIECES, 8, 256), BF)
    plan["ts"] = pltpu.VMEM((7, 8, D), BF)
    plan["mx"] = pltpu.VMEM((7, 8, D), F32)
    plan["cc"] = pltpu.VMEM((8, D), BF)
    plan["inv"] = pltpu.SMEM((CLIPS,), jnp.int32)
    plan["cl"] = pltpu.VMEM((8, D), BF)
    plan["cg"] = pltpu.VMEM((CLIPS, 8, D), BF)
    plan["ct"] = pltpu.VMEM((CLIPS, 8, D), BF)
    plan["gin"] = pltpu.VMEM((4, 24, D), F32)
    plan["gdx"] = pltpu.VMEM((4, 24, D), BF)
    plan["go"] = pltpu.VMEM((3, 16, 48, D), BF)
    for u in range(len(UNITS)):
        plan["g", u] = pltpu.VMEM((16, 48, D), BF)
        plan["far4", u] = pltpu.VMEM((4, 48, D), BF)
        plan["near4", u] = pltpu.VMEM((2, 4, 48, D), BF)
        plan["far1", u] = pltpu.VMEM((48, D), BF)
        plan["near1", u] = pltpu.VMEM((2, 48, D), BF)
        plan["gx", u] = pltpu.VMEM((48, D), BF)
        plan["ga", u] = pltpu.VMEM((4, 48, D), BF)
    plan["sva"] = pltpu.VMEM((16, D), F32)
    plan["svb"] = pltpu.VMEM((16, D), F32)
    plan["svr"] = pltpu.VMEM((3, 16, D), F32)
    for step in range(3):
        plan["svs", step] = pltpu.VMEM((32, D), BF)
        plan["svt", step] = pltpu.VMEM((3, 32, D), BF)
    plan["ssem"] = pltpu.SemaphoreType.DMA((256,))
    plan["rsem"] = pltpu.SemaphoreType.DMA((256,))
    plan["lsem"] = pltpu.SemaphoreType.DMA((48,))
    return plan


def kernel(names, *refs):
    (
        partner,
        mix,
        lengths,
        tok,
        cot,
        cotg,
        gain,
        shift,
        b_out,
        b_down,
        b_up,
        b_qv,
        wq_all,
        wo_all,
        wu_all,
        wd_all,
        out_tok,
        out_glob,
        out_grad,
        out_small,
        out_qo,
        out_up,
        out_down,
    ) = refs[:23]
    b = dict(zip(names, refs[23:]))
    ssem, rsem, lsem = b["ssem"], b["rsem"], b["lsem"]
    outs = {"qo": out_qo, "up": out_up, "down": out_down}
    me = lax.axis_index("dp")
    m = lax.axis_index("mp")
    place = {"y": lax.div(me, 8), "x": lax.rem(lax.div(me, 4), 2), "z": lax.rem(me, 4)}

    def at(**moved):
        p = dict(place)
        p.update(moved)
        return ((p["y"] * 2 + p["x"]) * 4 + p["z"], m)

    count = {"s": 0, "l": 0}
    drains = []

    def new(kind):
        count[kind] += 1
        return count[kind] - 1

    def send(src, dst, s, dev):
        pltpu.make_async_remote_copy(
            src_ref=src,
            dst_ref=dst,
            send_sem=ssem.at[s],
            recv_sem=rsem.at[s],
            device_id=dev,
            device_id_type=MESH,
        ).start()

    def wait(like, sem):
        pltpu.make_async_copy(like, like, sem).wait()

    def landed(like, s):
        wait(like, rsem.at[s])
        drains.append((like, s))

    barrier = pltpu.get_barrier_semaphore()

    def greet(k, _):
        pl.semaphore_signal(
            barrier, inc=1, device_id=(lax.rem(me + k, CLIPS), m), device_id_type=MESH
        )
        return 0

    lax.fori_loop(1, CLIPS, greet, 0)
    for k in (1, 2, 3):
        pl.semaphore_signal(barrier, inc=1, device_id=(me, lax.rem(m + k, 4)), device_id_type=MESH)

    fetch = {}
    for i in range(4):
        for name, src in (("wq", wq_all), ("wo", wo_all), ("wu", wu_all), ("wd", wd_all)):
            copy = pltpu.make_async_copy(src.at[i], b[name, i], lsem.at[new("l")])
            copy.start()
            fetch[name, i] = copy

    def weight(name, i):
        if (name, i) in fetch:
            fetch.pop((name, i)).wait()
        return b[name, i]

    pl.semaphore_wait(barrier, CLIPS - 1 + 3)

    def gather_start(buf):
        s = new("s")
        for k in (2, 1, 3):
            send(buf.at[m], buf.at[m], s, (me, lax.rem(m + k, 4)))
        return buf.at[pl.ds(0, 3)], s

    def scatter_start(src, dst):
        s = new("s")
        for k in (2, 1, 3):
            t = lax.rem(m + k, 4)
            send(src.at[t], dst.at[k - 1], s, (me, t))
        return dst, s

    def dp_gather_start(src, dst):
        s = new("s")

        def step(k, _):
            send(src, dst.at[me], s, (lax.rem(me + k, CLIPS), m))
            return 0

        lax.fori_loop(1, CLIPS, step, 0)
        dst[me] = src[...]
        return dst.at[pl.ds(0, CLIPS - 1)], s

    def rows_of(buf, i):
        span, slab = SPANS[i], SLABS[i]
        if slab % 16 == 0:
            return buf[...].reshape(span, D)
        return buf[...].astype(F32).reshape(span, D).astype(BF)

    groups = [m * 4 + r for r in range(4)] + [16 + m * 2 + r for r in range(2)] + [24 + m]

    def deal_start(turn, src_at):
        keep = b["pa", turn]
        s = new("s")
        for j in range(PIECES):

            @pl.when(me != j)
            def _():
                send(src_at(j // 3).at[:, pl.ds((j % 3) * 256, 256)], keep.at[me], s, (j, m))

            @pl.when(me == j)
            def _():
                keep[me] = src_at(j // 3)[:, (j % 3) * 256 : (j % 3) * 256 + 256]

        return s

    def few_or_all(buf, sem):
        @pl.when(me < PIECES)
        def _():
            wait(buf.at[pl.ds(0, PIECES - 1)], sem)

        @pl.when(me >= PIECES)
        def _():
            wait(buf, sem)

    def deal_turn(turn, s, index):
        keep, stage, got = b["pa", turn], b["pb", turn], b["pc", turn]
        t = new("s")

        @pl.when(me < PIECES)
        def _():
            wait(keep.at[pl.ds(0, CLIPS - 1)], rsem.at[s])
            for d in range(CLIPS):
                stage[d] = keep[index[d]]
            got[me] = stage[me]

            def step(k, _):
                d = lax.rem(me + k, CLIPS)
                send(stage.at[d], got.at[me], t, (d, m))
                return 0

            lax.fori_loop(1, CLIPS, step, 0)

        few_or_all(got, ssem.at[s])
        return t

    def deal_end(turn, t):
        stage, got = b["pb", turn], b["pc", turn]
        few_or_all(got, rsem.at[t])

        @pl.when(me < PIECES)
        def _():
            wait(stage.at[pl.ds(0, CLIPS - 1)], ssem.at[t])

        return [
            jnp.concatenate([got[3 * r + c].astype(F32) for c in range(3)], 1) for r in range(7)
        ]

    lam = mix[me]
    b["cc"][...] = jnp.zeros((8, D), BF)
    b["cc"][0:3] = cotg[0]
    s = deal_start(0, lambda r: tok.at[groups[r]])
    cot_ticket = dp_gather_start(b["cc"], b["ct"])
    t = deal_turn(0, s, partner)
    taken = deal_end(0, t)
    for r in range(7):
        value = lam * tok[groups[r]].astype(F32) + (1.0 - lam) * taken[r]
        if r < 4:
            b["x", 0][8 * r : 8 * r + 8] = value
        elif r < 6:
            b["x", 1][8 * (r - 4) : 8 * (r - 4) + 8] = value
        else:
            b["x", 2][...] = value

    def vec(ref, row):
        if len(ref.shape) == 3:
            return ref[row // 2, row % 2 : row % 2 + 1, :]
        return ref[row : row + 1, :]

    def norm(x, i, j):
        hat, _ = layer_stats(x)
        return hat * vec(gain, 2 * i + j) + vec(shift, 2 * i + j)

    def head_mask(h):
        lane = lax.broadcasted_iota(jnp.int32, (1, KD), 1)
        return (lane >= h * HD) & (lane < h * HD + HD)

    masks = [head_mask(h) for h in range(3)]
    zero = jnp.zeros((), BF)

    def stacked(a):
        return jnp.concatenate(
            [jnp.where(masks[h], a.astype(F32), 0.0) for h in range(3)], 0
        ).astype(BF)

    def folded(a, span):
        total = None
        for h in range(3):
            part = jnp.where(masks[h], a[h * span : (h + 1) * span], 0.0)
            total = part if total is None else total + part
        return total

    scale = HD ** (-0.5)

    def attend(i):
        span = SPANS[i]
        normed = rows_of(b["n1", i], i)
        wq = weight("wq", i)
        query = (nt(normed, wq[0:KD]) + vec(b_qv, 2 * i)).astype(BF)
        keys = nt(normed, wq[KD : 2 * KD]).astype(BF)
        values = (nt(normed, wq[2 * KD : 3 * KD]) + vec(b_qv, 2 * i + 1)).astype(BF)
        b["q", i][...] = query
        b["k", i][...] = keys
        b["v", i][...] = values
        scores = nt(stacked(query), keys) * scale
        if i < 3:
            col = lax.broadcasted_iota(jnp.int32, (1, span), 1)
            scores = jnp.where(col < lengths[0, i], scores, NEG)
        expo = jnp.exp(scores - jnp.max(scores, -1, keepdims=True))
        probs = expo / jnp.sum(expo, -1, keepdims=True)
        b["pr", i][...] = probs
        heads_out = folded(nn(probs.astype(BF), values), span).astype(BF)
        b["ho", i][...] = heads_out
        part = nn(heads_out, weight("wo", i)[...])
        b["s1", i][...] = part.astype(BF).reshape(4, SLABS[i], D) if SLABS[i] % 16 == 0 else (
            part.reshape(4, SLABS[i], D).astype(BF)
        )
        return scatter_start(b["s1", i], b["r1", i])

    def put_slabs(name, i, value):
        b[name, i][...] = value.reshape(4, SLABS[i], D).astype(BF)

    def summed(send_name, recv_name, i, ticket):
        landed(*ticket)
        got = b[recv_name, i]
        total = b[send_name, i][m].astype(F32)
        for k in range(3):
            total = total + got[k].astype(F32)
        return total

    def middle(i, ticket):
        after = b["x", i][...] + summed("s1", "r1", i, ticket) + vec(b_out, i)
        b["af", i][...] = after
        b["n2", i][m] = norm(after, i, 1).astype(BF)
        return gather_start(b["n2", i])

    def feed(i, ticket):
        landed(*ticket)
        normed2 = rows_of(b["n2", i], i)
        inner = nn(normed2, weight("wu", i)[...]) + vec(b_up, i)
        c0, c1 = 0.7978845608028654, 0.044715
        square = inner * inner
        th = jnp.tanh(c0 * inner * (1.0 + c1 * square))
        half = 0.5 * (1.0 + th)
        active = (inner * half).astype(BF)
        b["dg", i][...] = half + 0.5 * inner * (1.0 - th * th) * c0 * (1.0 + 3.0 * c1 * square)
        b["ac", i][...] = active
        put_slabs("s2", i, nn(active, weight("wd", i)[...]))
        return scatter_start(b["s2", i], b["r2", i])

    def finish(i, ticket):
        total = b["af", i][...] + summed("s2", "r2", i, ticket) + vec(b_down, i)
        b["zo", i][m] = total.astype(BF)
        return gather_start(b["zo", i])

    tickets = [None] * 3
    for i in range(3):
        b["n1", i][m] = norm(b["x", i][...], i, 0).astype(BF)
        tickets[i] = gather_start(b["n1", i])
    for i in range(3):
        landed(*tickets[i])
        tickets[i] = attend(i)
    for i in range(3):
        tickets[i] = middle(i, tickets[i])
    for i in range(3):
        tickets[i] = feed(i, tickets[i])
    for i in range(3):
        tickets[i] = finish(i, tickets[i])
    row8 = lax.broadcasted_iota(jnp.int32, (8, 1), 0)
    classes = jnp.zeros((8, D), F32)
    for i in range(3):
        landed(*tickets[i])
        first = b["zo", i][0].astype(F32)[0:1]
        classes = jnp.where(row8 == i, first, classes)
    b["cl"][...] = classes.astype(BF)
    ticket = dp_gather_start(b["cl"], b["cg"])
    for i in range(3):
        out_tok[OFFS[i] : OFFS[i] + SPANS[i]] = rows_of(b["zo", i], i)

    r_at = lax.broadcasted_iota(jnp.int32, (96, 256), 0)
    k_at = lax.broadcasted_iota(jnp.int32, (96, 256), 1)
    pick = (k_at == lax.rem(r_at, 32) * 8 + lax.div(r_at, 32)).astype(F32).astype(BF)

    def class_rows(buf):
        return nn(pick, buf[...].astype(F32).reshape(256, D).astype(BF))

    landed(*ticket)
    gin = class_rows(b["cg"])
    b["gin"][...] = gin.reshape(4, 24, D)
    b["x", 3][...] = b["gin"][m]
    put_slabs("n1", 3, norm(gin, 3, 0))
    ticket = attend(3)
    ticket = middle(3, ticket)
    ticket = feed(3, ticket)
    glob_ticket = finish(3, ticket)
    landed(*cot_ticket)
    b["dz", 3][...] = class_rows(b["ct"]).reshape(4, 24, D)

    def put_unit(name, i, row, value):
        value = value.astype(BF)
        chunks = value.shape[0] // 48
        lo = row // 48
        if i == 3:
            b["go"][OUT_OF[name], lo : lo + chunks] = value.reshape(chunks, 48, D)
            return
        b["g", UNIT_OF[name, i]][lo : lo + chunks] = value.reshape(chunks, 48, D)

    def back_feed(i):
        span = SPANS[i]
        dz = b["dz", i][...].reshape(span, D)
        b["svb"][4 * i : 4 * i + 1] = jnp.sum(dz, 0, keepdims=True)
        dm = dz.astype(BF)
        for part in range(2):
            cols = slice(part * 384, part * 384 + 384)
            put_unit("down", i, part * 384, tn(b["ac", i][:, cols], dm))
        start_unit("down", i)
        dact = nt(dm, weight("wd", i)[...])
        dinner = (b["dg", i][...] * dact).astype(BF)
        put_slabs("s3", i, nt(dinner, weight("wu", i)[...]))
        ticket = scatter_start(b["s3", i], b["r3", i])
        b["svb"][4 * i + 2 : 4 * i + 3] = jnp.sum(dinner.astype(F32), 0, keepdims=True)
        normed2 = rows_of(b["n2", i], i)
        for part in range(2):
            cols = slice(part * 384, part * 384 + 384)
            put_unit("up", i, part * 384, tn(normed2[:, cols], dinner))
        start_unit("up", i)
        return ticket

    def norm_back(x, dy, i, j):
        hat, inv = layer_stats(x)
        b["sva"][4 * i + 2 * j : 4 * i + 2 * j + 1] = jnp.sum(dy * hat, 0, keepdims=True)
        b["sva"][4 * i + 2 * j + 1 : 4 * i + 2 * j + 2] = jnp.sum(dy, 0, keepdims=True)
        g = dy * vec(gain, 2 * i + j)
        return inv * (
            g - jnp.mean(g, -1, keepdims=True) - hat * jnp.mean(g * hat, -1, keepdims=True)
        )

    def back_middle(i, ticket):
        dn2 = summed("s3", "r3", i, ticket)
        dafter = b["dz", i][m] + norm_back(b["af", i][...], dn2, i, 1)
        b["daf", i][...] = dafter
        b["da", i][m] = dafter.astype(BF)
        return gather_start(b["da", i])

    def back_attend(i, ticket):
        span = SPANS[i]
        landed(*ticket)
        da = rows_of(b["da", i], i)
        b["svb"][4 * i + 1 : 4 * i + 2] = jnp.sum(da.astype(F32), 0, keepdims=True)
        dheads = nt(da, weight("wo", i)[...]).astype(BF)
        query, keys, values = b["q", i][...], b["k", i][...], b["v", i][...]
        probs = b["pr", i][...]
        d3 = stacked(dheads)
        dprob = nt(d3, values)
        dscore = probs * (dprob - jnp.sum(dprob * probs, -1, keepdims=True))
        dscore = dscore.astype(BF)
        dquery = (folded(nn(dscore, keys), span) * scale).astype(BF)
        dkeys = (tn(dscore, stacked(query)) * scale).astype(BF)
        dvalues = tn(probs.astype(BF), d3).astype(BF)
        wq = weight("wq", i)
        part = nn(dquery, wq[0:KD]) + nn(dkeys, wq[KD : 2 * KD]) + nn(dvalues, wq[2 * KD : 3 * KD])
        put_slabs("s4", i, part)
        ticket = scatter_start(b["s4", i], b["r4", i])
        b["svb"][4 * i + 3 : 4 * i + 4, 0:KD] = jnp.sum(dquery.astype(F32), 0, keepdims=True)
        b["svb"][4 * i + 3 : 4 * i + 4, 256 : 256 + KD] = jnp.sum(
            dvalues.astype(F32), 0, keepdims=True
        )
        normed = rows_of(b["n1", i], i)
        put_unit("qo", i, 0, tn(dquery, normed))
        put_unit("qo", i, KD, tn(dkeys, normed))
        put_unit("qo", i, 2 * KD, tn(dvalues, normed))
        put_unit("qo", i, 3 * KD, tn(b["ho", i][...], da))
        start_unit("qo", i)
        return ticket

    def back_finish(i, ticket):
        dn1 = summed("s4", "r4", i, ticket)
        return b["daf", i][...] + norm_back(b["x", i][...], dn1, i, 0)

    def halves(ref):
        if len(ref.shape) == 3:
            n = ref.shape[0] // 2
            return ref.at[pl.ds(0, n)], ref.at[pl.ds(n, n)]
        return ref.at[:, pl.ds(0, 384)], ref.at[:, pl.ds(384, 384)]

    def add_to(dst, *srcs):
        for c in range(dst.shape[0]) if len(dst.shape) == 3 else (Ellipsis,):
            total = dst[c].astype(F32)
            for src in srcs:
                total = total + src[c].astype(F32)
            dst[c] = total.astype(BF)

    def ring_sum(axis, chunk, far_buf, near_buf):
        p = place[axis]
        up, down, far = lax.rem(p + 1, 4), lax.rem(p + 3, 4), lax.rem(p + 2, 4)
        to_up, to_down = at(**{axis: up}), at(**{axis: down})
        s0, s1, s2, s3 = new("s"), new("s"), new("s"), new("s")
        f0, f1 = halves(chunk(far))
        r0, r1 = halves(far_buf)
        send(f0, r0, s0, to_up)
        send(f1, r1, s1, to_down)
        yield
        landed(r0, s0)
        add_to(halves(chunk(up))[0], r0)
        send(chunk(up), near_buf.at[0], s2, to_up)
        landed(r1, s1)
        add_to(halves(chunk(down))[1], r1)
        send(chunk(down), near_buf.at[1], s3, to_down)
        yield
        landed(near_buf.at[0], s2)
        landed(near_buf.at[1], s3)
        add_to(chunk(p), near_buf.at[0], near_buf.at[1])

    def ring_spread(axis, slot, own, like):
        p = place[axis]
        up, down = lax.rem(p + 1, 4), lax.rem(p + 3, 4)
        to_up, to_down = at(**{axis: up}), at(**{axis: down})
        s0, s1, s2, s3 = new("s"), new("s"), new("s"), new("s")
        send(own, slot(p), s0, to_up)
        send(own, slot(p), s1, to_down)
        yield
        landed(like, s0)
        part = halves(slot(down))[0]
        send(part, part, s2, to_up)
        landed(like, s1)
        part = halves(slot(up))[1]
        send(part, part, s3, to_down)
        yield
        landed(halves(like)[0], s2)
        landed(halves(like)[1], s3)

    def sum_unit(u):
        name, view, (one, two) = UNITS[u]
        g, gx, ga = b["g", u], b["gx", u], b["ga", u]
        p1, p2 = place[one], place[two]
        out = outs[name].at[view]
        yield from ring_sum(one, lambda t: g.at[pl.ds(t * 4, 4)], b["far4", u], b["near4", u])
        yield from ring_sum(two, lambda t: g.at[p1 * 4 + t], b["far1", u], b["near1", u])
        s = new("s")
        send(g.at[p1 * 4 + p2], gx, s, at(x=1 - place["x"]))
        yield
        landed(gx, s)
        ga[p2] = (g[p1 * 4 + p2].astype(F32) + gx[...].astype(F32)).astype(BF)
        yield from ring_spread(two, lambda t: ga.at[t], ga.at[p2], ga.at[0])
        own = out.at[pl.ds(p1 * 4, 4)]
        store(ga, own)
        yield from ring_spread(one, lambda t: out.at[pl.ds(t * 4, 4)], ga, out.at[pl.ds(0, 4)])

    stores = []

    def store(src, dst):
        copy = pltpu.make_async_copy(src, dst, lsem.at[new("l")])
        copy.start()
        stores.append(copy)

    running = []

    def start_unit(name, i):
        if i == 3:
            store(b["go"].at[OUT_OF[name]], outs[name].at[3])
            return
        u = UNIT_OF[name, i]
        unit = sum_unit(u)
        next(unit)
        running.append(unit)

    def advance(some):
        for unit in some:
            if unit in running and next(unit, "end") == "end":
                running.remove(unit)

    ticket = back_feed(3)
    ticket = back_middle(3, ticket)
    ticket = back_attend(3, ticket)
    dx = back_finish(3, ticket)
    b["gdx"][m] = dx.astype(BF)
    ticket = gather_start(b["gdx"])
    landed(*glob_ticket)
    o_at = lax.broadcasted_iota(jnp.int32, (8, 96), 0)
    w_at = lax.broadcasted_iota(jnp.int32, (8, 96), 1)
    mine = ((w_at == o_at * 32 + me) & (o_at < 3)).astype(F32).astype(BF)
    out_glob[...] = nn(mine, rows_of(b["zo", 3], 3)).astype(BF)
    landed(*ticket)
    dgin = nn(mine, rows_of(b["gdx"], 3))

    for i in range(3):
        dz = cot[OFFS[i] : OFFS[i] + SPANS[i]].astype(F32)
        row = lax.broadcasted_iota(jnp.int32, (SPANS[i], 1), 0)
        dz = dz + jnp.where(row == 0, dgin[i : i + 1], 0.0)
        b["dz", i][...] = dz.reshape(4, SLABS[i], D)
        tickets[i] = back_feed(i)
    for i in range(3):
        tickets[i] = back_middle(i, tickets[i])
    for i in range(3):
        tickets[i] = back_attend(i, tickets[i])
    for i in range(3):
        dx = back_finish(i, tickets[i])
        base = (0, 4, 6)[i]
        for r in range(SLABS[i] // 8):
            rows = dx[8 * r : 8 * r + 8]
            b["mx"][base + r] = lam * rows
            b["ts"][base + r] = ((1.0 - lam) * rows).astype(BF)
    order = list(running)

    def invert(d, _):
        found = jnp.int32(0)
        for c in range(CLIPS):
            found = jnp.where(partner[c] == d, c, found)
        b["inv"][d] = found
        return 0

    lax.fori_loop(0, CLIPS, invert, 0)
    s = deal_start(1, lambda r: b["ts"].at[r])

    s_mp = new("s")
    for k in (2, 1, 3):
        send(b["sva"], b["svr"].at[k - 1], s_mp, (me, lax.rem(m + k, 4)))
    advance(order[:3])
    t = deal_turn(1, s, b["inv"])
    advance(order[3:6])
    landed(b["svr"], s_mp)
    sva = b["sva"][...] + b["svr"][0] + b["svr"][1] + b["svr"][2]
    svb = b["svb"][...]
    b["svs", 0][...] = jnp.concatenate([sva, svb], 0).astype(BF)

    def small_start(step, axis):
        s = new("s")
        far = (1, 3, 2) if axis != "x" else (1,)
        size = 4 if axis != "x" else 2
        for k in far:
            dev = at(**{axis: lax.rem(place[axis] + k, size)})
            send(b["svs", step], b["svt", step].at[k - 1], s, dev)
        return b["svt", step].at[pl.ds(0, len(far))], s

    def small_end(step, ticket, axis):
        landed(*ticket)
        total = b["svs", step][...].astype(F32)
        for k in range(3 if axis != "x" else 1):
            total = total + b["svt", step][k].astype(F32)
        return total

    ticket = small_start(0, "y")
    taken = deal_end(1, t)
    for i in range(3):
        base = (0, 4, 6)[i]
        for r in range(SLABS[i] // 8):
            rows = b["mx"][base + r] + taken[base + r]
            b["gt", i][m, 8 * r : 8 * r + 8] = rows.astype(BF)
        tickets[i] = gather_start(b["gt", i])
    advance(order[:3])
    b["svs", 1][...] = small_end(0, ticket, "y").astype(BF)
    ticket = small_start(1, "z")
    advance(order[3:6])
    for i in range(3):
        landed(*tickets[i])
        out_grad[OFFS[i] : OFFS[i] + SPANS[i]] = rows_of(b["gt", i], i)
    b["svs", 2][...] = small_end(1, ticket, "z").astype(BF)
    ticket = small_start(2, "x")
    advance(order)
    total = small_end(2, ticket, "x")
    out_small[0:12] = total[0:12]
    out_small[12:16] = sva[12:16]
    out_small[16:28] = total[16:28]
    out_small[28:32] = svb[12:16]
    while running:
        advance(list(running))
    for like, s in drains:
        wait(like, ssem.at[s])
    for copy in stores:
        copy.wait()


def shards(
    tokens,
    lengths,
    partner,
    mix_coef,
    norm_gain,
    norm_bias,
    w_qkv,
    b_qv,
    w_out,
    b_out,
    w_up,
    b_up,
    w_down,
    b_down,
    cot_tokens,
    cot_global,
):
    wq = jnp.transpose(w_qkv, (0, 2, 3, 1)).reshape(4, 3 * KD, D)
    plan = scratch_plan()
    names = list(plan)
    smem = pl.BlockSpec(memory_space=pltpu.SMEM)
    vmem = pl.BlockSpec(memory_space=pltpu.VMEM)
    hbm = pl.BlockSpec(memory_space=pl.ANY)
    unit = jax.ShapeDtypeStruct((4, 16, 48, D), BF)
    out_tok, out_glob, out_grad, small, qo, up, down = pl.pallas_call(
        functools.partial(kernel, names),
        out_shape=(
            jax.ShapeDtypeStruct((224, D), BF),
            jax.ShapeDtypeStruct((8, D), BF),
            jax.ShapeDtypeStruct((224, D), BF),
            jax.ShapeDtypeStruct((32, D), F32),
            unit,
            unit,
            unit,
        ),
        in_specs=[smem] * 3 + [vmem] * 9 + [hbm] * 4,
        out_specs=(vmem,) * 4 + (hbm,) * 3,
        scratch_shapes=list(plan.values()),
        compiler_params=pltpu.CompilerParams(
            collective_id=0, has_side_effects=True, vmem_limit_bytes=60 * 2**20
        ),
    )(
        partner,
        mix_coef,
        lengths,
        tokens.reshape(28, 8, D),
        cot_tokens[0],
        cot_global,
        norm_gain,
        norm_bias,
        b_out,
        b_down,
        b_up,
        b_qv,
        wq,
        w_out,
        w_up,
        w_down,
    )
    out_tok, out_glob, out_grad, gain, shift, qkv, qv, out, bout, ups, bup, downs, bdown = widen(
        out_tok, out_glob, out_grad, small, *(a.reshape(4, D, D) for a in (qo, up, down))
    )
    return (
        out_tok,
        out_glob,
        out_grad,
        gain,
        shift,
        jnp.transpose(qkv.reshape(4, 3, KD, D), (0, 3, 1, 2)),
        qv,
        out,
        bout,
        ups,
        bup,
        downs,
        bdown,
    )


def widen_kernel(*refs):
    tok, glob, grad, small, qkv, out, up, down = refs[:8]
    o_tok, o_glob, o_grad, o_gain, o_shift, o_qkv, o_qv, o_out, o_bout, o_up, o_bup, o_down, o_bdown = refs[8:]
    o_qkv[...] = qkv[...].astype(F32)
    o_out[...] = out[...].astype(F32)
    o_up[...] = up[...].astype(F32)
    o_down[...] = down[...].astype(F32)

    @pl.when((pl.program_id(0) == 0) & (pl.program_id(1) == 0))
    def _():
        o_tok[0] = tok[...]
        o_grad[0] = grad[...]
        o_glob[0] = glob[0:3]
        m = lax.axis_index("mp")

        def share(row):
            value = small[row : row + 1]
            mine = value[:, 0:KD]
            for k in range(1, 4):
                mine = jnp.where(m == k, value[:, k * KD : (k + 1) * KD], mine)
            return mine

        for i in range(4):
            for j in range(2):
                o_gain[i, j : j + 1] = share(4 * i + 2 * j)
                o_shift[i, j : j + 1] = share(4 * i + 2 * j + 1)
            row = 16 + 4 * i
            o_bdown[i : i + 1] = share(row)
            o_bout[i : i + 1] = share(row + 1)
            o_bup[i : i + 1] = small[row + 2 : row + 3]
            o_qv[i, 0:1] = small[row + 3 : row + 4, 0:KD]
            o_qv[i, 1:2] = small[row + 3 : row + 4, 256 : 256 + KD]


def widen(tok, glob, grad, small, qo, up, down):
    def whole(*shape):
        return pl.BlockSpec(shape, lambda i, j: (0,) * len(shape))

    def rows(n, base=0):
        return pl.BlockSpec((1, n, D), lambda i, j: (i, base + j, 0))

    shape = jax.ShapeDtypeStruct
    return pl.pallas_call(
        widen_kernel,
        grid=(4, 3),
        in_specs=[whole(224, D), whole(8, D), whole(224, D), whole(32, D)]
        + [rows(192), rows(64, 9), rows(256), rows(256)],
        out_specs=[whole(1, 224, D), whole(1, 3, D), whole(1, 224, D)]
        + [whole(4, 2, KD), whole(4, 2, KD), rows(192), whole(4, 2, KD), rows(64), whole(4, KD)]
        + [rows(256), whole(4, D), rows(256), whole(4, KD)],
        out_shape=[shape((1, 224, D), BF), shape((1, 3, D), BF), shape((1, 224, D), BF)]
        + [shape((4, 2, KD), F32), shape((4, 2, KD), F32), shape((4, 3 * KD, D), F32)]
        + [shape((4, 2, KD), F32), shape((4, KD, D), F32), shape((4, KD), F32)]
        + [shape((4, D, D), F32), shape((4, D), F32), shape((4, D, D), F32), shape((4, KD), F32)],
        compiler_params=pltpu.CompilerParams(vmem_limit_bytes=60 * 2**20),
    )(tok, glob, grad, small, qo, qo, up, down)


def solution(mesh):
    placed = (
        P("dp", None, None),
        P("dp", None),
        P(),
        P(),
        P(),
        P(),
        P(None, None, None, "mp"),
        P(None, None, "mp"),
        P(None, "mp", None),
        P(),
        P(None, None, "mp"),
        P(None, "mp"),
        P(None, "mp", None),
        P(),
        P("dp", None, None),
        P("dp", None, None),
    )
    return jax.shard_map(
        shards,
        mesh=mesh,
        in_specs=placed,
        out_specs=(
            P("dp", None, None),
            P("dp", None, None),
            P("dp", None, None),
            P(None, None, "mp"),
            P(None, None, "mp"),
            P(None, None, None, "mp"),
            P(None, None, "mp"),
            P(None, "mp", None),
            P(None, "mp"),
            P(None, None, "mp"),
            P(None, "mp"),
            P(None, "mp", None),
            P(None, "mp"),
        ),
        check_vma=False,
    )
```

```python
import functools

import jax
import jax.numpy as jnp
from jax import lax
from jax.experimental import pallas as pl
from jax.experimental.pallas import tpu as pltpu
from jax.sharding import PartitionSpec as P

HD = 64
D = 768
KD = 192
SPANS = (128, 64, 32, 96)
SLABS = (32, 16, 8, 24)
OFFS = (0, 128, 192)
CLIPS = 32
PIECES = 21
EPS = 1e-06
NEG = -1000000000.0
MESH = pl.DeviceIdType.MESH
BF = jnp.bfloat16
F32 = jnp.float32
UNITS = (
    ("down", 0, "yz"),
    ("up", 0, "zy"),
    ("down", 1, "zy"),
    ("up", 1, "yz"),
    ("down", 2, "zy"),
    ("up", 2, "yz"),
    ("qo", 0, "yz"),
    ("qo", 1, "zy"),
    ("qo", 2, "zy"),
)
UNIT_OF = {(name, view): place for place, (name, view, _) in enumerate(UNITS)}
TICKS = (2, 2, 2, 3, 3, 3, 3, 3, 4, 3, 4, 3, 3, 3)
OUT_OF = {"qo": 0, "up": 1, "down": 2}


def nn(a, b):
    return lax.dot_general(a, b, (((1,), (0,)), ((), ())), preferred_element_type=F32)


def nt(a, b):
    return lax.dot_general(a, b, (((1,), (1,)), ((), ())), preferred_element_type=F32)


def tn(a, b):
    return lax.dot_general(a, b, (((0,), (0,)), ((), ())), preferred_element_type=F32)


def layer_stats(x):
    center = x - jnp.mean(x, -1, keepdims=True)
    spread = jnp.mean(center * center, -1, keepdims=True)
    inv = lax.rsqrt(spread + EPS)
    return center * inv, inv


def scratch_plan():
    plan = {}
    for i in range(4):
        span, slab = SPANS[i], SLABS[i]
        for name in ("n1", "s1", "n2", "s2", "zo", "s3", "da", "s4"):
            plan[name, i] = pltpu.VMEM((4, slab, D), BF)
        for name in ("r1", "r2", "r3", "r4"):
            plan[name, i] = pltpu.VMEM((3, slab, D), BF)
        for name in ("x", "af", "daf"):
            plan[name, i] = pltpu.VMEM((slab, D), F32)
        plan["dz", i] = pltpu.VMEM((4, slab, D), F32)
        for name in ("q", "k", "v", "ho"):
            plan[name, i] = pltpu.VMEM((span, KD), BF)
        plan["pr", i] = pltpu.VMEM((3 * span, span), F32)
        plan["dg", i] = pltpu.VMEM((span, D), F32)
        plan["ac", i] = pltpu.VMEM((span, D), BF)
        plan["wq", i] = pltpu.VMEM((3 * KD, D), BF)
        plan["wo", i] = pltpu.VMEM((KD, D), BF)
        plan["wu", i] = pltpu.VMEM((D, D), BF)
        plan["wd", i] = pltpu.VMEM((D, D), BF)
        if i < 3:
            plan["gt", i] = pltpu.VMEM((4, slab, D), BF)
            for name in ("ac4", "n24", "pj4"):
                plan[name, i] = pltpu.VMEM((4, span, KD), BF)
            for name in ("cz", "nr", "di", "dh"):
                plan[name, i] = pltpu.VMEM((span, D), BF)
    for turn in range(2):
        plan["pa", turn] = pltpu.VMEM((CLIPS, 8, 256), BF)
        plan["pb", turn] = pltpu.VMEM((CLIPS, 8, 256), BF)
        plan["pc", turn] = pltpu.VMEM((PIECES, 8, 256), BF)
    plan["ts"] = pltpu.VMEM((7, 8, D), BF)
    plan["mx"] = pltpu.VMEM((7, 8, D), F32)
    plan["cc"] = pltpu.VMEM((8, D), BF)
    plan["inv"] = pltpu.SMEM((CLIPS,), jnp.int32)
    plan["cl"] = pltpu.VMEM((8, D), BF)
    plan["cg"] = pltpu.VMEM((CLIPS, 8, D), BF)
    plan["ct"] = pltpu.VMEM((CLIPS, 8, D), BF)
    for name in ("al", "bc"):
        plan[name] = pltpu.VMEM((8, D), BF)
    for name in ("ag", "bg"):
        plan[name] = pltpu.VMEM((CLIPS, 8, D), BF)
    plan["afc"] = pltpu.VMEM((4, 8, D), F32)
    plan["pc"] = pltpu.VMEM((4, 8, D), BF)
    plan["dac"] = pltpu.VMEM((8, D), F32)
    plan["gin"] = pltpu.VMEM((4, 24, D), F32)
    plan["gdx"] = pltpu.VMEM((4, 24, D), BF)
    plan["go"] = pltpu.VMEM((3, 16, 48, D), BF)
    for u, (name, view, _) in enumerate(UNITS):
        plan["fa", u] = pltpu.VMEM((4, SPANS[view], KD), BF)
        plan["fb", u] = pltpu.VMEM((4, SPANS[view], D), BF)
        if name == "qo":
            plan["fc", u] = pltpu.VMEM((4, SPANS[view], D), BF)
        plan["g", u] = pltpu.VMEM((4, 48, D), BF)
        plan["near", u] = pltpu.VMEM((3, 48, D), BF)
        plan["gx", u] = pltpu.VMEM((48, D), BF)
        plan["ga", u] = pltpu.VMEM((4, 48, D), BF)
    plan["sva"] = pltpu.VMEM((16, D), F32)
    plan["svb"] = pltpu.VMEM((16, D), F32)
    plan["svr"] = pltpu.VMEM((3, 16, D), F32)
    for step in range(3):
        plan["svs", step] = pltpu.VMEM((32, D), BF)
        plan["svt", step] = pltpu.VMEM((3, 32, D), BF)
    plan["ssem"] = pltpu.SemaphoreType.DMA((256,))
    plan["rsem"] = pltpu.SemaphoreType.DMA((256,))
    plan["lsem"] = pltpu.SemaphoreType.DMA((48,))
    return plan


def kernel(names, *refs):
    (
        partner,
        mix,
        lengths,
        tok,
        cot,
        cotg,
        gain,
        shift,
        b_out,
        b_down,
        b_up,
        b_qv,
        wq_all,
        wo_all,
        wu_all,
        wd_all,
        out_tok,
        out_glob,
        out_grad,
        out_small,
        out_left,
        out_right,
        out_qo,
        out_up,
        out_down,
    ) = refs[:25]
    b = dict(zip(names, refs[25:]))
    ssem, rsem, lsem = b["ssem"], b["rsem"], b["lsem"]
    outs = {"qo": out_qo, "up": out_up, "down": out_down}
    me = lax.axis_index("dp")
    m = lax.axis_index("mp")
    place = {"y": lax.div(me, 8), "x": lax.rem(lax.div(me, 4), 2), "z": lax.rem(me, 4)}

    def at(**moved):
        p = dict(place)
        p.update(moved)
        return ((p["y"] * 2 + p["x"]) * 4 + p["z"], m)

    count = {"s": 0, "l": 0}
    drains = []

    def new(kind):
        count[kind] += 1
        return count[kind] - 1

    def send(src, dst, s, dev):
        pltpu.make_async_remote_copy(
            src_ref=src,
            dst_ref=dst,
            send_sem=ssem.at[s],
            recv_sem=rsem.at[s],
            device_id=dev,
            device_id_type=MESH,
        ).start()

    def wait(like, sem):
        pltpu.make_async_copy(like, like, sem).wait()

    def landed(like, s):
        wait(like, rsem.at[s])
        drains.append(lambda: wait(like, ssem.at[s]))

    barrier = pltpu.get_barrier_semaphore()

    def greet(k, _):
        pl.semaphore_signal(
            barrier, inc=1, device_id=(lax.rem(me + k, CLIPS), m), device_id_type=MESH
        )
        return 0

    lax.fori_loop(1, CLIPS, greet, 0)
    for k in (1, 2, 3):
        pl.semaphore_signal(barrier, inc=1, device_id=(me, lax.rem(m + k, 4)), device_id_type=MESH)

    fetch = {}
    for i in range(4):
        for name, src in (("wq", wq_all), ("wo", wo_all), ("wu", wu_all), ("wd", wd_all)):
            copy = pltpu.make_async_copy(src.at[i], b[name, i], lsem.at[new("l")])
            copy.start()
            fetch[name, i] = copy

    def weight(name, i):
        if (name, i) in fetch:
            fetch.pop((name, i)).wait()
        return b[name, i]

    pl.semaphore_wait(barrier, CLIPS - 1 + 3)

    def gather_start(buf):
        s = new("s")
        for k in (2, 1, 3):
            send(buf.at[m], buf.at[m], s, (me, lax.rem(m + k, 4)))
        return buf.at[pl.ds(0, 3)], s

    def scatter_start(src, dst):
        s = new("s")
        for k in (2, 1, 3):
            t = lax.rem(m + k, 4)
            send(src.at[t], dst.at[k - 1], s, (me, t))
        return dst, s

    def dp_gather_start(src, dst):
        s = new("s")

        def step(k, _):
            send(src, dst.at[me], s, (lax.rem(me + k, CLIPS), m))
            return 0

        lax.fori_loop(1, CLIPS, step, 0)
        dst[me] = src[...]
        return dst.at[pl.ds(0, CLIPS - 1)], s

    factors = {}

    def share_rows(name, i, part, src_of):
        u = UNIT_OF[name, i]
        one = UNITS[u][2][0]
        p = place[one]
        dst = b[part, u]
        s = new("s")
        for k in (1, 3, 2):
            t = lax.rem(p + k, 4)
            send(src_of(t), dst.at[p], s, at(**{one: t}))
        dst[p] = src_of(p)[...]
        factors[part, u] = (dst.at[pl.ds(0, 3)], s)

    def rows_of(buf, i):
        span, slab = SPANS[i], SLABS[i]
        if slab % 16 == 0:
            return buf[...].reshape(span, D)
        return buf[...].astype(F32).reshape(span, D).astype(BF)

    groups = [m * 4 + r for r in range(4)] + [16 + m * 2 + r for r in range(2)] + [24 + m]

    def deal_start(turn, src_at):
        keep = b["pa", turn]
        s = new("s")
        for j in range(PIECES):

            @pl.when(me != j)
            def _():
                send(src_at(j // 3).at[:, pl.ds((j % 3) * 256, 256)], keep.at[me], s, (j, m))

            @pl.when(me == j)
            def _():
                keep[me] = src_at(j // 3)[:, (j % 3) * 256 : (j % 3) * 256 + 256]

        return s

    def few_or_all(buf, sem):
        @pl.when(me < PIECES)
        def _():
            wait(buf.at[pl.ds(0, PIECES - 1)], sem)

        @pl.when(me >= PIECES)
        def _():
            wait(buf, sem)

    def deal_turn(turn, s, index):
        keep, stage, got = b["pa", turn], b["pb", turn], b["pc", turn]
        t = new("s")

        @pl.when(me < PIECES)
        def _():
            wait(keep.at[pl.ds(0, CLIPS - 1)], rsem.at[s])
            for d in range(CLIPS):
                stage[d] = keep[index[d]]
            got[me] = stage[me]

            def step(k, _):
                d = lax.rem(me + k, CLIPS)
                send(stage.at[d], got.at[me], t, (d, m))
                return 0

            lax.fori_loop(1, CLIPS, step, 0)

        few_or_all(got, ssem.at[s])
        return t

    def deal_end(turn, t):
        stage, got = b["pb", turn], b["pc", turn]
        few_or_all(got, rsem.at[t])

        @pl.when(me < PIECES)
        def _():
            wait(stage.at[pl.ds(0, CLIPS - 1)], ssem.at[t])

        return [
            jnp.concatenate([got[3 * r + c].astype(F32) for c in range(3)], 1) for r in range(7)
        ]

    lam = mix[me]
    b["cc"][...] = jnp.zeros((8, D), BF)
    b["cc"][0:3] = cotg[0]
    s = deal_start(0, lambda r: tok.at[groups[r]])
    cot_ticket = dp_gather_start(b["cc"], b["ct"])
    t = deal_turn(0, s, partner)
    for i in range(3):
        row = lax.broadcasted_iota(jnp.int32, (SPANS[i], 1), 0)
        dz = jnp.where(row == 0, 0.0, cot[OFFS[i] : OFFS[i] + SPANS[i]].astype(F32))
        b["cz", i][...] = dz.astype(BF)
        b["dz", i][...] = dz.reshape(4, SLABS[i], D)
        share_rows("down", i, "fb", lambda t: b["cz", i])
    taken = deal_end(0, t)
    for r in range(7):
        value = lam * tok[groups[r]].astype(F32) + (1.0 - lam) * taken[r]
        if r < 4:
            b["x", 0][8 * r : 8 * r + 8] = value
        elif r < 6:
            b["x", 1][8 * (r - 4) : 8 * (r - 4) + 8] = value
        else:
            b["x", 2][...] = value

    def vec(ref, row):
        if len(ref.shape) == 3:
            return ref[row // 2, row % 2 : row % 2 + 1, :]
        return ref[row : row + 1, :]

    def norm(x, i, j):
        hat, _ = layer_stats(x)
        return hat * vec(gain, 2 * i + j) + vec(shift, 2 * i + j)

    def head_mask(h):
        lane = lax.broadcasted_iota(jnp.int32, (1, KD), 1)
        return (lane >= h * HD) & (lane < h * HD + HD)

    masks = [head_mask(h) for h in range(3)]
    zero = jnp.zeros((), BF)

    def stacked(a):
        return jnp.concatenate(
            [jnp.where(masks[h], a.astype(F32), 0.0) for h in range(3)], 0
        ).astype(BF)

    def folded(a, span):
        total = None
        for h in range(3):
            part = jnp.where(masks[h], a[h * span : (h + 1) * span], 0.0)
            total = part if total is None else total + part
        return total

    scale = HD ** (-0.5)

    def attend(i):
        span = SPANS[i]
        normed = rows_of(b["n1", i], i)
        wq = weight("wq", i)
        query = (nt(normed, wq[0:KD]) + vec(b_qv, 2 * i)).astype(BF)
        keys = nt(normed, wq[KD : 2 * KD]).astype(BF)
        values = (nt(normed, wq[2 * KD : 3 * KD]) + vec(b_qv, 2 * i + 1)).astype(BF)
        b["q", i][...] = query
        b["k", i][...] = keys
        b["v", i][...] = values
        scores = nt(stacked(query), keys) * scale
        if i < 3:
            col = lax.broadcasted_iota(jnp.int32, (1, span), 1)
            scores = jnp.where(col < lengths[0, i], scores, NEG)
        expo = jnp.exp(scores - jnp.max(scores, -1, keepdims=True))
        probs = expo / jnp.sum(expo, -1, keepdims=True)
        b["pr", i][...] = probs
        heads_out = folded(nn(probs.astype(BF), values), span).astype(BF)
        b["ho", i][...] = heads_out
        part = nn(heads_out, weight("wo", i)[...])
        b["s1", i][...] = part.astype(BF).reshape(4, SLABS[i], D) if SLABS[i] % 16 == 0 else (
            part.reshape(4, SLABS[i], D).astype(BF)
        )
        ticket = scatter_start(b["s1", i], b["r1", i])
        if i < 3:
            b["nr", i][...] = normed
            share_rows("qo", i, "fb", lambda t: b["nr", i])
        return ticket

    def put_slabs(name, i, value):
        b[name, i][...] = value.reshape(4, SLABS[i], D).astype(BF)

    def summed(send_name, recv_name, i, ticket):
        landed(*ticket)
        got = b[recv_name, i]
        total = b[send_name, i][m].astype(F32)
        for k in range(3):
            total = total + got[k].astype(F32)
        return total

    def middle(i, ticket):
        after = b["x", i][...] + summed("s1", "r1", i, ticket) + vec(b_out, i)
        b["af", i][...] = after
        b["n2", i][m] = norm(after, i, 1).astype(BF)
        return gather_start(b["n2", i])

    def feed(i, ticket):
        landed(*ticket)
        normed2 = rows_of(b["n2", i], i)
        inner = nn(normed2, weight("wu", i)[...]) + vec(b_up, i)
        c0, c1 = 0.7978845608028654, 0.044715
        square = inner * inner
        th = jnp.tanh(c0 * inner * (1.0 + c1 * square))
        half = 0.5 * (1.0 + th)
        active = (inner * half).astype(BF)
        b["dg", i][...] = half + 0.5 * inner * (1.0 - th * th) * c0 * (1.0 + 3.0 * c1 * square)
        b["ac", i][...] = active
        put_slabs("s2", i, nn(active, weight("wd", i)[...]))
        ticket = scatter_start(b["s2", i], b["r2", i])
        if i < 3:
            for t in range(4):
                cols = slice(t * KD, t * KD + KD)
                b["ac4", i][t] = active[:, cols]
                b["n24", i][t] = normed2[:, cols]
            share_rows("down", i, "fa", lambda t: b["ac4", i].at[t])
            start_unit("down", i)
            share_rows("up", i, "fa", lambda t: b["n24", i].at[t])
        return ticket

    def finish(i, ticket):
        total = b["af", i][...] + summed("s2", "r2", i, ticket) + vec(b_down, i)
        b["zo", i][m] = total.astype(BF)
        return gather_start(b["zo", i])

    row8 = lax.broadcasted_iota(jnp.int32, (8, 1), 0)

    def rows8_at(buf, kinds):
        r_at = lax.broadcasted_iota(jnp.int32, (32 * kinds, 256), 0)
        k_at = lax.broadcasted_iota(jnp.int32, (32 * kinds, 256), 1)
        pick = (k_at == lax.rem(r_at, 32) * 8 + lax.div(r_at, 32)).astype(F32).astype(BF)
        return nn(pick, buf[...].astype(F32).reshape(256, D).astype(BF))

    def put_unit(name, row, value):
        value = value.astype(BF)
        chunks = value.shape[0] // 48
        lo = row // 48
        b["go"][OUT_OF[name], lo : lo + chunks] = value.reshape(chunks, 48, D)

    def back_feed(i):
        span = SPANS[i]
        dz = b["dz", i][...].reshape(span, D)
        dm = dz.astype(BF)
        dact = nt(dm, weight("wd", i)[...])
        dinner = (b["dg", i][...] * dact).astype(BF)
        put_slabs("s3", i, nt(dinner, weight("wu", i)[...]))
        ticket = scatter_start(b["s3", i], b["r3", i])
        if i < 3:
            b["di", i][...] = dinner
            share_rows("up", i, "fb", lambda t: b["di", i])
            start_unit("up", i)
        else:
            for part in range(2):
                cols = slice(part * 384, part * 384 + 384)
                put_unit("down", part * 384, tn(b["ac", i][:, cols], dm))
            store_global("down")
            normed2 = rows_of(b["n2", i], i)
            for part in range(2):
                cols = slice(part * 384, part * 384 + 384)
                put_unit("up", part * 384, tn(normed2[:, cols], dinner))
            store_global("up")
        b["svb"][4 * i : 4 * i + 1] = jnp.sum(dz, 0, keepdims=True)
        b["svb"][4 * i + 2 : 4 * i + 3] = jnp.sum(dinner.astype(F32), 0, keepdims=True)
        return ticket

    def norm_back(x, dy, i, j):
        hat, inv = layer_stats(x)
        b["sva"][4 * i + 2 * j : 4 * i + 2 * j + 1] = jnp.sum(dy * hat, 0, keepdims=True)
        b["sva"][4 * i + 2 * j + 1 : 4 * i + 2 * j + 2] = jnp.sum(dy, 0, keepdims=True)
        g = dy * vec(gain, 2 * i + j)
        return inv * (
            g - jnp.mean(g, -1, keepdims=True) - hat * jnp.mean(g * hat, -1, keepdims=True)
        )

    def back_middle(i, ticket):
        dn2 = summed("s3", "r3", i, ticket)
        dafter = b["dz", i][m] + norm_back(b["af", i][...], dn2, i, 1)
        b["daf", i][...] = dafter
        b["da", i][m] = dafter.astype(BF)
        return gather_start(b["da", i])

    def back_attend(i, ticket):
        span = SPANS[i]
        landed(*ticket)
        da = rows_of(b["da", i], i)
        if i < 3:
            row = lax.broadcasted_iota(jnp.int32, (span, 1), 0)
            da = jnp.where(row == 0, b["dac"][i : i + 1], da.astype(F32)).astype(BF)
        b["svb"][4 * i + 1 : 4 * i + 2] = jnp.sum(da.astype(F32), 0, keepdims=True)
        dheads = nt(da, weight("wo", i)[...]).astype(BF)
        query, keys, values = b["q", i][...], b["k", i][...], b["v", i][...]
        probs = b["pr", i][...]
        d3 = stacked(dheads)
        dprob = nt(d3, values)
        dscore = probs * (dprob - jnp.sum(dprob * probs, -1, keepdims=True))
        dscore = dscore.astype(BF)
        dquery = (folded(nn(dscore, keys), span) * scale).astype(BF)
        dkeys = (tn(dscore, stacked(query)) * scale).astype(BF)
        dvalues = tn(probs.astype(BF), d3).astype(BF)
        wq = weight("wq", i)
        part = nn(dquery, wq[0:KD]) + nn(dkeys, wq[KD : 2 * KD]) + nn(dvalues, wq[2 * KD : 3 * KD])
        put_slabs("s4", i, part)
        ticket = scatter_start(b["s4", i], b["r4", i])
        b["svb"][4 * i + 3 : 4 * i + 4, 0:KD] = jnp.sum(dquery.astype(F32), 0, keepdims=True)
        b["svb"][4 * i + 3 : 4 * i + 4, 256 : 256 + KD] = jnp.sum(
            dvalues.astype(F32), 0, keepdims=True
        )
        if i < 3:
            b["pj4", i][0] = dquery
            b["pj4", i][1] = dkeys
            b["pj4", i][2] = dvalues
            b["pj4", i][3] = b["ho", i][...]
            share_rows("qo", i, "fa", lambda t: b["pj4", i].at[t])
            b["dh", i][...] = da
            u = UNIT_OF["qo", i]
            one = UNITS[u][2][0]
            s = new("s")

            @pl.when(place[one] != 3)
            def _():
                send(b["dh", i], b["fc", u].at[place[one]], s, at(**{one: 3}))

            @pl.when(place[one] == 3)
            def _():
                b["fc", u][3] = b["dh", i][...]

            factors["fc", u] = s
            start_unit("qo", i)
            return ticket
        normed = rows_of(b["n1", i], i)
        put_unit("qo", 0, tn(dquery, normed))
        put_unit("qo", KD, tn(dkeys, normed))
        put_unit("qo", 2 * KD, tn(dvalues, normed))
        put_unit("qo", 3 * KD, tn(b["ho", i][...], da))
        store_global("qo")
        return ticket

    def back_finish(i, ticket):
        dn1 = summed("s4", "r4", i, ticket)
        dafter = b["daf", i][...]
        if i < 3:
            row = lax.broadcasted_iota(jnp.int32, (SLABS[i], 1), 0)
            dafter = jnp.where((row == 0) & (m == 0), b["dac"][i : i + 1], dafter)
        return dafter + norm_back(b["x", i][...], dn1, i, 0)

    def class_feed(dgin):
        dz = jnp.zeros((8, D), F32)
        slope = jnp.zeros((8, D), F32)
        for i in range(3):
            first = cot[OFFS[i] : OFFS[i] + 16].astype(F32)[0:1]
            dz = jnp.where(row8 == i, first + dgin[i : i + 1], dz)
            slope = jnp.where(row8 == i, b["dg", i][0:8][0:1], slope)
        dm = dz.astype(BF)
        dact = jnp.zeros((8, D), F32)
        for i in range(3):
            dact = jnp.where(row8 == i, nt(dm, weight("wd", i)[...]), dact)
        dinner = (slope * dact).astype(BF)
        dn2 = jnp.zeros((8, D), F32)
        for i in range(3):
            dn2 = jnp.where(row8 == i, nt(dinner, weight("wu", i)[...]), dn2)
        b["pc"][m] = dn2.astype(BF)
        ticket = gather_start(b["pc"])
        both = dm.astype(F32)
        dinner = dinner.astype(F32)
        for i in range(3):
            both = jnp.where(row8 == 3 + i, dinner[i : i + 1], both)
            b["svb"][4 * i : 4 * i + 1] += dz[i : i + 1]
            b["svb"][4 * i + 2 : 4 * i + 3] += dinner[i : i + 1]
        b["bc"][...] = both.astype(BF)
        b["dac"][...] = dz
        return ticket, dp_gather_start(b["bc"], b["bg"])

    def class_middle(ticket):
        landed(*ticket)
        dn2 = b["pc"][0].astype(F32)
        for k in range(1, 4):
            dn2 = dn2 + b["pc"][k].astype(F32)
        hat, inv = layer_stats(b["afc"][0])
        lead = jnp.where(m == 0, 1.0, 0.0)
        scales = jnp.zeros((8, D), F32)
        for i in range(3):
            scales = jnp.where(row8 == i, vec(gain, 2 * i + 1), scales)
            b["sva"][4 * i + 2 : 4 * i + 3] += lead * (dn2 * hat)[i : i + 1]
            b["sva"][4 * i + 3 : 4 * i + 4] += lead * dn2[i : i + 1]
        g = dn2 * scales
        b["dac"][...] += inv * (
            g - jnp.mean(g, -1, keepdims=True) - hat * jnp.mean(g * hat, -1, keepdims=True)
        )

    def halves(ref):
        n = ref.shape[0] // 2
        return ref.at[pl.ds(0, n)], ref.at[pl.ds(n, n)]

    def ring_spread(axis, slot, own, like):
        p = place[axis]
        up, down = lax.rem(p + 1, 4), lax.rem(p + 3, 4)
        to_up, to_down = at(**{axis: up}), at(**{axis: down})
        s0, s1, s2, s3 = new("s"), new("s"), new("s"), new("s")
        send(own, slot(p), s0, to_up)
        send(own, slot(p), s1, to_down)
        yield
        landed(like, s0)
        part = halves(slot(down))[0]
        send(part, part, s2, to_up)
        landed(like, s1)
        part = halves(slot(up))[1]
        send(part, part, s3, to_down)
        yield
        landed(halves(like)[0], s2)
        landed(halves(like)[1], s3)

    def sum_unit(u):
        name, view, (one, two) = UNITS[u]
        span = SPANS[view]
        g, near, gx, ga = b["g", u], b["near", u], b["gx", u], b["ga", u]
        p1, p2 = place[one], place[two]
        out = outs[name].at[view]
        yield
        landed(*factors["fa", u])
        landed(*factors["fb", u])

        def multiply(rows):
            left = b["fa", u][...].reshape(4 * span, KD)
            g[...] = tn(left, rows[...].reshape(4 * span, D)).astype(BF).reshape(4, 48, D)

        if name == "qo":
            s_da = factors["fc", u]
            fc = b["fc", u]

            @pl.when(p1 == 3)
            def _():
                wait(fc.at[pl.ds(0, 3)], rsem.at[s_da])
                multiply(fc)

            @pl.when(p1 != 3)
            def _():
                multiply(b["fb", u])

            def drain():
                @pl.when(p1 != 3)
                def _():
                    wait(fc.at[0], ssem.at[s_da])

            drains.append(drain)
        else:
            multiply(b["fb", u])
        s = new("s")
        for k in (1, 3, 2):
            t = lax.rem(p2 + k, 4)
            send(g.at[t], near.at[k - 1], s, at(**{two: t}))
        yield
        landed(near, s)
        total = g[p2].astype(F32)
        for k in range(3):
            total = total + near[k].astype(F32)
        ga[p2] = total.astype(BF)
        s = new("s")
        send(ga.at[p2], gx, s, at(x=1 - place["x"]))
        yield
        landed(gx, s)
        wait(gx, ssem.at[s])
        drains.pop()
        ga[p2] = (ga[p2].astype(F32) + gx[...].astype(F32)).astype(BF)
        s = new("s")
        for k in (1, 3, 2):
            send(ga.at[p2], ga.at[p2], s, at(**{two: lax.rem(p2 + k, 4)}))
        yield
        landed(ga.at[pl.ds(0, 3)], s)
        own = out.at[pl.ds(p1 * 4, 4)]
        store(ga, own)
        yield from ring_spread(one, lambda t: out.at[pl.ds(t * 4, 4)], ga, out.at[pl.ds(0, 4)])

    stores = []

    def store(src, dst):
        copy = pltpu.make_async_copy(src, dst, lsem.at[new("l")])
        copy.start()
        stores.append(copy)

    running = []

    def store_global(name):
        store(b["go"].at[OUT_OF[name]], outs[name].at[3])

    def start_unit(name, i):
        unit = sum_unit(UNIT_OF[name, i])
        next(unit)
        running.append(unit)

    def tick(n):
        for _ in range(min(n, len(running))):
            unit = running.pop(0)
            if next(unit, "end") != "end":
                running.append(unit)

    tickets = [None] * 3
    back = [None] * 3
    for i in range(3):
        b["n1", i][m] = norm(b["x", i][...], i, 0).astype(BF)
        tickets[i] = gather_start(b["n1", i])
    for i in range(3):
        landed(*tickets[i])
        tickets[i] = attend(i)
    for i in range(3):
        tickets[i] = middle(i, tickets[i])
    firsts = jnp.zeros((8, D), F32)
    for i in range(3):
        firsts = jnp.where(row8 == i, b["af", i][0:8][0:1], firsts)
    b["afc"][m] = firsts
    after_ticket = gather_start(b["afc"])
    for i in range(3):
        tickets[i] = feed(i, tickets[i])
    back[0] = back_feed(0)
    for i in range(3):
        tickets[i] = finish(i, tickets[i])
    back[1] = back_feed(1)
    classes = jnp.zeros((8, D), F32)
    for i in range(3):
        landed(*tickets[i])
        classes = jnp.where(row8 == i, b["zo", i][0].astype(F32)[0:1], classes)
    b["cl"][...] = classes.astype(BF)
    class_ticket = dp_gather_start(b["cl"], b["cg"])
    back[2] = back_feed(2)
    left = jnp.zeros((8, D), F32)
    for i in range(3):
        left = jnp.where(row8 == i, b["ac", i][0:16].astype(F32)[0:1], left)
        left = jnp.where(row8 == 3 + i, b["n2", i][0].astype(F32)[0:1], left)
    b["al"][...] = left.astype(BF)
    left_ticket = dp_gather_start(b["al"], b["ag"])
    for i in range(3):
        out_tok[OFFS[i] : OFFS[i] + SPANS[i]] = rows_of(b["zo", i], i)
    for i in range(3):
        back[i] = back_middle(i, back[i])
    tick(TICKS[0])

    landed(*class_ticket)
    gin = rows8_at(b["cg"], 3)
    b["gin"][...] = gin.reshape(4, 24, D)
    b["x", 3][...] = b["gin"][m]
    put_slabs("n1", 3, norm(gin, 3, 0))
    ticket = attend(3)
    landed(*cot_ticket)
    b["dz", 3][...] = rows8_at(b["ct"], 3).reshape(4, 24, D)
    tick(TICKS[1])
    ticket = middle(3, ticket)
    tick(TICKS[2])
    glob_ticket = feed(3, ticket)
    ticket = back_feed(3)
    tick(TICKS[3])
    ticket = back_middle(3, ticket)
    tick(TICKS[4])
    glob_ticket = finish(3, glob_ticket)
    ticket = back_attend(3, ticket)
    tick(TICKS[5])
    dx = back_finish(3, ticket)
    b["gdx"][m] = dx.astype(BF)
    ticket = gather_start(b["gdx"])
    landed(*glob_ticket)
    o_at = lax.broadcasted_iota(jnp.int32, (8, 96), 0)
    w_at = lax.broadcasted_iota(jnp.int32, (8, 96), 1)
    mine = ((w_at == o_at * 32 + me) & (o_at < 3)).astype(F32).astype(BF)
    out_glob[...] = nn(mine, rows_of(b["zo", 3], 3)).astype(BF)
    tick(TICKS[6])
    landed(*ticket)
    dgin = nn(mine, rows_of(b["gdx"], 3))

    landed(*after_ticket)
    ticket, right_ticket = class_feed(dgin)
    tick(TICKS[7])
    class_middle(ticket)
    for i in range(3):
        tickets[i] = back_attend(i, back[i])
    tick(TICKS[8])
    for i in range(3):
        dx = back_finish(i, tickets[i])
        base = (0, 4, 6)[i]
        for r in range(SLABS[i] // 8):
            rows = dx[8 * r : 8 * r + 8]
            b["mx"][base + r] = lam * rows
            b["ts"][base + r] = ((1.0 - lam) * rows).astype(BF)
    def invert(d, _):
        found = jnp.int32(0)
        for c in range(CLIPS):
            found = jnp.where(partner[c] == d, c, found)
        b["inv"][d] = found
        return 0

    lax.fori_loop(0, CLIPS, invert, 0)
    s = deal_start(1, lambda r: b["ts"].at[r])

    s_mp = new("s")
    for k in (2, 1, 3):
        send(b["sva"], b["svr"].at[k - 1], s_mp, (me, lax.rem(m + k, 4)))
    tick(TICKS[9])
    t = deal_turn(1, s, b["inv"])
    tick(TICKS[10])
    landed(b["svr"], s_mp)
    sva = b["sva"][...] + b["svr"][0] + b["svr"][1] + b["svr"][2]
    svb = b["svb"][...]
    b["svs", 0][...] = jnp.concatenate([sva, svb], 0).astype(BF)

    def small_start(step, axis):
        s = new("s")
        far = (1, 3, 2) if axis != "x" else (1,)
        size = 4 if axis != "x" else 2
        for k in far:
            dev = at(**{axis: lax.rem(place[axis] + k, size)})
            send(b["svs", step], b["svt", step].at[k - 1], s, dev)
        return b["svt", step].at[pl.ds(0, len(far))], s

    def small_end(step, ticket, axis):
        landed(*ticket)
        total = b["svs", step][...].astype(F32)
        for k in range(3 if axis != "x" else 1):
            total = total + b["svt", step][k].astype(F32)
        return total

    ticket = small_start(0, "y")
    taken = deal_end(1, t)
    for i in range(3):
        base = (0, 4, 6)[i]
        for r in range(SLABS[i] // 8):
            rows = b["mx"][base + r] + taken[base + r]
            b["gt", i][m, 8 * r : 8 * r + 8] = rows.astype(BF)
        tickets[i] = gather_start(b["gt", i])
    tick(TICKS[11])
    b["svs", 1][...] = small_end(0, ticket, "y").astype(BF)
    ticket = small_start(1, "z")
    tick(TICKS[12])
    for i in range(3):
        landed(*tickets[i])
        out_grad[OFFS[i] : OFFS[i] + SPANS[i]] = rows_of(b["gt", i], i)
    b["svs", 2][...] = small_end(1, ticket, "z").astype(BF)
    ticket = small_start(2, "x")
    landed(*left_ticket)
    landed(*right_ticket)
    out_left[...] = rows8_at(b["ag"], 6).astype(BF)
    out_right[...] = rows8_at(b["bg"], 6).astype(BF)
    tick(TICKS[13])
    total = small_end(2, ticket, "x")
    out_small[0:12] = total[0:12]
    out_small[12:16] = sva[12:16]
    out_small[16:28] = total[16:28]
    out_small[28:32] = svb[12:16]
    while running:
        tick(1)
    for drain in drains:
        drain()
    for copy in stores:
        copy.wait()


def shards(
    tokens,
    lengths,
    partner,
    mix_coef,
    norm_gain,
    norm_bias,
    w_qkv,
    b_qv,
    w_out,
    b_out,
    w_up,
    b_up,
    w_down,
    b_down,
    cot_tokens,
    cot_global,
):
    wq = jnp.transpose(w_qkv, (0, 2, 3, 1)).reshape(4, 3 * KD, D)
    plan = scratch_plan()
    names = list(plan)
    smem = pl.BlockSpec(memory_space=pltpu.SMEM)
    vmem = pl.BlockSpec(memory_space=pltpu.VMEM)
    hbm = pl.BlockSpec(memory_space=pl.ANY)
    unit = jax.ShapeDtypeStruct((4, 16, 48, D), BF)
    out_tok, out_glob, out_grad, small, left, right, qo, up, down = pl.pallas_call(
        functools.partial(kernel, names),
        out_shape=(
            jax.ShapeDtypeStruct((224, D), BF),
            jax.ShapeDtypeStruct((8, D), BF),
            jax.ShapeDtypeStruct((224, D), BF),
            jax.ShapeDtypeStruct((32, D), F32),
            jax.ShapeDtypeStruct((6 * CLIPS, D), BF),
            jax.ShapeDtypeStruct((6 * CLIPS, D), BF),
            unit,
            unit,
            unit,
        ),
        in_specs=[smem] * 3 + [vmem] * 9 + [hbm] * 4,
        out_specs=(vmem,) * 6 + (hbm,) * 3,
        scratch_shapes=list(plan.values()),
        compiler_params=pltpu.CompilerParams(
            collective_id=0, has_side_effects=True, vmem_limit_bytes=60 * 2**20
        ),
    )(
        partner,
        mix_coef,
        lengths,
        tokens.reshape(28, 8, D),
        cot_tokens[0],
        cot_global,
        norm_gain,
        norm_bias,
        b_out,
        b_down,
        b_up,
        b_qv,
        wq,
        w_out,
        w_up,
        w_down,
    )
    out_tok, out_glob, out_grad, gain, shift, qkv, qv, out, bout, ups, bup, downs, bdown = widen(
        out_tok,
        out_glob,
        out_grad,
        small,
        left,
        right,
        *(a.reshape(4, D, D) for a in (qo, up, down)),
    )
    return (
        out_tok,
        out_glob,
        out_grad,
        gain,
        shift,
        jnp.transpose(qkv.reshape(4, 3, KD, D), (0, 3, 1, 2)),
        qv,
        out,
        bout,
        ups,
        bup,
        downs,
        bdown,
    )


def widen_kernel(*refs):
    tok, glob, grad, small, left_d, left_u, right_d, right_u, qkv, out, up, down = refs[:12]
    o_tok, o_glob, o_grad, o_gain, o_shift, o_qkv, o_qv, o_out, o_bout, o_up, o_bup, o_down, o_bdown = refs[12:]
    o_qkv[...] = qkv[...].astype(F32)
    o_out[...] = out[...].astype(F32)
    is_view = jnp.where(pl.program_id(0) < 3, 1.0, 0.0)
    o_up[0] = up[0].astype(F32) + is_view * tn(left_u[...], right_u[...])
    o_down[0] = down[0].astype(F32) + is_view * tn(left_d[...], right_d[...])

    @pl.when((pl.program_id(0) == 0) & (pl.program_id(1) == 0))
    def _():
        o_tok[0] = tok[...]
        o_grad[0] = grad[...]
        o_glob[0] = glob[0:3]
        m = lax.axis_index("mp")

        def share(row):
            value = small[row : row + 1]
            mine = value[:, 0:KD]
            for k in range(1, 4):
                mine = jnp.where(m == k, value[:, k * KD : (k + 1) * KD], mine)
            return mine

        for i in range(4):
            for j in range(2):
                o_gain[i, j : j + 1] = share(4 * i + 2 * j)
                o_shift[i, j : j + 1] = share(4 * i + 2 * j + 1)
            row = 16 + 4 * i
            o_bdown[i : i + 1] = share(row)
            o_bout[i : i + 1] = share(row + 1)
            o_bup[i : i + 1] = small[row + 2 : row + 3]
            o_qv[i, 0:1] = small[row + 3 : row + 4, 0:KD]
            o_qv[i, 1:2] = small[row + 3 : row + 4, 256 : 256 + KD]


def widen(tok, glob, grad, small, left, right, qo, up, down):
    def whole(*shape):
        return pl.BlockSpec(shape, lambda i, j: (0,) * len(shape))

    def rows(n, base=0):
        return pl.BlockSpec((1, n, D), lambda i, j: (i, base + j, 0))

    def lefts(base):
        return pl.BlockSpec((CLIPS, 256), lambda i, j: (base + jnp.minimum(i, 2), j))

    def rights(base):
        return pl.BlockSpec((CLIPS, D), lambda i, j: (base + jnp.minimum(i, 2), 0))

    shape = jax.ShapeDtypeStruct
    return pl.pallas_call(
        widen_kernel,
        grid=(4, 3),
        in_specs=[whole(224, D), whole(8, D), whole(224, D), whole(32, D)]
        + [lefts(0), lefts(3), rights(0), rights(3)]
        + [rows(192), rows(64, 9), rows(256), rows(256)],
        out_specs=[whole(1, 224, D), whole(1, 3, D), whole(1, 224, D)]
        + [whole(4, 2, KD), whole(4, 2, KD), rows(192), whole(4, 2, KD), rows(64), whole(4, KD)]
        + [rows(256), whole(4, D), rows(256), whole(4, KD)],
        out_shape=[shape((1, 224, D), BF), shape((1, 3, D), BF), shape((1, 224, D), BF)]
        + [shape((4, 2, KD), F32), shape((4, 2, KD), F32), shape((4, 3 * KD, D), F32)]
        + [shape((4, 2, KD), F32), shape((4, KD, D), F32), shape((4, KD), F32)]
        + [shape((4, D, D), F32), shape((4, D), F32), shape((4, D, D), F32), shape((4, KD), F32)],
        compiler_params=pltpu.CompilerParams(vmem_limit_bytes=60 * 2**20),
    )(tok, glob, grad, small, left, left, right, right, qo, qo, up, down)


def solution(mesh):
    placed = (
        P("dp", None, None),
        P("dp", None),
        P(),
        P(),
        P(),
        P(),
        P(None, None, None, "mp"),
        P(None, None, "mp"),
        P(None, "mp", None),
        P(),
        P(None, None, "mp"),
        P(None, "mp"),
        P(None, "mp", None),
        P(),
        P("dp", None, None),
        P("dp", None, None),
    )
    return jax.shard_map(
        shards,
        mesh=mesh,
        in_specs=placed,
        out_specs=(
            P("dp", None, None),
            P("dp", None, None),
            P("dp", None, None),
            P(None, None, "mp"),
            P(None, None, "mp"),
            P(None, None, None, "mp"),
            P(None, None, "mp"),
            P(None, "mp", None),
            P(None, "mp"),
            P(None, None, "mp"),
            P(None, "mp"),
            P(None, "mp", None),
            P(None, "mp"),
        ),
        check_vma=False,
    )
```

```python
import functools

import jax
import jax.numpy as jnp
from jax import lax
from jax.experimental import pallas as pl
from jax.experimental.pallas import tpu as pltpu
from jax.sharding import PartitionSpec as P

HD = 64
D = 768
KD = 192
SPANS = (128, 64, 32, 96)
SLABS = (32, 16, 8, 24)
OFFS = (0, 128, 192)
CLIPS = 32
PIECES = 21
EPS = 1e-06
NEG = -1000000000.0
MESH = pl.DeviceIdType.MESH
BF = jnp.bfloat16
F32 = jnp.float32
UNITS = (
    ("down", 0, "yz"),
    ("up", 0, "zy"),
    ("down", 1, "zy"),
    ("up", 1, "yz"),
    ("down", 2, "zy"),
    ("up", 2, "yz"),
    ("qo", 0, "yz"),
    ("qo", 1, "zy"),
    ("qo", 2, "zy"),
)
UNIT_OF = {(name, view): place for place, (name, view, _) in enumerate(UNITS)}
TICKS = (0, 1, 1, 2, 2, 3, 3, 3, 3, 6, 6, 6, 6, 6)
OUT_OF = {"qo": 0, "up": 1, "down": 2}


def nn(a, b):
    return lax.dot_general(a, b, (((1,), (0,)), ((), ())), preferred_element_type=F32)


def nt(a, b):
    return lax.dot_general(a, b, (((1,), (1,)), ((), ())), preferred_element_type=F32)


def tn(a, b):
    return lax.dot_general(a, b, (((0,), (0,)), ((), ())), preferred_element_type=F32)


def gelu(inner):
    c0, c1 = 0.7978845608028654, 0.044715
    square = inner * inner
    th = jnp.tanh(c0 * inner * (1.0 + c1 * square))
    half = 0.5 * (1.0 + th)
    slope = half + 0.5 * inner * (1.0 - th * th) * c0 * (1.0 + 3.0 * c1 * square)
    return (inner * half).astype(BF), slope


def layer_stats(x):
    center = x - jnp.mean(x, -1, keepdims=True)
    spread = jnp.mean(center * center, -1, keepdims=True)
    inv = lax.rsqrt(spread + EPS)
    return center * inv, inv


def scratch_plan():
    plan = {}
    for i in range(4):
        span, slab = SPANS[i], SLABS[i]
        for name in ("n1", "s1", "n2", "s2", "zo", "s3", "da", "s4"):
            plan[name, i] = pltpu.VMEM((4, slab, D), BF)
        for name in ("r1", "r2", "r3", "r4"):
            plan[name, i] = pltpu.VMEM((3, slab, D), BF)
        for name in ("x", "af", "daf"):
            plan[name, i] = pltpu.VMEM((slab, D), F32)
        plan["dz", i] = pltpu.VMEM((4, slab, D), F32)
        for name in ("q", "k", "v", "ho"):
            plan[name, i] = pltpu.VMEM((span, KD), BF)
        plan["pr", i] = pltpu.VMEM((3 * span, span), F32)
        plan["dg", i] = pltpu.VMEM((span, D), F32)
        plan["ac", i] = pltpu.VMEM((span, D), BF)
        plan["wq", i] = pltpu.VMEM((3 * KD, D), BF)
        plan["wo", i] = pltpu.VMEM((KD, D), BF)
        plan["wu", i] = pltpu.VMEM((D, D), BF)
        plan["wd", i] = pltpu.VMEM((D, D), BF)
        if i < 3:
            plan["gt", i] = pltpu.VMEM((4, slab, D), BF)
            for name in ("ac4", "n24", "pj4"):
                plan[name, i] = pltpu.VMEM((4, span, KD), BF)
            for name in ("cz", "nr", "di", "dh"):
                plan[name, i] = pltpu.VMEM((span, D), BF)
    for turn in range(2):
        plan["pa", turn] = pltpu.VMEM((CLIPS, 8, 256), BF)
        plan["pb", turn] = pltpu.VMEM((CLIPS, 8, 256), BF)
        plan["pc", turn] = pltpu.VMEM((PIECES, 8, 256), BF)
    plan["ts"] = pltpu.VMEM((7, 8, D), BF)
    plan["mx"] = pltpu.VMEM((7, 8, D), F32)
    plan["cc"] = pltpu.VMEM((8, D), BF)
    plan["inv"] = pltpu.SMEM((CLIPS,), jnp.int32)
    plan["cl"] = pltpu.VMEM((8, D), BF)
    plan["cg"] = pltpu.VMEM((CLIPS, 8, D), BF)
    plan["ct"] = pltpu.VMEM((CLIPS, 8, D), BF)
    for name in ("bc", "dcb"):
        plan[name] = pltpu.VMEM((8, D), BF)
    for axis in "yz":
        plan["dc", axis] = pltpu.VMEM((4, 8, D), BF)
    plan["bg"] = pltpu.VMEM((CLIPS, 8, D), BF)
    plan["n20"] = pltpu.VMEM((3 * CLIPS, D), BF)
    plan["zc"] = pltpu.VMEM((4, 8, D), BF)
    plan["afc"] = pltpu.VMEM((4, 8, D), F32)
    plan["pc"] = pltpu.VMEM((4, 8, D), BF)
    plan["dac"] = pltpu.VMEM((8, D), F32)
    plan["gin"] = pltpu.VMEM((4, 24, D), F32)
    plan["gdx"] = pltpu.VMEM((4, 8, D), BF)
    plan["go"] = pltpu.VMEM((3, 16, 48, D), BF)
    for u, (name, view, _) in enumerate(UNITS):
        plan["fa", u] = pltpu.VMEM((4, SPANS[view], KD), BF)
        plan["fb", u] = pltpu.VMEM((4, SPANS[view], D), BF)
        if name == "qo":
            plan["fc", u] = pltpu.VMEM((4, SPANS[view], D), BF)
        plan["g", u] = pltpu.VMEM((4, 48, D), BF)
        plan["near", u] = pltpu.VMEM((3, 48, D), BF)
        plan["gx", u] = pltpu.VMEM((48, D), BF)
        plan["ga", u] = pltpu.VMEM((4, 48, D), BF)
    plan["sva"] = pltpu.VMEM((16, D), F32)
    plan["svb"] = pltpu.VMEM((16, D), F32)
    plan["svr"] = pltpu.VMEM((3, 16, D), F32)
    for step in range(3):
        plan["svs", step] = pltpu.VMEM((32, D), BF)
        plan["svt", step] = pltpu.VMEM((3, 32, D), BF)
    plan["ssem"] = pltpu.SemaphoreType.DMA((256,))
    plan["rsem"] = pltpu.SemaphoreType.DMA((256,))
    plan["lsem"] = pltpu.SemaphoreType.DMA((48,))
    return plan


def kernel(names, *refs):
    (
        partner,
        mix,
        lengths,
        tok,
        cot,
        cotg,
        gain,
        shift,
        b_out,
        b_down,
        b_up,
        b_qv,
        wq_all,
        wo_all,
        wu_all,
        wd_all,
        out_tok,
        out_glob,
        out_grad,
        out_small,
        out_left,
        out_right,
        out_qo,
        out_up,
        out_down,
    ) = refs[:25]
    b = dict(zip(names, refs[25:]))
    ssem, rsem, lsem = b["ssem"], b["rsem"], b["lsem"]
    outs = {"qo": out_qo, "up": out_up, "down": out_down}
    me = lax.axis_index("dp")
    m = lax.axis_index("mp")
    place = {"y": lax.div(me, 8), "x": lax.rem(lax.div(me, 4), 2), "z": lax.rem(me, 4)}

    def at(**moved):
        p = dict(place)
        p.update(moved)
        return ((p["y"] * 2 + p["x"]) * 4 + p["z"], m)

    count = {"s": 0, "l": 0}
    drains = []

    def new(kind):
        count[kind] += 1
        return count[kind] - 1

    def send(src, dst, s, dev):
        pltpu.make_async_remote_copy(
            src_ref=src,
            dst_ref=dst,
            send_sem=ssem.at[s],
            recv_sem=rsem.at[s],
            device_id=dev,
            device_id_type=MESH,
        ).start()

    def wait(like, sem):
        pltpu.make_async_copy(like, like, sem).wait()

    def landed(like, s):
        wait(like, rsem.at[s])
        drains.append(lambda: wait(like, ssem.at[s]))

    barrier = pltpu.get_barrier_semaphore()

    def greet(k, _):
        pl.semaphore_signal(
            barrier, inc=1, device_id=(lax.rem(me + k, CLIPS), m), device_id_type=MESH
        )
        return 0

    lax.fori_loop(1, CLIPS, greet, 0)
    for k in (1, 2, 3):
        pl.semaphore_signal(barrier, inc=1, device_id=(me, lax.rem(m + k, 4)), device_id_type=MESH)

    fetch = {}
    for i in range(4):
        for name, src in (("wq", wq_all), ("wo", wo_all), ("wu", wu_all), ("wd", wd_all)):
            copy = pltpu.make_async_copy(src.at[i], b[name, i], lsem.at[new("l")])
            copy.start()
            fetch[name, i] = copy

    def weight(name, i):
        if (name, i) in fetch:
            fetch.pop((name, i)).wait()
        return b[name, i]

    pl.semaphore_wait(barrier, CLIPS - 1 + 3)

    def gather_start(buf):
        s = new("s")
        for k in (2, 1, 3):
            send(buf.at[m], buf.at[m], s, (me, lax.rem(m + k, 4)))
        return buf.at[pl.ds(0, 3)], s

    def scatter_start(src, dst):
        s = new("s")
        for k in (2, 1, 3):
            t = lax.rem(m + k, 4)
            send(src.at[t], dst.at[k - 1], s, (me, t))
        return dst, s

    def dp_gather_start(src, dst):
        s = new("s")

        def step(k, _):
            send(src, dst.at[me], s, (lax.rem(me + k, CLIPS), m))
            return 0

        lax.fori_loop(1, CLIPS, step, 0)
        dst[me] = src[...]
        return dst.at[pl.ds(0, CLIPS - 1)], s

    factors = {}

    def share_rows(name, i, part, src_of):
        u = UNIT_OF[name, i]
        one = UNITS[u][2][0]
        p = place[one]
        dst = b[part, u]
        s = new("s")
        for k in (1, 3, 2):
            t = lax.rem(p + k, 4)
            send(src_of(t), dst.at[p], s, at(**{one: t}))
        dst[p] = src_of(p)[...]
        factors[part, u] = (dst.at[pl.ds(0, 3)], s)

    def rows_of(buf, i):
        span, slab = SPANS[i], SLABS[i]
        if slab % 16 == 0:
            return buf[...].reshape(span, D)
        return buf[...].astype(F32).reshape(span, D).astype(BF)

    groups = [m * 4 + r for r in range(4)] + [16 + m * 2 + r for r in range(2)] + [24 + m]

    def deal_start(turn, src_at):
        keep = b["pa", turn]
        s = new("s")
        for j in range(PIECES):

            @pl.when(me != j)
            def _():
                send(src_at(j // 3).at[:, pl.ds((j % 3) * 256, 256)], keep.at[me], s, (j, m))

            @pl.when(me == j)
            def _():
                keep[me] = src_at(j // 3)[:, (j % 3) * 256 : (j % 3) * 256 + 256]

        return s

    def few_or_all(buf, sem):
        @pl.when(me < PIECES)
        def _():
            wait(buf.at[pl.ds(0, PIECES - 1)], sem)

        @pl.when(me >= PIECES)
        def _():
            wait(buf, sem)

    def deal_turn(turn, s, index):
        keep, stage, got = b["pa", turn], b["pb", turn], b["pc", turn]
        t = new("s")

        @pl.when(me < PIECES)
        def _():
            wait(keep.at[pl.ds(0, CLIPS - 1)], rsem.at[s])
            for d in range(CLIPS):
                stage[d] = keep[index[d]]
            got[me] = stage[me]

            def step(k, _):
                d = lax.rem(me + k, CLIPS)
                send(stage.at[d], got.at[me], t, (d, m))
                return 0

            lax.fori_loop(1, CLIPS, step, 0)

        few_or_all(got, ssem.at[s])
        return t

    def deal_end(turn, t):
        stage, got = b["pb", turn], b["pc", turn]
        few_or_all(got, rsem.at[t])

        @pl.when(me < PIECES)
        def _():
            wait(stage.at[pl.ds(0, CLIPS - 1)], ssem.at[t])

        return [
            jnp.concatenate([got[3 * r + c].astype(F32) for c in range(3)], 1) for r in range(7)
        ]

    lam = mix[me]
    b["cc"][...] = jnp.zeros((8, D), BF)
    b["cc"][0:3] = cotg[0]
    s = deal_start(0, lambda r: tok.at[groups[r]])
    cot_ticket = dp_gather_start(b["cc"], b["ct"])
    t = deal_turn(0, s, partner)
    for i in range(3):
        row = lax.broadcasted_iota(jnp.int32, (SPANS[i], 1), 0)
        dz = jnp.where(row == 0, 0.0, cot[OFFS[i] : OFFS[i] + SPANS[i]].astype(F32))
        b["cz", i][...] = dz.astype(BF)
        b["dz", i][...] = dz.reshape(4, SLABS[i], D)
        share_rows("down", i, "fb", lambda t: b["cz", i])
    taken = deal_end(0, t)
    for r in range(7):
        value = lam * tok[groups[r]].astype(F32) + (1.0 - lam) * taken[r]
        if r < 4:
            b["x", 0][8 * r : 8 * r + 8] = value
        elif r < 6:
            b["x", 1][8 * (r - 4) : 8 * (r - 4) + 8] = value
        else:
            b["x", 2][...] = value

    def vec(ref, row):
        if len(ref.shape) == 3:
            return ref[row // 2, row % 2 : row % 2 + 1, :]
        return ref[row : row + 1, :]

    def norm(x, i, j):
        hat, _ = layer_stats(x)
        return hat * vec(gain, 2 * i + j) + vec(shift, 2 * i + j)

    def head_mask(h):
        lane = lax.broadcasted_iota(jnp.int32, (1, KD), 1)
        return (lane >= h * HD) & (lane < h * HD + HD)

    masks = [head_mask(h) for h in range(3)]
    zero = jnp.zeros((), BF)

    def stacked(a):
        return jnp.concatenate(
            [jnp.where(masks[h], a.astype(F32), 0.0) for h in range(3)], 0
        ).astype(BF)

    def folded(a, span):
        total = None
        for h in range(3):
            part = jnp.where(masks[h], a[h * span : (h + 1) * span], 0.0)
            total = part if total is None else total + part
        return total

    scale = HD ** (-0.5)

    def attend(i):
        span = SPANS[i]
        normed = rows_of(b["n1", i], i)
        wq = weight("wq", i)
        query = (nt(normed, wq[0:KD]) + vec(b_qv, 2 * i)).astype(BF)
        keys = nt(normed, wq[KD : 2 * KD]).astype(BF)
        values = (nt(normed, wq[2 * KD : 3 * KD]) + vec(b_qv, 2 * i + 1)).astype(BF)
        b["q", i][...] = query
        b["k", i][...] = keys
        b["v", i][...] = values
        scores = nt(stacked(query), keys) * scale
        if i < 3:
            col = lax.broadcasted_iota(jnp.int32, (1, span), 1)
            scores = jnp.where(col < lengths[0, i], scores, NEG)
        expo = jnp.exp(scores - jnp.max(scores, -1, keepdims=True))
        probs = expo / jnp.sum(expo, -1, keepdims=True)
        b["pr", i][...] = probs
        heads_out = folded(nn(probs.astype(BF), values), span).astype(BF)
        b["ho", i][...] = heads_out
        part = nn(heads_out, weight("wo", i)[...])
        b["s1", i][...] = part.astype(BF).reshape(4, SLABS[i], D) if SLABS[i] % 16 == 0 else (
            part.reshape(4, SLABS[i], D).astype(BF)
        )
        ticket = scatter_start(b["s1", i], b["r1", i])
        if i < 3:
            b["nr", i][...] = normed
            share_rows("qo", i, "fb", lambda t: b["nr", i])
        return ticket

    def put_slabs(name, i, value):
        b[name, i][...] = value.reshape(4, SLABS[i], D).astype(BF)

    def summed(send_name, recv_name, i, ticket):
        landed(*ticket)
        got = b[recv_name, i]
        total = b[send_name, i][m].astype(F32)
        for k in range(3):
            total = total + got[k].astype(F32)
        return total

    def middle(i, ticket):
        after = b["x", i][...] + summed("s1", "r1", i, ticket) + vec(b_out, i)
        b["af", i][...] = after
        b["n2", i][m] = norm(after, i, 1).astype(BF)
        return gather_start(b["n2", i])

    def feed(i, ticket):
        landed(*ticket)
        normed2 = rows_of(b["n2", i], i)
        inner = nn(normed2, weight("wu", i)[...]) + vec(b_up, i)
        active, b["dg", i][...] = gelu(inner)
        b["ac", i][...] = active
        part = nn(active, weight("wd", i)[...])
        put_slabs("s2", i, part)
        if i == 3:
            return scatter_start(b["s2", i], b["r2", i])
        for t in range(4):
            cols = slice(t * KD, t * KD + KD)
            b["ac4", i][t] = active[:, cols]
            b["n24", i][t] = normed2[:, cols]
        return part[0:8][0:1]

    def feed_send(i):
        share_rows("down", i, "fa", lambda t: b["ac4", i].at[t])
        start_unit("down", i)
        share_rows("up", i, "fa", lambda t: b["n24", i].at[t])
        return scatter_start(b["s2", i], b["r2", i])

    def finish(i, ticket):
        total = b["af", i][...] + summed("s2", "r2", i, ticket) + vec(b_down, i)
        b["zo", i][m] = total.astype(BF)
        return gather_start(b["zo", i])

    row8 = lax.broadcasted_iota(jnp.int32, (8, 1), 0)

    def rows8_at(buf, kinds):
        r_at = lax.broadcasted_iota(jnp.int32, (32 * kinds, 256), 0)
        k_at = lax.broadcasted_iota(jnp.int32, (32 * kinds, 256), 1)
        pick = (k_at == lax.rem(r_at, 32) * 8 + lax.div(r_at, 32)).astype(F32).astype(BF)
        return nn(pick, buf[...].astype(F32).reshape(256, D).astype(BF))

    def put_unit(name, row, value):
        value = value.astype(BF)
        chunks = value.shape[0] // 48
        lo = row // 48
        b["go"][OUT_OF[name], lo : lo + chunks] = value.reshape(chunks, 48, D)

    def back_feed(i):
        span = SPANS[i]
        dz = b["dz", i][...].reshape(span, D)
        dm = dz.astype(BF)
        dact = nt(dm, weight("wd", i)[...])
        dinner = (b["dg", i][...] * dact).astype(BF)
        put_slabs("s3", i, nt(dinner, weight("wu", i)[...]))
        if i < 3:
            b["di", i][...] = dinner
        else:
            ticket = scatter_start(b["s3", i], b["r3", i])
            for part in range(2):
                cols = slice(part * 384, part * 384 + 384)
                put_unit("down", part * 384, tn(b["ac", i][:, cols], dm))
            store_global("down")
            normed2 = rows_of(b["n2", i], i)
            for part in range(2):
                cols = slice(part * 384, part * 384 + 384)
                put_unit("up", part * 384, tn(normed2[:, cols], dinner))
            store_global("up")
        b["svb"][4 * i : 4 * i + 1] = jnp.sum(dz, 0, keepdims=True)
        b["svb"][4 * i + 2 : 4 * i + 3] = jnp.sum(dinner.astype(F32), 0, keepdims=True)
        return ticket if i == 3 else None

    def back_feed_send(i):
        share_rows("up", i, "fb", lambda t: b["di", i])
        start_unit("up", i)
        return scatter_start(b["s3", i], b["r3", i])

    def norm_back(x, dy, i, j):
        hat, inv = layer_stats(x)
        b["sva"][4 * i + 2 * j : 4 * i + 2 * j + 1] = jnp.sum(dy * hat, 0, keepdims=True)
        b["sva"][4 * i + 2 * j + 1 : 4 * i + 2 * j + 2] = jnp.sum(dy, 0, keepdims=True)
        g = dy * vec(gain, 2 * i + j)
        return inv * (
            g - jnp.mean(g, -1, keepdims=True) - hat * jnp.mean(g * hat, -1, keepdims=True)
        )

    def back_middle(i, ticket):
        dn2 = summed("s3", "r3", i, ticket)
        dafter = b["dz", i][m] + norm_back(b["af", i][...], dn2, i, 1)
        b["daf", i][...] = dafter
        b["da", i][m] = dafter.astype(BF)
        return gather_start(b["da", i])

    def with_class_row(rows, first):
        row = lax.broadcasted_iota(jnp.int32, (rows.shape[0], 1), 0)
        return jnp.where(row == 0, first, rows.astype(F32)).astype(BF)

    def rows_send(i, ticket):
        landed(*ticket)
        b["dh", i][...] = rows_of(b["da", i], i)
        u = UNIT_OF["qo", i]
        one = UNITS[u][2][0]
        s = new("s")

        @pl.when(place[one] != 3)
        def _():
            send(b["dh", i], b["fc", u].at[place[one]], s, at(**{one: 3}))

        @pl.when(place[one] == 3)
        def _():
            b["fc", u][3] = b["dh", i][...]

        factors["fc", u] = s

    def class_rows_send():
        b["dcb"][...] = b["dac"][...].astype(BF)
        for axis in "yz":
            dst, p = b["dc", axis], place[axis]
            s = new("s")
            for k in (1, 3, 2):
                t = lax.rem(p + k, 4)
                send(b["dcb"], dst.at[p], s, at(**{axis: t}))
            dst[p] = b["dcb"][...]
            factors["dc", axis] = (dst.at[pl.ds(0, 3)], s)

    def back_attend(i, ticket):
        span = SPANS[i]
        if i < 3:
            da = with_class_row(b["dh", i][...], b["dac"][i : i + 1])
        else:
            landed(*ticket)
            da = rows_of(b["da", i], i)
        b["svb"][4 * i + 1 : 4 * i + 2] = jnp.sum(da.astype(F32), 0, keepdims=True)
        dheads = nt(da, weight("wo", i)[...]).astype(BF)
        query, keys, values = b["q", i][...], b["k", i][...], b["v", i][...]
        probs = b["pr", i][...]
        d3 = stacked(dheads)
        dprob = nt(d3, values)
        dscore = probs * (dprob - jnp.sum(dprob * probs, -1, keepdims=True))
        dscore = dscore.astype(BF)
        dquery = (folded(nn(dscore, keys), span) * scale).astype(BF)
        dkeys = (tn(dscore, stacked(query)) * scale).astype(BF)
        dvalues = tn(probs.astype(BF), d3).astype(BF)
        wq = weight("wq", i)
        part = nn(dquery, wq[0:KD]) + nn(dkeys, wq[KD : 2 * KD]) + nn(dvalues, wq[2 * KD : 3 * KD])
        put_slabs("s4", i, part)
        ticket = scatter_start(b["s4", i], b["r4", i])
        b["svb"][4 * i + 3 : 4 * i + 4, 0:KD] = jnp.sum(dquery.astype(F32), 0, keepdims=True)
        b["svb"][4 * i + 3 : 4 * i + 4, 256 : 256 + KD] = jnp.sum(
            dvalues.astype(F32), 0, keepdims=True
        )
        if i < 3:
            b["pj4", i][0] = dquery
            b["pj4", i][1] = dkeys
            b["pj4", i][2] = dvalues
            b["pj4", i][3] = b["ho", i][...]
            share_rows("qo", i, "fa", lambda t: b["pj4", i].at[t])
            start_unit("qo", i)
            return ticket
        normed = rows_of(b["n1", i], i)
        put_unit("qo", 0, tn(dquery, normed))
        put_unit("qo", KD, tn(dkeys, normed))
        put_unit("qo", 2 * KD, tn(dvalues, normed))
        put_unit("qo", 3 * KD, tn(b["ho", i][...], da))
        store_global("qo")
        return ticket

    def back_finish(i, ticket):
        dn1 = summed("s4", "r4", i, ticket)
        dafter = b["daf", i][...]
        if i < 3:
            row = lax.broadcasted_iota(jnp.int32, (SLABS[i], 1), 0)
            dafter = jnp.where((row == 0) & (m == 0), b["dac"][i : i + 1], dafter)
        return dafter + norm_back(b["x", i][...], dn1, i, 0)

    def class_feed(dgin):
        dz = jnp.zeros((8, D), F32)
        slope = jnp.zeros((8, D), F32)
        for i in range(3):
            first = cot[OFFS[i] : OFFS[i] + 16].astype(F32)[0:1]
            dz = jnp.where(row8 == i, first + dgin[i : i + 1], dz)
            slope = jnp.where(row8 == i, b["dg", i][0:8][0:1], slope)
        dm = dz.astype(BF)
        dact = jnp.zeros((8, D), F32)
        for i in range(3):
            dact = jnp.where(row8 == i, nt(dm, weight("wd", i)[...]), dact)
        dinner = (slope * dact).astype(BF)
        dn2 = jnp.zeros((8, D), F32)
        for i in range(3):
            dn2 = jnp.where(row8 == i, nt(dinner, weight("wu", i)[...]), dn2)
        b["pc"][m] = dn2.astype(BF)
        ticket = gather_start(b["pc"])
        both = dm.astype(F32)
        dinner = dinner.astype(F32)
        for i in range(3):
            both = jnp.where(row8 == 3 + i, dinner[i : i + 1], both)
            b["svb"][4 * i : 4 * i + 1] += dz[i : i + 1]
            b["svb"][4 * i + 2 : 4 * i + 3] += dinner[i : i + 1]
        b["bc"][...] = both.astype(BF)
        b["dac"][...] = dz
        return ticket, dp_gather_start(b["bc"], b["bg"])

    def class_middle(ticket):
        landed(*ticket)
        dn2 = b["pc"][0].astype(F32)
        for k in range(1, 4):
            dn2 = dn2 + b["pc"][k].astype(F32)
        hat, inv = layer_stats(b["afc"][0])
        lead = jnp.where(m == 0, 1.0, 0.0)
        scales = jnp.zeros((8, D), F32)
        for i in range(3):
            scales = jnp.where(row8 == i, vec(gain, 2 * i + 1), scales)
            b["sva"][4 * i + 2 : 4 * i + 3] += lead * (dn2 * hat)[i : i + 1]
            b["sva"][4 * i + 3 : 4 * i + 4] += lead * dn2[i : i + 1]
        g = dn2 * scales
        b["dac"][...] += inv * (
            g - jnp.mean(g, -1, keepdims=True) - hat * jnp.mean(g * hat, -1, keepdims=True)
        )

    def halves(ref):
        n = ref.shape[0] // 2
        return ref.at[pl.ds(0, n)], ref.at[pl.ds(n, n)]

    def ring_spread(axis, slot, own, like):
        p = place[axis]
        up, down = lax.rem(p + 1, 4), lax.rem(p + 3, 4)
        to_up, to_down = at(**{axis: up}), at(**{axis: down})
        s0, s1, s2, s3 = new("s"), new("s"), new("s"), new("s")
        send(own, slot(p), s0, to_up)
        send(own, slot(p), s1, to_down)
        yield
        landed(like, s0)
        part = halves(slot(down))[0]
        send(part, part, s2, to_up)
        landed(like, s1)
        part = halves(slot(up))[1]
        send(part, part, s3, to_down)
        yield
        landed(halves(like)[0], s2)
        landed(halves(like)[1], s3)

    def sum_unit(u):
        name, view, (one, two) = UNITS[u]
        span = SPANS[view]
        g, near, gx, ga = b["g", u], b["near", u], b["gx", u], b["ga", u]
        p1, p2 = place[one], place[two]
        out = outs[name].at[view]
        yield
        landed(*factors["fa", u])
        landed(*factors["fb", u])

        def multiply(rows):
            left = b["fa", u][...].reshape(4 * span, KD)
            g[...] = tn(left, rows).astype(BF).reshape(4, 48, D)

        if name == "qo":
            s_da = factors["fc", u]
            fc = b["fc", u]
            if ("dc", one) in factors:
                landed(*factors.pop(("dc", one)))

            @pl.when(p1 == 3)
            def _():
                wait(fc.at[pl.ds(0, 3)], rsem.at[s_da])
                first = b["dc", one][...].astype(F32)
                multiply(
                    jnp.concatenate(
                        [with_class_row(fc[k], first[k, view : view + 1]) for k in range(4)], 0
                    )
                )

            @pl.when(p1 != 3)
            def _():
                multiply(b["fb", u][...].reshape(4 * span, D))

            def drain():
                @pl.when(p1 != 3)
                def _():
                    wait(fc.at[0], ssem.at[s_da])

            drains.append(drain)
        else:
            multiply(b["fb", u][...].reshape(4 * span, D))
        s = new("s")
        for k in (1, 3, 2):
            t = lax.rem(p2 + k, 4)
            send(g.at[t], near.at[k - 1], s, at(**{two: t}))
        yield
        landed(near, s)
        total = g[p2].astype(F32)
        for k in range(3):
            total = total + near[k].astype(F32)
        ga[p2] = total.astype(BF)
        s = new("s")
        send(ga.at[p2], gx, s, at(x=1 - place["x"]))
        yield
        landed(gx, s)
        wait(gx, ssem.at[s])
        drains.pop()
        ga[p2] = (ga[p2].astype(F32) + gx[...].astype(F32)).astype(BF)
        s = new("s")
        for k in (1, 3, 2):
            send(ga.at[p2], ga.at[p2], s, at(**{two: lax.rem(p2 + k, 4)}))
        yield
        landed(ga.at[pl.ds(0, 3)], s)
        own = out.at[pl.ds(p1 * 4, 4)]
        store(ga, own)
        yield from ring_spread(one, lambda t: out.at[pl.ds(t * 4, 4)], ga, out.at[pl.ds(0, 4)])

    stores = []

    def store(src, dst):
        copy = pltpu.make_async_copy(src, dst, lsem.at[new("l")])
        copy.start()
        stores.append(copy)

    running = []

    def store_global(name):
        store(b["go"].at[OUT_OF[name]], outs[name].at[3])

    def start_unit(name, i):
        unit = sum_unit(UNIT_OF[name, i])
        next(unit)
        running.append(unit)

    def tick(n):
        for _ in range(min(n, len(running))):
            unit = running.pop(0)
            if next(unit, "end") != "end":
                running.append(unit)

    tickets = [None] * 3
    back = [None] * 3
    for i in range(3):
        b["n1", i][m] = norm(b["x", i][...], i, 0).astype(BF)
        tickets[i] = gather_start(b["n1", i])
    for i in range(3):
        landed(*tickets[i])
        tickets[i] = attend(i)
    for i in range(3):
        tickets[i] = middle(i, tickets[i])
    firsts = jnp.zeros((8, D), F32)
    for i in range(3):
        firsts = jnp.where(row8 == i, b["af", i][0:8][0:1], firsts)
    b["afc"][m] = firsts
    after_ticket = gather_start(b["afc"])
    parts = jnp.zeros((8, D), F32)
    for i in range(3):
        parts = jnp.where(row8 == i, feed(i, tickets[i]), parts)
    b["zc"][m] = parts.astype(BF)
    ticket = gather_start(b["zc"])
    back_feed(0)
    landed(*after_ticket)
    classes = b["afc"][0]
    for i in range(3):
        classes = jnp.where(row8 == i, classes + vec(b_down, i), classes)
    landed(*ticket)
    for k in range(4):
        classes = classes + b["zc"][k].astype(F32)
    for i in range(3):
        classes = jnp.where(row8 == 3 + i, b["n2", i][0].astype(F32)[0:1], classes)
    b["cl"][...] = classes.astype(BF)
    class_ticket = dp_gather_start(b["cl"], b["cg"])
    for i in range(3):
        tickets[i] = feed_send(i)
    back[0] = back_feed_send(0)
    for i in (1, 2):
        back_feed(i)
        back[i] = back_feed_send(i)
    tick(TICKS[0])

    landed(*class_ticket)
    gathered = rows8_at(b["cg"], 6)
    gin = gathered[0:96]
    b["n20"][...] = gathered[96:192].astype(BF)
    b["gin"][...] = gin.reshape(4, 24, D)
    b["x", 3][...] = b["gin"][m]
    put_slabs("n1", 3, norm(gin, 3, 0))
    ticket = attend(3)
    landed(*cot_ticket)
    b["dz", 3][...] = rows8_at(b["ct"], 3).reshape(4, 24, D)
    tick(TICKS[1])
    ticket = middle(3, ticket)
    for i in range(3):
        tickets[i] = finish(i, tickets[i])
    tick(TICKS[2])
    glob_ticket = feed(3, ticket)
    ticket = back_feed(3)
    back[0] = back_middle(0, back[0])
    tick(TICKS[3])
    ticket = back_middle(3, ticket)
    for i in (1, 2):
        back[i] = back_middle(i, back[i])
    tick(TICKS[4])
    ticket = back_attend(3, ticket)
    for i in range(3):
        rows_send(i, back[i])
    tick(TICKS[5])
    dx = back_finish(3, ticket)
    o_at = lax.broadcasted_iota(jnp.int32, (8, 24), 0)
    w_at = lax.broadcasted_iota(jnp.int32, (8, 24), 1) + m * 24
    chosen = ((w_at == o_at * 32 + me) & (o_at < 3)).astype(F32).astype(BF)
    b["gdx"][m] = nn(chosen, dx.astype(BF)).astype(BF)
    ticket = gather_start(b["gdx"])
    glob_ticket = finish(3, glob_ticket)
    o_at = lax.broadcasted_iota(jnp.int32, (8, 96), 0)
    w_at = lax.broadcasted_iota(jnp.int32, (8, 96), 1)
    mine = ((w_at == o_at * 32 + me) & (o_at < 3)).astype(F32).astype(BF)
    tick(TICKS[6])
    landed(*ticket)
    dgin = b["gdx"][0].astype(F32)
    for k in range(1, 4):
        dgin = dgin + b["gdx"][k].astype(F32)

    ticket, right_ticket = class_feed(dgin)
    for i in range(3):
        landed(*tickets[i])
        out_tok[OFFS[i] : OFFS[i] + SPANS[i]] = rows_of(b["zo", i], i)
    landed(*glob_ticket)
    out_glob[...] = nn(mine, rows_of(b["zo", 3], 3)).astype(BF)
    tick(TICKS[7])
    class_middle(ticket)
    class_rows_send()
    for i in range(3):
        tickets[i] = back_attend(i, None)
    tick(TICKS[8])
    for i in range(3):
        dx = back_finish(i, tickets[i])
        base = (0, 4, 6)[i]
        for r in range(SLABS[i] // 8):
            rows = dx[8 * r : 8 * r + 8]
            b["mx"][base + r] = lam * rows
            b["ts"][base + r] = ((1.0 - lam) * rows).astype(BF)
    def invert(d, _):
        found = jnp.int32(0)
        for c in range(CLIPS):
            found = jnp.where(partner[c] == d, c, found)
        b["inv"][d] = found
        return 0

    lax.fori_loop(0, CLIPS, invert, 0)
    s = deal_start(1, lambda r: b["ts"].at[r])

    s_mp = new("s")
    for k in (2, 1, 3):
        send(b["sva"], b["svr"].at[k - 1], s_mp, (me, lax.rem(m + k, 4)))
    tick(TICKS[9])
    t = deal_turn(1, s, b["inv"])
    tick(TICKS[10])
    landed(b["svr"], s_mp)
    sva = b["sva"][...] + b["svr"][0] + b["svr"][1] + b["svr"][2]
    svb = b["svb"][...]
    b["svs", 0][...] = jnp.concatenate([sva, svb], 0).astype(BF)

    def small_start(step, axis):
        s = new("s")
        far = (1, 3, 2) if axis != "x" else (1,)
        size = 4 if axis != "x" else 2
        for k in far:
            dev = at(**{axis: lax.rem(place[axis] + k, size)})
            send(b["svs", step], b["svt", step].at[k - 1], s, dev)
        return b["svt", step].at[pl.ds(0, len(far))], s

    def small_end(step, ticket, axis):
        landed(*ticket)
        total = b["svs", step][...].astype(F32)
        for k in range(3 if axis != "x" else 1):
            total = total + b["svt", step][k].astype(F32)
        return total

    ticket = small_start(0, "y")
    taken = deal_end(1, t)
    for i in range(3):
        base = (0, 4, 6)[i]
        for r in range(SLABS[i] // 8):
            rows = b["mx"][base + r] + taken[base + r]
            b["gt", i][m, 8 * r : 8 * r + 8] = rows.astype(BF)
        tickets[i] = gather_start(b["gt", i])
    tick(TICKS[11])
    b["svs", 1][...] = small_end(0, ticket, "y").astype(BF)
    ticket = small_start(1, "z")
    tick(TICKS[12])
    for i in range(3):
        landed(*tickets[i])
        out_grad[OFFS[i] : OFFS[i] + SPANS[i]] = rows_of(b["gt", i], i)
    b["svs", 2][...] = small_end(1, ticket, "z").astype(BF)
    ticket = small_start(2, "x")
    landed(*right_ticket)
    for i in range(3):
        rows = b["n20"][CLIPS * i : CLIPS * i + CLIPS]
        active, _ = gelu(nn(rows, weight("wu", i)[...]) + vec(b_up, i))
        out_left[CLIPS * i : CLIPS * i + CLIPS] = active
    out_left[3 * CLIPS : 6 * CLIPS] = b["n20"][...]
    out_right[...] = rows8_at(b["bg"], 6).astype(BF)
    tick(TICKS[13])
    total = small_end(2, ticket, "x")
    out_small[0:12] = total[0:12]
    out_small[12:16] = sva[12:16]
    out_small[16:28] = total[16:28]
    out_small[28:32] = svb[12:16]
    while running:
        tick(1)
    for drain in drains:
        drain()
    for copy in stores:
        copy.wait()


def shards(
    tokens,
    lengths,
    partner,
    mix_coef,
    norm_gain,
    norm_bias,
    w_qkv,
    b_qv,
    w_out,
    b_out,
    w_up,
    b_up,
    w_down,
    b_down,
    cot_tokens,
    cot_global,
):
    wq = jnp.transpose(w_qkv, (0, 2, 3, 1)).reshape(4, 3 * KD, D)
    plan = scratch_plan()
    names = list(plan)
    smem = pl.BlockSpec(memory_space=pltpu.SMEM)
    vmem = pl.BlockSpec(memory_space=pltpu.VMEM)
    hbm = pl.BlockSpec(memory_space=pl.ANY)
    unit = jax.ShapeDtypeStruct((4, 16, 48, D), BF)
    out_tok, out_glob, out_grad, small, left, right, qo, up, down = pl.pallas_call(
        functools.partial(kernel, names),
        out_shape=(
            jax.ShapeDtypeStruct((224, D), BF),
            jax.ShapeDtypeStruct((8, D), BF),
            jax.ShapeDtypeStruct((224, D), BF),
            jax.ShapeDtypeStruct((32, D), F32),
            jax.ShapeDtypeStruct((6 * CLIPS, D), BF),
            jax.ShapeDtypeStruct((6 * CLIPS, D), BF),
            unit,
            unit,
            unit,
        ),
        in_specs=[smem] * 3 + [vmem] * 9 + [hbm] * 4,
        out_specs=(vmem,) * 6 + (hbm,) * 3,
        scratch_shapes=list(plan.values()),
        compiler_params=pltpu.CompilerParams(
            collective_id=0, has_side_effects=True, vmem_limit_bytes=60 * 2**20
        ),
    )(
        partner,
        mix_coef,
        lengths,
        tokens.reshape(28, 8, D),
        cot_tokens[0],
        cot_global,
        norm_gain,
        norm_bias,
        b_out,
        b_down,
        b_up,
        b_qv,
        wq,
        w_out,
        w_up,
        w_down,
    )
    out_tok, out_glob, out_grad, gain, shift, qkv, qv, out, bout, ups, bup, downs, bdown = widen(
        out_tok,
        out_glob,
        out_grad,
        small,
        left,
        right,
        *(a.reshape(4, D, D) for a in (qo, up, down)),
    )
    return (
        out_tok,
        out_glob,
        out_grad,
        gain,
        shift,
        jnp.transpose(qkv.reshape(4, 3, KD, D), (0, 3, 1, 2)),
        qv,
        out,
        bout,
        ups,
        bup,
        downs,
        bdown,
    )


def widen_kernel(*refs):
    tok, glob, grad, small, left, right, qo, up, down = refs[:9]
    o_tok, o_glob, o_grad, o_gain, o_shift, o_qkv, o_qv, o_out, o_bout, o_up, o_bup, o_down, o_bdown = refs[9:22]
    held, wide, sem_in, sem_out, sem_same = refs[22:]
    order = [(i, a) for i in (3, 0, 1, 2) for a in range(3)]
    fetches = []
    for n, (i, a) in enumerate(order):
        copy = pltpu.make_async_copy((qo, up, down)[a].at[i], held.at[n], sem_in.at[n])
        copy.start()
        fetches.append(copy)
    same = []
    for n, (src, dst) in enumerate(((tok, o_tok.at[0]), (grad, o_grad.at[0]))):
        copy = pltpu.make_async_copy(src, dst, sem_same.at[n])
        copy.start()
        same.append(copy)
    o_glob[0] = glob[0:3]
    m = lax.axis_index("mp")

    def share(row):
        value = small[row : row + 1]
        mine = value[:, 0:KD]
        for k in range(1, 4):
            mine = jnp.where(m == k, value[:, k * KD : (k + 1) * KD], mine)
        return mine

    for i in range(4):
        for j in range(2):
            o_gain[i, j : j + 1] = share(4 * i + 2 * j)
            o_shift[i, j : j + 1] = share(4 * i + 2 * j + 1)
        row = 16 + 4 * i
        o_bdown[i : i + 1] = share(row)
        o_bout[i : i + 1] = share(row + 1)
        o_bup[i : i + 1] = small[row + 2 : row + 3]
        o_qv[i, 0:1] = small[row + 3 : row + 4, 0:KD]
        o_qv[i, 1:2] = small[row + 3 : row + 4, 256 : 256 + KD]
    slots = wide.shape[0]
    busy = [[] for _ in range(slots)]
    for n, (i, a) in enumerate(order):
        slot = n % slots
        fetches[n].wait()
        for copy in busy[slot]:
            copy.wait()
        value = held[n].astype(F32)
        if a > 0 and i < 3:
            base = CLIPS * (3 * (a == 1) + i)
            value = value + tn(left[base : base + CLIPS], right[base : base + CLIPS])
        wide[slot] = value
        src = wide.at[slot]
        if a == 0:
            pairs = (
                (src.at[pl.ds(0, 3 * KD)], o_qkv.at[i]),
                (src.at[pl.ds(3 * KD, KD)], o_out.at[i]),
            )
        else:
            pairs = ((src, (o_up, o_down)[a - 1].at[i]),)
        busy[slot] = []
        for k, (part, dst) in enumerate(pairs):
            copy = pltpu.make_async_copy(part, dst, sem_out.at[slot, k])
            copy.start()
            busy[slot].append(copy)
    for copies in busy:
        for copy in copies:
            copy.wait()
    for copy in same:
        copy.wait()


def widen(tok, glob, grad, small, left, right, qo, up, down):
    shape = jax.ShapeDtypeStruct
    vmem = pl.BlockSpec(memory_space=pltpu.VMEM)
    hbm = pl.BlockSpec(memory_space=pl.ANY)
    return pl.pallas_call(
        widen_kernel,
        in_specs=[hbm, vmem, hbm, vmem, vmem, vmem, hbm, hbm, hbm],
        out_specs=[hbm, vmem, hbm, vmem, vmem, hbm, vmem, hbm, vmem, hbm, vmem, hbm, vmem],
        out_shape=[shape((1, 224, D), BF), shape((1, 3, D), BF), shape((1, 224, D), BF)]
        + [shape((4, 2, KD), F32), shape((4, 2, KD), F32), shape((4, 3 * KD, D), F32)]
        + [shape((4, 2, KD), F32), shape((4, KD, D), F32), shape((4, KD), F32)]
        + [shape((4, D, D), F32), shape((4, D), F32), shape((4, D, D), F32), shape((4, KD), F32)],
        scratch_shapes=[
            pltpu.VMEM((12, D, D), BF),
            pltpu.VMEM((5, D, D), F32),
            pltpu.SemaphoreType.DMA((12,)),
            pltpu.SemaphoreType.DMA((5, 2)),
            pltpu.SemaphoreType.DMA((2,)),
        ],
        compiler_params=pltpu.CompilerParams(vmem_limit_bytes=60 * 2**20),
    )(tok, glob, grad, small, left, right, qo, up, down)


def solution(mesh):
    placed = (
        P("dp", None, None),
        P("dp", None),
        P(),
        P(),
        P(),
        P(),
        P(None, None, None, "mp"),
        P(None, None, "mp"),
        P(None, "mp", None),
        P(),
        P(None, None, "mp"),
        P(None, "mp"),
        P(None, "mp", None),
        P(),
        P("dp", None, None),
        P("dp", None, None),
    )
    return jax.shard_map(
        shards,
        mesh=mesh,
        in_specs=placed,
        out_specs=(
            P("dp", None, None),
            P("dp", None, None),
            P("dp", None, None),
            P(None, None, "mp"),
            P(None, None, "mp"),
            P(None, None, None, "mp"),
            P(None, None, "mp"),
            P(None, "mp", None),
            P(None, "mp"),
            P(None, None, "mp"),
            P(None, "mp"),
            P(None, "mp", None),
            P(None, "mp"),
        ),
        check_vma=False,
    )
```

```python
import functools

import jax
import jax.numpy as jnp
from jax import lax
from jax.experimental import pallas as pl
from jax.experimental.pallas import tpu as pltpu
from jax.sharding import PartitionSpec as P

HD = 64
D = 768
KD = 192
SPANS = (128, 64, 32, 96)
SLABS = (32, 16, 8, 24)
OFFS = (0, 128, 192)
CLIPS = 32
PIECES = 21
EPS = 1e-06
NEG = -1000000000.0
MESH = pl.DeviceIdType.MESH
BF = jnp.bfloat16
F32 = jnp.float32
UNITS = (
    ("down", 0, "yz"),
    ("up", 0, "zy"),
    ("down", 1, "zy"),
    ("up", 1, "yz"),
    ("down", 2, "zy"),
    ("up", 2, "yz"),
    ("qo", 0, "yz"),
    ("qo", 1, "zy"),
    ("qo", 2, "zy"),
)
UNIT_OF = {(name, view): place for place, (name, view, _) in enumerate(UNITS)}
TICKS = (0, 1, 1, 2, 2, 3, 3, 3, 3, 6, 6, 6, 6, 6)
OUT_OF = {"qo": 0, "up": 1, "down": 2}


def nn(a, b):
    return lax.dot_general(a, b, (((1,), (0,)), ((), ())), preferred_element_type=F32)


def nt(a, b):
    return lax.dot_general(a, b, (((1,), (1,)), ((), ())), preferred_element_type=F32)


def tn(a, b):
    return lax.dot_general(a, b, (((0,), (0,)), ((), ())), preferred_element_type=F32)


def gelu(inner):
    c0, c1 = 0.7978845608028654, 0.044715
    square = inner * inner
    th = jnp.tanh(c0 * inner * (1.0 + c1 * square))
    half = 0.5 * (1.0 + th)
    slope = half + 0.5 * inner * (1.0 - th * th) * c0 * (1.0 + 3.0 * c1 * square)
    return (inner * half).astype(BF), slope


def layer_stats(x):
    center = x - jnp.mean(x, -1, keepdims=True)
    spread = jnp.mean(center * center, -1, keepdims=True)
    inv = lax.rsqrt(spread + EPS)
    return center * inv, inv


def scratch_plan():
    plan = {}
    for i in range(4):
        span, slab = SPANS[i], SLABS[i]
        for name in ("n1", "s1", "n2", "s2", "zo", "s3", "da", "s4"):
            plan[name, i] = pltpu.VMEM((4, slab, D), BF)
        for name in ("r1", "r2", "r3", "r4"):
            plan[name, i] = pltpu.VMEM((3, slab, D), BF)
        for name in ("x", "af", "daf"):
            plan[name, i] = pltpu.VMEM((slab, D), F32)
        plan["dz", i] = pltpu.VMEM((4, slab, D), F32)
        for name in ("q", "k", "v", "ho"):
            plan[name, i] = pltpu.VMEM((span, KD), BF)
        plan["pr", i] = pltpu.VMEM((3 * span, span), F32)
        plan["dg", i] = pltpu.VMEM((span, D), F32)
        plan["ac", i] = pltpu.VMEM((span, D), BF)
        plan["wq", i] = pltpu.VMEM((3 * KD, D), BF)
        plan["wo", i] = pltpu.VMEM((KD, D), BF)
        plan["wu", i] = pltpu.VMEM((D, D), BF)
        plan["wd", i] = pltpu.VMEM((D, D), BF)
        if i < 3:
            plan["gt", i] = pltpu.VMEM((4, slab, D), BF)
            for name in ("ac4", "n24", "pj4"):
                plan[name, i] = pltpu.VMEM((4, span, KD), BF)
            for name in ("cz", "nr", "di", "dh"):
                plan[name, i] = pltpu.VMEM((span, D), BF)
    for turn in range(2):
        plan["pa", turn] = pltpu.VMEM((CLIPS, 8, 256), BF)
        plan["pb", turn] = pltpu.VMEM((CLIPS, 8, 256), BF)
        plan["pc", turn] = pltpu.VMEM((PIECES, 8, 256), BF)
    plan["ts"] = pltpu.VMEM((7, 8, D), BF)
    plan["mx"] = pltpu.VMEM((7, 8, D), F32)
    plan["cc"] = pltpu.VMEM((8, D), BF)
    plan["inv"] = pltpu.SMEM((CLIPS,), jnp.int32)
    plan["cl"] = pltpu.VMEM((8, D), BF)
    plan["cg"] = pltpu.VMEM((CLIPS, 8, D), BF)
    plan["ct"] = pltpu.VMEM((CLIPS, 8, D), BF)
    for name in ("bc", "dcb"):
        plan[name] = pltpu.VMEM((8, D), BF)
    for axis in "yz":
        plan["dc", axis] = pltpu.VMEM((4, 8, D), BF)
    plan["bg"] = pltpu.VMEM((CLIPS, 8, D), BF)
    plan["n20"] = pltpu.VMEM((3 * CLIPS, D), BF)
    plan["zc"] = pltpu.VMEM((4, 8, D), BF)
    plan["afc"] = pltpu.VMEM((4, 8, D), F32)
    plan["pc"] = pltpu.VMEM((4, 8, D), BF)
    plan["dac"] = pltpu.VMEM((8, D), F32)
    plan["gin"] = pltpu.VMEM((4, 24, D), F32)
    plan["gdx"] = pltpu.VMEM((4, 8, D), BF)
    plan["go"] = pltpu.VMEM((3, 16, 48, D), BF)
    for u, (name, view, _) in enumerate(UNITS):
        plan["fa", u] = pltpu.VMEM((4, SPANS[view], KD), BF)
        plan["fb", u] = pltpu.VMEM((4, SPANS[view], D), BF)
        if name == "qo":
            plan["fc", u] = pltpu.VMEM((4, SPANS[view], D), BF)
        plan["g", u] = pltpu.VMEM((4, 48, D), BF)
        plan["near", u] = pltpu.VMEM((3, 48, D), BF)
        plan["gx", u] = pltpu.VMEM((48, D), BF)
        plan["ga", u] = pltpu.VMEM((4, 48, D), BF)
    plan["sva"] = pltpu.VMEM((16, D), F32)
    plan["svb"] = pltpu.VMEM((16, D), F32)
    plan["svr"] = pltpu.VMEM((3, 16, D), F32)
    for step in range(3):
        plan["svs", step] = pltpu.VMEM((32, D), BF)
        plan["svt", step] = pltpu.VMEM((3, 32, D), BF)
    plan["ssem"] = pltpu.SemaphoreType.DMA((256,))
    plan["rsem"] = pltpu.SemaphoreType.DMA((256,))
    plan["lsem"] = pltpu.SemaphoreType.DMA((48,))
    return plan


def kernel(names, *refs):
    (
        partner,
        mix,
        lengths,
        tok,
        cot,
        cotg,
        gain,
        shift,
        b_out,
        b_down,
        b_up,
        b_qv,
        wq_all,
        wo_all,
        wu_all,
        wd_all,
        out_tok,
        out_glob,
        out_grad,
        out_small,
        out_left,
        out_right,
        out_qo,
        out_up,
        out_down,
    ) = refs[:25]
    b = dict(zip(names, refs[25:]))
    ssem, rsem, lsem = b["ssem"], b["rsem"], b["lsem"]
    outs = {"qo": out_qo, "up": out_up, "down": out_down}
    me = lax.axis_index("dp")
    m = lax.axis_index("mp")
    place = {"y": lax.div(me, 8), "x": lax.rem(lax.div(me, 4), 2), "z": lax.rem(me, 4)}

    def at(**moved):
        p = dict(place)
        p.update(moved)
        return ((p["y"] * 2 + p["x"]) * 4 + p["z"], m)

    count = {"s": 0, "l": 0}
    drains = []

    def new(kind):
        count[kind] += 1
        return count[kind] - 1

    def send(src, dst, s, dev):
        pltpu.make_async_remote_copy(
            src_ref=src,
            dst_ref=dst,
            send_sem=ssem.at[s],
            recv_sem=rsem.at[s],
            device_id=dev,
            device_id_type=MESH,
        ).start()

    def wait(like, sem):
        pltpu.make_async_copy(like, like, sem).wait()

    def landed(like, s):
        wait(like, rsem.at[s])
        drains.append(lambda: wait(like, ssem.at[s]))

    barrier = pltpu.get_barrier_semaphore()

    def greet(k, _):
        pl.semaphore_signal(
            barrier, inc=1, device_id=(lax.rem(me + k, CLIPS), m), device_id_type=MESH
        )
        return 0

    lax.fori_loop(1, CLIPS, greet, 0)
    for k in (1, 2, 3):
        pl.semaphore_signal(barrier, inc=1, device_id=(me, lax.rem(m + k, 4)), device_id_type=MESH)

    fetch = {}
    for i in range(4):
        for name, src in (("wq", wq_all), ("wo", wo_all), ("wu", wu_all), ("wd", wd_all)):
            copy = pltpu.make_async_copy(src.at[i], b[name, i], lsem.at[new("l")])
            copy.start()
            fetch[name, i] = copy

    def weight(name, i):
        if (name, i) in fetch:
            fetch.pop((name, i)).wait()
        return b[name, i]

    pl.semaphore_wait(barrier, CLIPS - 1 + 3)

    def gather_start(buf):
        s = new("s")
        for k in (2, 1, 3):
            send(buf.at[m], buf.at[m], s, (me, lax.rem(m + k, 4)))
        return buf.at[pl.ds(0, 3)], s

    def scatter_start(src, dst):
        s = new("s")
        for k in (2, 1, 3):
            t = lax.rem(m + k, 4)
            send(src.at[t], dst.at[k - 1], s, (me, t))
        return dst, s

    def dp_gather_start(src, dst):
        s = new("s")

        def step(k, _):
            send(src, dst.at[me], s, (lax.rem(me + k, CLIPS), m))
            return 0

        lax.fori_loop(1, CLIPS, step, 0)
        dst[me] = src[...]
        return dst.at[pl.ds(0, CLIPS - 1)], s

    factors = {}

    def share_rows(name, i, part, src_of):
        u = UNIT_OF[name, i]
        one = UNITS[u][2][0]
        p = place[one]
        dst = b[part, u]
        s = new("s")
        for k in (1, 3, 2):
            t = lax.rem(p + k, 4)
            send(src_of(t), dst.at[p], s, at(**{one: t}))
        dst[p] = src_of(p)[...]
        factors[part, u] = (dst.at[pl.ds(0, 3)], s)

    def rows_of(buf, i):
        span, slab = SPANS[i], SLABS[i]
        if slab % 16 == 0:
            return buf[...].reshape(span, D)
        return buf[...].astype(F32).reshape(span, D).astype(BF)

    groups = [m * 4 + r for r in range(4)] + [16 + m * 2 + r for r in range(2)] + [24 + m]

    def deal_start(turn, src_at):
        keep = b["pa", turn]
        s = new("s")
        for j in range(PIECES):

            @pl.when(me != j)
            def _():
                send(src_at(j // 3).at[:, pl.ds((j % 3) * 256, 256)], keep.at[me], s, (j, m))

            @pl.when(me == j)
            def _():
                keep[me] = src_at(j // 3)[:, (j % 3) * 256 : (j % 3) * 256 + 256]

        return s

    def few_or_all(buf, sem):
        @pl.when(me < PIECES)
        def _():
            wait(buf.at[pl.ds(0, PIECES - 1)], sem)

        @pl.when(me >= PIECES)
        def _():
            wait(buf, sem)

    def deal_turn(turn, s, index):
        keep, stage, got = b["pa", turn], b["pb", turn], b["pc", turn]
        t = new("s")

        @pl.when(me < PIECES)
        def _():
            wait(keep.at[pl.ds(0, CLIPS - 1)], rsem.at[s])
            for d in range(CLIPS):
                stage[d] = keep[index[d]]
            got[me] = stage[me]

            def step(k, _):
                d = lax.rem(me + k, CLIPS)
                send(stage.at[d], got.at[me], t, (d, m))
                return 0

            lax.fori_loop(1, CLIPS, step, 0)

        few_or_all(got, ssem.at[s])
        return t

    def deal_end(turn, t):
        stage, got = b["pb", turn], b["pc", turn]
        few_or_all(got, rsem.at[t])

        @pl.when(me < PIECES)
        def _():
            wait(stage.at[pl.ds(0, CLIPS - 1)], ssem.at[t])

        return [
            jnp.concatenate([got[3 * r + c].astype(F32) for c in range(3)], 1) for r in range(7)
        ]

    lam = mix[me]
    b["cc"][...] = jnp.zeros((8, D), BF)
    b["cc"][0:3] = cotg[0]
    s = deal_start(0, lambda r: tok.at[groups[r]])
    cot_ticket = dp_gather_start(b["cc"], b["ct"])
    t = deal_turn(0, s, partner)
    for i in range(3):
        row = lax.broadcasted_iota(jnp.int32, (SPANS[i], 1), 0)
        dz = jnp.where(row == 0, 0.0, cot[OFFS[i] : OFFS[i] + SPANS[i]].astype(F32))
        b["cz", i][...] = dz.astype(BF)
        b["dz", i][...] = dz.reshape(4, SLABS[i], D)
        share_rows("down", i, "fb", lambda t: b["cz", i])
    taken = deal_end(0, t)
    for r in range(7):
        value = lam * tok[groups[r]].astype(F32) + (1.0 - lam) * taken[r]
        if r < 4:
            b["x", 0][8 * r : 8 * r + 8] = value
        elif r < 6:
            b["x", 1][8 * (r - 4) : 8 * (r - 4) + 8] = value
        else:
            b["x", 2][...] = value

    def vec(ref, row):
        if len(ref.shape) == 3:
            return ref[row // 2, row % 2 : row % 2 + 1, :]
        return ref[row : row + 1, :]

    def norm(x, i, j):
        hat, _ = layer_stats(x)
        return hat * vec(gain, 2 * i + j) + vec(shift, 2 * i + j)

    def head_mask(h):
        lane = lax.broadcasted_iota(jnp.int32, (1, KD), 1)
        return (lane >= h * HD) & (lane < h * HD + HD)

    masks = [head_mask(h) for h in range(3)]
    zero = jnp.zeros((), BF)

    def stacked(a):
        return jnp.concatenate(
            [jnp.where(masks[h], a.astype(F32), 0.0) for h in range(3)], 0
        ).astype(BF)

    def folded(a, span):
        total = None
        for h in range(3):
            part = jnp.where(masks[h], a[h * span : (h + 1) * span], 0.0)
            total = part if total is None else total + part
        return total

    scale = HD ** (-0.5)

    def attend(i):
        span = SPANS[i]
        normed = rows_of(b["n1", i], i)
        wq = weight("wq", i)
        query = (nt(normed, wq[0:KD]) + vec(b_qv, 2 * i)).astype(BF)
        keys = nt(normed, wq[KD : 2 * KD]).astype(BF)
        values = (nt(normed, wq[2 * KD : 3 * KD]) + vec(b_qv, 2 * i + 1)).astype(BF)
        b["q", i][...] = query
        b["k", i][...] = keys
        b["v", i][...] = values
        scores = nt(stacked(query), keys) * scale
        if i < 3:
            col = lax.broadcasted_iota(jnp.int32, (1, span), 1)
            scores = jnp.where(col < lengths[0, i], scores, NEG)
        expo = jnp.exp(scores - jnp.max(scores, -1, keepdims=True))
        probs = expo / jnp.sum(expo, -1, keepdims=True)
        b["pr", i][...] = probs
        heads_out = folded(nn(probs.astype(BF), values), span).astype(BF)
        b["ho", i][...] = heads_out
        part = nn(heads_out, weight("wo", i)[...])
        b["s1", i][...] = part.astype(BF).reshape(4, SLABS[i], D) if SLABS[i] % 16 == 0 else (
            part.reshape(4, SLABS[i], D).astype(BF)
        )
        ticket = scatter_start(b["s1", i], b["r1", i])
        if i < 3:
            b["nr", i][...] = normed
            share_rows("qo", i, "fb", lambda t: b["nr", i])
        return ticket

    def put_slabs(name, i, value):
        b[name, i][...] = value.reshape(4, SLABS[i], D).astype(BF)

    def summed(send_name, recv_name, i, ticket):
        landed(*ticket)
        got = b[recv_name, i]
        total = b[send_name, i][m].astype(F32)
        for k in range(3):
            total = total + got[k].astype(F32)
        return total

    def middle(i, ticket):
        after = b["x", i][...] + summed("s1", "r1", i, ticket) + vec(b_out, i)
        b["af", i][...] = after
        b["n2", i][m] = norm(after, i, 1).astype(BF)
        return gather_start(b["n2", i])

    def feed(i, ticket):
        landed(*ticket)
        normed2 = rows_of(b["n2", i], i)
        inner = nn(normed2, weight("wu", i)[...]) + vec(b_up, i)
        active, b["dg", i][...] = gelu(inner)
        b["ac", i][...] = active
        part = nn(active, weight("wd", i)[...])
        put_slabs("s2", i, part)
        if i == 3:
            return scatter_start(b["s2", i], b["r2", i])
        for t in range(4):
            cols = slice(t * KD, t * KD + KD)
            b["ac4", i][t] = active[:, cols]
            b["n24", i][t] = normed2[:, cols]
        return part[0:8][0:1]

    def feed_send(i):
        share_rows("down", i, "fa", lambda t: b["ac4", i].at[t])
        start_unit("down", i)
        share_rows("up", i, "fa", lambda t: b["n24", i].at[t])
        return scatter_start(b["s2", i], b["r2", i])

    def finish(i, ticket):
        total = b["af", i][...] + summed("s2", "r2", i, ticket) + vec(b_down, i)
        b["zo", i][m] = total.astype(BF)
        return gather_start(b["zo", i])

    row8 = lax.broadcasted_iota(jnp.int32, (8, 1), 0)

    def rows8_at(buf, kinds):
        r_at = lax.broadcasted_iota(jnp.int32, (32 * kinds, 256), 0)
        k_at = lax.broadcasted_iota(jnp.int32, (32 * kinds, 256), 1)
        pick = (k_at == lax.rem(r_at, 32) * 8 + lax.div(r_at, 32)).astype(F32).astype(BF)
        return nn(pick, buf[...].astype(F32).reshape(256, D).astype(BF))

    def put_unit(name, row, value):
        value = value.astype(BF)
        chunks = value.shape[0] // 48
        lo = row // 48
        b["go"][OUT_OF[name], lo : lo + chunks] = value.reshape(chunks, 48, D)

    def back_feed(i):
        span = SPANS[i]
        dz = b["dz", i][...].reshape(span, D)
        dm = dz.astype(BF)
        dact = nt(dm, weight("wd", i)[...])
        dinner = (b["dg", i][...] * dact).astype(BF)
        put_slabs("s3", i, nt(dinner, weight("wu", i)[...]))
        if i < 3:
            b["di", i][...] = dinner
        else:
            ticket = scatter_start(b["s3", i], b["r3", i])
            for part in range(2):
                cols = slice(part * 384, part * 384 + 384)
                put_unit("down", part * 384, tn(b["ac", i][:, cols], dm))
            store_global("down")
            normed2 = rows_of(b["n2", i], i)
            for part in range(2):
                cols = slice(part * 384, part * 384 + 384)
                put_unit("up", part * 384, tn(normed2[:, cols], dinner))
            store_global("up")
        b["svb"][4 * i : 4 * i + 1] = jnp.sum(dz, 0, keepdims=True)
        b["svb"][4 * i + 2 : 4 * i + 3] = jnp.sum(dinner.astype(F32), 0, keepdims=True)
        return ticket if i == 3 else None

    def back_feed_send(i):
        share_rows("up", i, "fb", lambda t: b["di", i])
        start_unit("up", i)
        return scatter_start(b["s3", i], b["r3", i])

    def norm_back(x, dy, i, j):
        hat, inv = layer_stats(x)
        b["sva"][4 * i + 2 * j : 4 * i + 2 * j + 1] = jnp.sum(dy * hat, 0, keepdims=True)
        b["sva"][4 * i + 2 * j + 1 : 4 * i + 2 * j + 2] = jnp.sum(dy, 0, keepdims=True)
        g = dy * vec(gain, 2 * i + j)
        return inv * (
            g - jnp.mean(g, -1, keepdims=True) - hat * jnp.mean(g * hat, -1, keepdims=True)
        )

    def back_middle(i, ticket):
        dn2 = summed("s3", "r3", i, ticket)
        dafter = b["dz", i][m] + norm_back(b["af", i][...], dn2, i, 1)
        b["daf", i][...] = dafter
        b["da", i][m] = dafter.astype(BF)
        return gather_start(b["da", i])

    def with_class_row(rows, first):
        row = lax.broadcasted_iota(jnp.int32, (rows.shape[0], 1), 0)
        return jnp.where(row == 0, first, rows.astype(F32)).astype(BF)

    def rows_send(i, ticket):
        landed(*ticket)
        b["dh", i][...] = rows_of(b["da", i], i)
        u = UNIT_OF["qo", i]
        one = UNITS[u][2][0]
        s = new("s")

        @pl.when(place[one] != 3)
        def _():
            send(b["dh", i], b["fc", u].at[place[one]], s, at(**{one: 3}))

        @pl.when(place[one] == 3)
        def _():
            b["fc", u][3] = b["dh", i][...]

        factors["fc", u] = s

    def class_rows_send():
        b["dcb"][...] = b["dac"][...].astype(BF)
        for axis in "yz":
            dst, p = b["dc", axis], place[axis]
            s = new("s")
            for k in (1, 3, 2):
                t = lax.rem(p + k, 4)
                send(b["dcb"], dst.at[p], s, at(**{axis: t}))
            dst[p] = b["dcb"][...]
            factors["dc", axis] = (dst.at[pl.ds(0, 3)], s)

    def back_attend(i, ticket):
        span = SPANS[i]
        if i < 3:
            da = with_class_row(b["dh", i][...], b["dac"][i : i + 1])
        else:
            landed(*ticket)
            da = rows_of(b["da", i], i)
        b["svb"][4 * i + 1 : 4 * i + 2] = jnp.sum(da.astype(F32), 0, keepdims=True)
        dheads = nt(da, weight("wo", i)[...]).astype(BF)
        query, keys, values = b["q", i][...], b["k", i][...], b["v", i][...]
        probs = b["pr", i][...]
        d3 = stacked(dheads)
        dprob = nt(d3, values)
        dscore = probs * (dprob - jnp.sum(dprob * probs, -1, keepdims=True))
        dscore = dscore.astype(BF)
        dquery = (folded(nn(dscore, keys), span) * scale).astype(BF)
        dkeys = (tn(dscore, stacked(query)) * scale).astype(BF)
        dvalues = tn(probs.astype(BF), d3).astype(BF)
        wq = weight("wq", i)
        part = nn(dquery, wq[0:KD]) + nn(dkeys, wq[KD : 2 * KD]) + nn(dvalues, wq[2 * KD : 3 * KD])
        put_slabs("s4", i, part)
        ticket = scatter_start(b["s4", i], b["r4", i])
        b["svb"][4 * i + 3 : 4 * i + 4, 0:KD] = jnp.sum(dquery.astype(F32), 0, keepdims=True)
        b["svb"][4 * i + 3 : 4 * i + 4, 256 : 256 + KD] = jnp.sum(
            dvalues.astype(F32), 0, keepdims=True
        )
        if i < 3:
            b["pj4", i][0] = dquery
            b["pj4", i][1] = dkeys
            b["pj4", i][2] = dvalues
            b["pj4", i][3] = b["ho", i][...]
            share_rows("qo", i, "fa", lambda t: b["pj4", i].at[t])
            start_unit("qo", i)
            return ticket
        normed = rows_of(b["n1", i], i)
        put_unit("qo", 0, tn(dquery, normed))
        put_unit("qo", KD, tn(dkeys, normed))
        put_unit("qo", 2 * KD, tn(dvalues, normed))
        put_unit("qo", 3 * KD, tn(b["ho", i][...], da))
        store_global("qo")
        return ticket

    def back_finish(i, ticket):
        dn1 = summed("s4", "r4", i, ticket)
        dafter = b["daf", i][...]
        if i < 3:
            row = lax.broadcasted_iota(jnp.int32, (SLABS[i], 1), 0)
            dafter = jnp.where((row == 0) & (m == 0), b["dac"][i : i + 1], dafter)
        return dafter + norm_back(b["x", i][...], dn1, i, 0)

    def class_feed(dgin):
        dz = jnp.zeros((8, D), F32)
        slope = jnp.zeros((8, D), F32)
        for i in range(3):
            first = cot[OFFS[i] : OFFS[i] + 16].astype(F32)[0:1]
            dz = jnp.where(row8 == i, first + dgin[i : i + 1], dz)
            slope = jnp.where(row8 == i, b["dg", i][0:8][0:1], slope)
        dm = dz.astype(BF)
        dact = jnp.zeros((8, D), F32)
        for i in range(3):
            dact = jnp.where(row8 == i, nt(dm, weight("wd", i)[...]), dact)
        dinner = (slope * dact).astype(BF)
        dn2 = jnp.zeros((8, D), F32)
        for i in range(3):
            dn2 = jnp.where(row8 == i, nt(dinner, weight("wu", i)[...]), dn2)
        b["pc"][m] = dn2.astype(BF)
        ticket = gather_start(b["pc"])
        both = dm.astype(F32)
        dinner = dinner.astype(F32)
        for i in range(3):
            both = jnp.where(row8 == 3 + i, dinner[i : i + 1], both)
            b["svb"][4 * i : 4 * i + 1] += dz[i : i + 1]
            b["svb"][4 * i + 2 : 4 * i + 3] += dinner[i : i + 1]
        b["bc"][...] = both.astype(BF)
        b["dac"][...] = dz
        return ticket, dp_gather_start(b["bc"], b["bg"])

    def class_middle(ticket):
        landed(*ticket)
        dn2 = b["pc"][0].astype(F32)
        for k in range(1, 4):
            dn2 = dn2 + b["pc"][k].astype(F32)
        hat, inv = layer_stats(b["afc"][0])
        lead = jnp.where(m == 0, 1.0, 0.0)
        scales = jnp.zeros((8, D), F32)
        for i in range(3):
            scales = jnp.where(row8 == i, vec(gain, 2 * i + 1), scales)
            b["sva"][4 * i + 2 : 4 * i + 3] += lead * (dn2 * hat)[i : i + 1]
            b["sva"][4 * i + 3 : 4 * i + 4] += lead * dn2[i : i + 1]
        g = dn2 * scales
        b["dac"][...] += inv * (
            g - jnp.mean(g, -1, keepdims=True) - hat * jnp.mean(g * hat, -1, keepdims=True)
        )

    def halves(ref):
        n = ref.shape[0] // 2
        return ref.at[pl.ds(0, n)], ref.at[pl.ds(n, n)]

    def ring_spread(axis, slot, own, like):
        p = place[axis]
        up, down = lax.rem(p + 1, 4), lax.rem(p + 3, 4)
        to_up, to_down = at(**{axis: up}), at(**{axis: down})
        s0, s1, s2, s3 = new("s"), new("s"), new("s"), new("s")
        send(own, slot(p), s0, to_up)
        send(own, slot(p), s1, to_down)
        yield
        landed(like, s0)
        part = halves(slot(down))[0]
        send(part, part, s2, to_up)
        landed(like, s1)
        part = halves(slot(up))[1]
        send(part, part, s3, to_down)
        yield
        landed(halves(like)[0], s2)
        landed(halves(like)[1], s3)

    def sum_unit(u):
        name, view, (one, two) = UNITS[u]
        span = SPANS[view]
        g, near, gx, ga = b["g", u], b["near", u], b["gx", u], b["ga", u]
        p1, p2 = place[one], place[two]
        out = outs[name].at[view]
        yield
        landed(*factors["fa", u])
        landed(*factors["fb", u])

        def multiply(rows):
            left = b["fa", u][...].reshape(4 * span, KD)
            g[...] = tn(left, rows).astype(BF).reshape(4, 48, D)

        if name == "qo":
            s_da = factors["fc", u]
            fc = b["fc", u]
            if ("dc", one) in factors:
                landed(*factors.pop(("dc", one)))

            @pl.when(p1 == 3)
            def _():
                wait(fc.at[pl.ds(0, 3)], rsem.at[s_da])
                first = b["dc", one][...].astype(F32)
                multiply(
                    jnp.concatenate(
                        [with_class_row(fc[k], first[k, view : view + 1]) for k in range(4)], 0
                    )
                )

            @pl.when(p1 != 3)
            def _():
                multiply(b["fb", u][...].reshape(4 * span, D))

            def drain():
                @pl.when(p1 != 3)
                def _():
                    wait(fc.at[0], ssem.at[s_da])

            drains.append(drain)
        else:
            multiply(b["fb", u][...].reshape(4 * span, D))
        s = new("s")
        for k in (1, 3, 2):
            t = lax.rem(p2 + k, 4)
            send(g.at[t], near.at[k - 1], s, at(**{two: t}))
        yield
        landed(near, s)
        total = g[p2].astype(F32)
        for k in range(3):
            total = total + near[k].astype(F32)
        ga[p2] = total.astype(BF)
        s = new("s")
        send(ga.at[p2], gx, s, at(x=1 - place["x"]))
        yield
        landed(gx, s)
        wait(gx, ssem.at[s])
        drains.pop()
        ga[p2] = (ga[p2].astype(F32) + gx[...].astype(F32)).astype(BF)
        s = new("s")
        for k in (1, 3, 2):
            send(ga.at[p2], ga.at[p2], s, at(**{two: lax.rem(p2 + k, 4)}))
        yield
        landed(ga.at[pl.ds(0, 3)], s)
        own = out.at[pl.ds(p1 * 4, 4)]
        store(ga, own)
        yield from ring_spread(one, lambda t: out.at[pl.ds(t * 4, 4)], ga, out.at[pl.ds(0, 4)])

    stores = []

    def store(src, dst):
        copy = pltpu.make_async_copy(src, dst, lsem.at[new("l")])
        copy.start()
        stores.append(copy)

    running = []

    def store_global(name):
        store(b["go"].at[OUT_OF[name]], outs[name].at[3])

    def start_unit(name, i):
        unit = sum_unit(UNIT_OF[name, i])
        next(unit)
        running.append(unit)

    def tick(n):
        for _ in range(min(n, len(running))):
            unit = running.pop(0)
            if next(unit, "end") != "end":
                running.append(unit)

    tickets = [None] * 3
    back = [None] * 3
    for i in range(3):
        b["n1", i][m] = norm(b["x", i][...], i, 0).astype(BF)
        tickets[i] = gather_start(b["n1", i])
    for i in range(3):
        landed(*tickets[i])
        tickets[i] = attend(i)
    for i in range(3):
        tickets[i] = middle(i, tickets[i])
    firsts = jnp.zeros((8, D), F32)
    for i in range(3):
        firsts = jnp.where(row8 == i, b["af", i][0:8][0:1], firsts)
    b["afc"][m] = firsts
    after_ticket = gather_start(b["afc"])
    parts = jnp.zeros((8, D), F32)
    for i in range(3):
        parts = jnp.where(row8 == i, feed(i, tickets[i]), parts)
    b["zc"][m] = parts.astype(BF)
    ticket = gather_start(b["zc"])
    back_feed(0)
    landed(*after_ticket)
    classes = b["afc"][0]
    for i in range(3):
        classes = jnp.where(row8 == i, classes + vec(b_down, i), classes)
    landed(*ticket)
    for k in range(4):
        classes = classes + b["zc"][k].astype(F32)
    for i in range(3):
        classes = jnp.where(row8 == 3 + i, b["n2", i][0].astype(F32)[0:1], classes)
    b["cl"][...] = classes.astype(BF)
    class_ticket = dp_gather_start(b["cl"], b["cg"])
    for i in range(3):
        tickets[i] = feed_send(i)
    back[0] = back_feed_send(0)
    for i in (1, 2):
        back_feed(i)
        back[i] = back_feed_send(i)
    tick(TICKS[0])

    landed(*class_ticket)
    gathered = rows8_at(b["cg"], 6)
    gin = gathered[0:96]
    b["n20"][...] = gathered[96:192].astype(BF)
    b["gin"][...] = gin.reshape(4, 24, D)
    b["x", 3][...] = b["gin"][m]
    put_slabs("n1", 3, norm(gin, 3, 0))
    ticket = attend(3)
    landed(*cot_ticket)
    b["dz", 3][...] = rows8_at(b["ct"], 3).reshape(4, 24, D)
    tick(TICKS[1])
    ticket = middle(3, ticket)
    for i in range(3):
        tickets[i] = finish(i, tickets[i])
    tick(TICKS[2])
    glob_ticket = feed(3, ticket)
    ticket = back_feed(3)
    back[0] = back_middle(0, back[0])
    tick(TICKS[3])
    ticket = back_middle(3, ticket)
    for i in (1, 2):
        back[i] = back_middle(i, back[i])
    tick(TICKS[4])
    ticket = back_attend(3, ticket)
    for i in range(3):
        rows_send(i, back[i])
    tick(TICKS[5])
    dx = back_finish(3, ticket)
    o_at = lax.broadcasted_iota(jnp.int32, (8, 24), 0)
    w_at = lax.broadcasted_iota(jnp.int32, (8, 24), 1) + m * 24
    chosen = ((w_at == o_at * 32 + me) & (o_at < 3)).astype(F32).astype(BF)
    b["gdx"][m] = nn(chosen, dx.astype(BF)).astype(BF)
    ticket = gather_start(b["gdx"])
    glob_ticket = finish(3, glob_ticket)
    o_at = lax.broadcasted_iota(jnp.int32, (8, 96), 0)
    w_at = lax.broadcasted_iota(jnp.int32, (8, 96), 1)
    mine = ((w_at == o_at * 32 + me) & (o_at < 3)).astype(F32).astype(BF)
    tick(TICKS[6])
    landed(*ticket)
    dgin = b["gdx"][0].astype(F32)
    for k in range(1, 4):
        dgin = dgin + b["gdx"][k].astype(F32)

    ticket, right_ticket = class_feed(dgin)
    for i in range(3):
        landed(*tickets[i])
        out_tok[OFFS[i] : OFFS[i] + SPANS[i]] = rows_of(b["zo", i], i)
    landed(*glob_ticket)
    out_glob[...] = nn(mine, rows_of(b["zo", 3], 3)).astype(BF)
    tick(TICKS[7])
    class_middle(ticket)
    class_rows_send()
    for i in range(3):
        tickets[i] = back_attend(i, None)
    tick(TICKS[8])
    for i in range(3):
        dx = back_finish(i, tickets[i])
        base = (0, 4, 6)[i]
        for r in range(SLABS[i] // 8):
            rows = dx[8 * r : 8 * r + 8]
            b["mx"][base + r] = lam * rows
            b["ts"][base + r] = ((1.0 - lam) * rows).astype(BF)
    def invert(d, _):
        found = jnp.int32(0)
        for c in range(CLIPS):
            found = jnp.where(partner[c] == d, c, found)
        b["inv"][d] = found
        return 0

    lax.fori_loop(0, CLIPS, invert, 0)
    s = deal_start(1, lambda r: b["ts"].at[r])

    s_mp = new("s")
    for k in (2, 1, 3):
        send(b["sva"], b["svr"].at[k - 1], s_mp, (me, lax.rem(m + k, 4)))
    tick(TICKS[9])
    t = deal_turn(1, s, b["inv"])
    tick(TICKS[10])
    landed(b["svr"], s_mp)
    sva = b["sva"][...] + b["svr"][0] + b["svr"][1] + b["svr"][2]
    svb = b["svb"][...]
    b["svs", 0][...] = jnp.concatenate([sva, svb], 0).astype(BF)

    def small_start(step, axis):
        s = new("s")
        far = (1, 3, 2) if axis != "x" else (1,)
        size = 4 if axis != "x" else 2
        for k in far:
            dev = at(**{axis: lax.rem(place[axis] + k, size)})
            send(b["svs", step], b["svt", step].at[k - 1], s, dev)
        return b["svt", step].at[pl.ds(0, len(far))], s

    def small_end(step, ticket, axis):
        landed(*ticket)
        total = b["svs", step][...].astype(F32)
        for k in range(3 if axis != "x" else 1):
            total = total + b["svt", step][k].astype(F32)
        return total

    ticket = small_start(0, "y")
    taken = deal_end(1, t)
    for i in range(3):
        base = (0, 4, 6)[i]
        for r in range(SLABS[i] // 8):
            rows = b["mx"][base + r] + taken[base + r]
            b["gt", i][m, 8 * r : 8 * r + 8] = rows.astype(BF)
        tickets[i] = gather_start(b["gt", i])
    tick(TICKS[11])
    b["svs", 1][...] = small_end(0, ticket, "y").astype(BF)
    ticket = small_start(1, "z")
    tick(TICKS[12])
    for i in range(3):
        landed(*tickets[i])
        out_grad[OFFS[i] : OFFS[i] + SPANS[i]] = rows_of(b["gt", i], i)
    b["svs", 2][...] = small_end(1, ticket, "z").astype(BF)
    ticket = small_start(2, "x")
    landed(*right_ticket)
    for i in range(3):
        rows = b["n20"][CLIPS * i : CLIPS * i + CLIPS]
        active, _ = gelu(nn(rows, weight("wu", i)[...]) + vec(b_up, i))
        out_left[CLIPS * i : CLIPS * i + CLIPS] = active
    out_left[3 * CLIPS : 6 * CLIPS] = b["n20"][...]
    out_right[...] = rows8_at(b["bg"], 6).astype(BF)
    tick(TICKS[13])
    total = small_end(2, ticket, "x")
    out_small[0:12] = total[0:12]
    out_small[12:16] = sva[12:16]
    out_small[16:28] = total[16:28]
    out_small[28:32] = svb[12:16]
    while running:
        tick(1)
    for drain in drains:
        drain()
    for copy in stores:
        copy.wait()


def shards(
    tokens,
    lengths,
    partner,
    mix_coef,
    norm_gain,
    norm_bias,
    w_qkv,
    b_qv,
    w_out,
    b_out,
    w_up,
    b_up,
    w_down,
    b_down,
    cot_tokens,
    cot_global,
):
    wq = jnp.transpose(w_qkv, (0, 2, 3, 1)).reshape(4, 3 * KD, D)
    plan = scratch_plan()
    names = list(plan)
    smem = pl.BlockSpec(memory_space=pltpu.SMEM)
    vmem = pl.BlockSpec(memory_space=pltpu.VMEM)
    hbm = pl.BlockSpec(memory_space=pl.ANY)
    unit = jax.ShapeDtypeStruct((4, 16, 48, D), BF)
    out_tok, out_glob, out_grad, small, left, right, qo, up, down = pl.pallas_call(
        functools.partial(kernel, names),
        out_shape=(
            jax.ShapeDtypeStruct((224, D), BF),
            jax.ShapeDtypeStruct((8, D), BF),
            jax.ShapeDtypeStruct((224, D), BF),
            jax.ShapeDtypeStruct((32, D), F32),
            jax.ShapeDtypeStruct((6 * CLIPS, D), BF),
            jax.ShapeDtypeStruct((6 * CLIPS, D), BF),
            unit,
            unit,
            unit,
        ),
        in_specs=[smem] * 3 + [vmem] * 9 + [hbm] * 4,
        out_specs=(vmem,) * 6 + (hbm,) * 3,
        scratch_shapes=list(plan.values()),
        compiler_params=pltpu.CompilerParams(
            collective_id=0, has_side_effects=True, vmem_limit_bytes=60 * 2**20
        ),
    )(
        partner,
        mix_coef,
        lengths,
        tokens.reshape(28, 8, D),
        cot_tokens[0],
        cot_global,
        norm_gain,
        norm_bias,
        b_out,
        b_down,
        b_up,
        b_qv,
        wq,
        w_out,
        w_up,
        w_down,
    )
    out_tok, out_glob, out_grad, gain, shift, qkv, qv, out, bout, ups, bup, downs, bdown = widen(
        out_tok,
        out_glob,
        out_grad,
        small,
        left,
        right,
        *(a.reshape(4, D, D) for a in (qo, up, down)),
    )
    return (
        out_tok,
        out_glob,
        out_grad,
        gain,
        shift,
        jnp.transpose(qkv.reshape(4, 3, KD, D), (0, 3, 1, 2)),
        qv,
        out,
        bout,
        ups,
        bup,
        downs,
        bdown,
    )


def widen_kernel(*refs):
    tok, glob, grad, small, left, right, qo, up, down = refs[:9]
    o_tok, o_glob, o_grad, o_gain, o_shift, o_qkv, o_qv, o_out, o_bout, o_up, o_bup, o_down, o_bdown = refs[9:22]
    held, wide, sem_in, sem_out = refs[22:]
    order = [(i, a) for i in (3, 0, 1, 2) for a in range(3)]
    fetches = []
    for n, (i, a) in enumerate(order):
        copy = pltpu.make_async_copy((qo, up, down)[a].at[i], held.at[n], sem_in.at[n])
        copy.start()
        fetches.append(copy)
    o_tok[0] = tok[...]
    o_grad[0] = grad[...]
    o_glob[0] = glob[0:3]
    m = lax.axis_index("mp")

    def share(row):
        value = small[row : row + 1]
        mine = value[:, 0:KD]
        for k in range(1, 4):
            mine = jnp.where(m == k, value[:, k * KD : (k + 1) * KD], mine)
        return mine

    for i in range(4):
        for j in range(2):
            o_gain[i, j : j + 1] = share(4 * i + 2 * j)
            o_shift[i, j : j + 1] = share(4 * i + 2 * j + 1)
        row = 16 + 4 * i
        o_bdown[i : i + 1] = share(row)
        o_bout[i : i + 1] = share(row + 1)
        o_bup[i : i + 1] = small[row + 2 : row + 3]
        o_qv[i, 0:1] = small[row + 3 : row + 4, 0:KD]
        o_qv[i, 1:2] = small[row + 3 : row + 4, 256 : 256 + KD]
    slots = wide.shape[0]
    busy = [[] for _ in range(slots)]
    for n, (i, a) in enumerate(order):
        slot = n % slots
        fetches[n].wait()
        for copy in busy[slot]:
            copy.wait()
        value = held[n].astype(F32)
        if a > 0 and i < 3:
            base = CLIPS * (3 * (a == 1) + i)
            value = value + tn(left[base : base + CLIPS], right[base : base + CLIPS])
        wide[slot] = value
        src = wide.at[slot]
        if a == 0:
            pairs = (
                (src.at[pl.ds(0, 3 * KD)], o_qkv.at[i]),
                (src.at[pl.ds(3 * KD, KD)], o_out.at[i]),
            )
        else:
            pairs = ((src, (o_up, o_down)[a - 1].at[i]),)
        busy[slot] = []
        for k, (part, dst) in enumerate(pairs):
            copy = pltpu.make_async_copy(part, dst, sem_out.at[slot, k])
            copy.start()
            busy[slot].append(copy)
    for copies in busy:
        for copy in copies:
            copy.wait()


def widen(tok, glob, grad, small, left, right, qo, up, down):
    shape = jax.ShapeDtypeStruct
    vmem = pl.BlockSpec(memory_space=pltpu.VMEM)
    hbm = pl.BlockSpec(memory_space=pl.ANY)
    return pl.pallas_call(
        widen_kernel,
        in_specs=[vmem] * 6 + [hbm] * 3,
        out_specs=[vmem, vmem, vmem, vmem, vmem, hbm, vmem, hbm, vmem, hbm, vmem, hbm, vmem],
        out_shape=[shape((1, 224, D), BF), shape((1, 3, D), BF), shape((1, 224, D), BF)]
        + [shape((4, 2, KD), F32), shape((4, 2, KD), F32), shape((4, 3 * KD, D), F32)]
        + [shape((4, 2, KD), F32), shape((4, KD, D), F32), shape((4, KD), F32)]
        + [shape((4, D, D), F32), shape((4, D), F32), shape((4, D, D), F32), shape((4, KD), F32)],
        scratch_shapes=[
            pltpu.VMEM((12, D, D), BF),
            pltpu.VMEM((5, D, D), F32),
            pltpu.SemaphoreType.DMA((12,)),
            pltpu.SemaphoreType.DMA((5, 2)),
        ],
        compiler_params=pltpu.CompilerParams(vmem_limit_bytes=60 * 2**20),
    )(tok, glob, grad, small, left, right, qo, up, down)


def solution(mesh):
    placed = (
        P("dp", None, None),
        P("dp", None),
        P(),
        P(),
        P(),
        P(),
        P(None, None, None, "mp"),
        P(None, None, "mp"),
        P(None, "mp", None),
        P(),
        P(None, None, "mp"),
        P(None, "mp"),
        P(None, "mp", None),
        P(),
        P("dp", None, None),
        P("dp", None, None),
    )
    return jax.shard_map(
        shards,
        mesh=mesh,
        in_specs=placed,
        out_specs=(
            P("dp", None, None),
            P("dp", None, None),
            P("dp", None, None),
            P(None, None, "mp"),
            P(None, None, "mp"),
            P(None, None, None, "mp"),
            P(None, None, "mp"),
            P(None, "mp", None),
            P(None, "mp"),
            P(None, None, "mp"),
            P(None, "mp"),
            P(None, "mp", None),
            P(None, "mp"),
        ),
        check_vma=False,
    )
```

```python
import functools

import jax
import jax.numpy as jnp
from jax import lax
from jax.experimental import pallas as pl
from jax.experimental.pallas import tpu as pltpu
from jax.sharding import PartitionSpec as P

HD = 64
D = 768
KD = 192
SPANS = (128, 64, 32, 96)
SLABS = (32, 16, 8, 24)
OFFS = (0, 128, 192)
CLIPS = 32
PIECES = 21
EPS = 1e-06
NEG = -1000000000.0
MESH = pl.DeviceIdType.MESH
BF = jnp.bfloat16
F32 = jnp.float32
UNITS = (
    ("down", 0, "yz"),
    ("up", 0, "zy"),
    ("down", 1, "zy"),
    ("up", 1, "yz"),
    ("down", 2, "zy"),
    ("up", 2, "yz"),
    ("qo", 0, "yz"),
    ("qo", 1, "zy"),
    ("qo", 2, "zy"),
)
UNIT_OF = {(name, view): place for place, (name, view, _) in enumerate(UNITS)}
TICKS = (0, 2, 1, 2, 2, 1, 6, 3, 2, 6, 6, 8, 8, 0)
OUT_OF = {"qo": 0, "up": 1, "down": 2}


def nn(a, b):
    return lax.dot_general(a, b, (((1,), (0,)), ((), ())), preferred_element_type=F32)


def nt(a, b):
    return lax.dot_general(a, b, (((1,), (1,)), ((), ())), preferred_element_type=F32)


def tn(a, b):
    return lax.dot_general(a, b, (((0,), (0,)), ((), ())), preferred_element_type=F32)


def gelu(inner):
    c0, c1 = 0.7978845608028654, 0.044715
    square = inner * inner
    th = jnp.tanh(c0 * inner * (1.0 + c1 * square))
    half = 0.5 * (1.0 + th)
    slope = half + 0.5 * inner * (1.0 - th * th) * c0 * (1.0 + 3.0 * c1 * square)
    return (inner * half).astype(BF), slope


def layer_stats(x):
    center = x - jnp.mean(x, -1, keepdims=True)
    spread = jnp.mean(center * center, -1, keepdims=True)
    inv = lax.rsqrt(spread + EPS)
    return center * inv, inv


def scratch_plan():
    plan = {}
    for i in range(4):
        span, slab = SPANS[i], SLABS[i]
        for name in ("n1", "s1", "n2", "s2", "zo", "s3", "da", "s4"):
            plan[name, i] = pltpu.VMEM((4, slab, D), BF)
        for name in ("r1", "r2", "r3", "r4"):
            plan[name, i] = pltpu.VMEM((3, slab, D), BF)
        for name in ("x", "af", "daf"):
            plan[name, i] = pltpu.VMEM((slab, D), F32)
        plan["dz", i] = pltpu.VMEM((4, slab, D), F32)
        for name in ("q", "k", "v", "ho"):
            plan[name, i] = pltpu.VMEM((span, KD), BF)
        plan["pr", i] = pltpu.VMEM((3 * span, span), F32)
        plan["dg", i] = pltpu.VMEM((span, D), F32)
        plan["ac", i] = pltpu.VMEM((span, D), BF)
        plan["wq", i] = pltpu.VMEM((3 * KD, D), BF)
        plan["wo", i] = pltpu.VMEM((KD, D), BF)
        plan["wu", i] = pltpu.VMEM((D, D), BF)
        plan["wd", i] = pltpu.VMEM((D, D), BF)
        if i < 3:
            plan["gt", i] = pltpu.VMEM((4, slab, D), BF)
            for name in ("ac4", "di4", "pj4"):
                plan[name, i] = pltpu.VMEM((4, span, KD), BF)
            for name in ("cz", "nr", "n2r", "dh"):
                plan[name, i] = pltpu.VMEM((span, D), BF)
    for turn in range(2):
        plan["pa", turn] = pltpu.VMEM((CLIPS, 8, 256), BF)
        plan["pb", turn] = pltpu.VMEM((CLIPS, 8, 256), BF)
        plan["pc", turn] = pltpu.VMEM((PIECES, 8, 256), BF)
    plan["ts"] = pltpu.VMEM((7, 8, D), BF)
    plan["mx"] = pltpu.VMEM((7, 8, D), F32)
    plan["cc"] = pltpu.VMEM((8, D), BF)
    plan["inv"] = pltpu.SMEM((CLIPS,), jnp.int32)
    plan["cl"] = pltpu.VMEM((8, D), BF)
    plan["cg"] = pltpu.VMEM((CLIPS, 8, D), BF)
    plan["ct"] = pltpu.VMEM((CLIPS, 8, D), BF)
    for name in ("bc", "dcb"):
        plan[name] = pltpu.VMEM((8, D), BF)
    for axis in "yz":
        plan["dc", axis] = pltpu.VMEM((4, 8, D), BF)
    plan["bg"] = pltpu.VMEM((4, 2, 4, 8, D), BF)
    plan["n20"] = pltpu.VMEM((3 * CLIPS, D), BF)
    plan["zc"] = pltpu.VMEM((4, 8, D), BF)
    plan["afc"] = pltpu.VMEM((4, 8, D), F32)
    plan["pc"] = pltpu.VMEM((4, 8, D), BF)
    plan["dac"] = pltpu.VMEM((8, D), F32)
    plan["gin"] = pltpu.VMEM((4, 24, D), F32)
    plan["gdx"] = pltpu.VMEM((4, 8, D), BF)
    plan["go"] = pltpu.VMEM((3, 16, 48, D), BF)
    for u, (name, view, _) in enumerate(UNITS):
        plan["fa", u] = pltpu.VMEM((4, SPANS[view], KD), BF)
        plan["fb", u] = pltpu.VMEM((4, SPANS[view], D), BF)
        if name == "qo":
            plan["fc", u] = pltpu.VMEM((4, SPANS[view], D), BF)
        plan["g", u] = pltpu.VMEM((4, 48, D), BF)
        plan["near", u] = pltpu.VMEM((3, 48, D), BF)
        plan["gx", u] = pltpu.VMEM((48, D), BF)
        plan["ga", u] = pltpu.VMEM((4, 48, D), BF)
    plan["sva"] = pltpu.VMEM((16, D), F32)
    plan["svb"] = pltpu.VMEM((16, D), F32)
    plan["svr"] = pltpu.VMEM((3, 16, D), F32)
    for step in range(3):
        plan["svs", step] = pltpu.VMEM((32, D), BF)
        plan["svt", step] = pltpu.VMEM((3, 32, D), BF)
    plan["ssem"] = pltpu.SemaphoreType.DMA((256,))
    plan["rsem"] = pltpu.SemaphoreType.DMA((256,))
    plan["lsem"] = pltpu.SemaphoreType.DMA((48,))
    return plan


def kernel(names, *refs):
    (
        partner,
        mix,
        lengths,
        tok,
        cot,
        cotg,
        gain,
        shift,
        b_out,
        b_down,
        b_up,
        b_qv,
        wq_all,
        wo_all,
        wu_all,
        wd_all,
        out_tok,
        out_glob,
        out_grad,
        out_small,
        out_left,
        out_right,
        out_qo,
        out_up,
        out_down,
    ) = refs[:25]
    b = dict(zip(names, refs[25:]))
    ssem, rsem, lsem = b["ssem"], b["rsem"], b["lsem"]
    outs = {"qo": out_qo, "up": out_up, "down": out_down}
    me = lax.axis_index("dp")
    m = lax.axis_index("mp")
    place = {"y": lax.div(me, 8), "x": lax.rem(lax.div(me, 4), 2), "z": lax.rem(me, 4)}

    def at(**moved):
        p = dict(place)
        p.update(moved)
        return ((p["y"] * 2 + p["x"]) * 4 + p["z"], m)

    count = {"s": 0, "l": 0}
    drains = []

    def new(kind):
        count[kind] += 1
        return count[kind] - 1

    def send(src, dst, s, dev):
        pltpu.make_async_remote_copy(
            src_ref=src,
            dst_ref=dst,
            send_sem=ssem.at[s],
            recv_sem=rsem.at[s],
            device_id=dev,
            device_id_type=MESH,
        ).start()

    def wait(like, sem):
        pltpu.make_async_copy(like, like, sem).wait()

    def landed(like, s):
        wait(like, rsem.at[s])
        drains.append(lambda: wait(like, ssem.at[s]))

    barrier = pltpu.get_barrier_semaphore()

    def greet(k, _):
        pl.semaphore_signal(
            barrier, inc=1, device_id=(lax.rem(me + k, CLIPS), m), device_id_type=MESH
        )
        return 0

    lax.fori_loop(1, CLIPS, greet, 0)
    for k in (1, 2, 3):
        pl.semaphore_signal(barrier, inc=1, device_id=(me, lax.rem(m + k, 4)), device_id_type=MESH)

    fetch = {}
    for i in range(4):
        for name, src in (("wq", wq_all), ("wo", wo_all), ("wu", wu_all), ("wd", wd_all)):
            copy = pltpu.make_async_copy(src.at[i], b[name, i], lsem.at[new("l")])
            copy.start()
            fetch[name, i] = copy

    def weight(name, i):
        if (name, i) in fetch:
            fetch.pop((name, i)).wait()
        return b[name, i]

    pl.semaphore_wait(barrier, CLIPS - 1 + 3)

    def gather_start(buf):
        s = new("s")
        for k in (2, 1, 3):
            send(buf.at[m], buf.at[m], s, (me, lax.rem(m + k, 4)))
        return buf.at[pl.ds(0, 3)], s

    def scatter_start(src, dst):
        s = new("s")
        for k in (2, 1, 3):
            t = lax.rem(m + k, 4)
            send(src.at[t], dst.at[k - 1], s, (me, t))
        return dst, s

    def dp_gather_start(src, dst):
        s = new("s")

        def step(k, _):
            send(src, dst.at[me], s, (lax.rem(me + k, CLIPS), m))
            return 0

        lax.fori_loop(1, CLIPS, step, 0)
        dst[me] = src[...]
        return dst.at[pl.ds(0, CLIPS - 1)], s

    factors = {}

    def share_rows(name, i, part, src_of):
        u = UNIT_OF[name, i]
        one = UNITS[u][2][0]
        p = place[one]
        dst = b[part, u]
        s = new("s")
        for k in (1, 3, 2):
            t = lax.rem(p + k, 4)
            send(src_of(t), dst.at[p], s, at(**{one: t}))
        dst[p] = src_of(p)[...]
        factors[part, u] = (dst.at[pl.ds(0, 3)], s)

    def rows_of(buf, i):
        span, slab = SPANS[i], SLABS[i]
        if slab % 16 == 0:
            return buf[...].reshape(span, D)
        return buf[...].astype(F32).reshape(span, D).astype(BF)

    groups = [m * 4 + r for r in range(4)] + [16 + m * 2 + r for r in range(2)] + [24 + m]

    def deal_start(turn, src_at):
        keep = b["pa", turn]
        s = new("s")
        for j in range(PIECES):

            @pl.when(me != j)
            def _():
                send(src_at(j // 3).at[:, pl.ds((j % 3) * 256, 256)], keep.at[me], s, (j, m))

            @pl.when(me == j)
            def _():
                keep[me] = src_at(j // 3)[:, (j % 3) * 256 : (j % 3) * 256 + 256]

        return s

    def few_or_all(buf, sem):
        @pl.when(me < PIECES)
        def _():
            wait(buf.at[pl.ds(0, PIECES - 1)], sem)

        @pl.when(me >= PIECES)
        def _():
            wait(buf, sem)

    def deal_turn(turn, s, index):
        keep, stage, got = b["pa", turn], b["pb", turn], b["pc", turn]
        t = new("s")

        @pl.when(me < PIECES)
        def _():
            wait(keep.at[pl.ds(0, CLIPS - 1)], rsem.at[s])
            for d in range(CLIPS):
                stage[d] = keep[index[d]]
            got[me] = stage[me]

            def step(k, _):
                d = lax.rem(me + k, CLIPS)
                send(stage.at[d], got.at[me], t, (d, m))
                return 0

            lax.fori_loop(1, CLIPS, step, 0)

        few_or_all(got, ssem.at[s])
        return t

    def deal_end(turn, t):
        stage, got = b["pb", turn], b["pc", turn]
        few_or_all(got, rsem.at[t])

        @pl.when(me < PIECES)
        def _():
            wait(stage.at[pl.ds(0, CLIPS - 1)], ssem.at[t])

        return [
            jnp.concatenate([got[3 * r + c].astype(F32) for c in range(3)], 1) for r in range(7)
        ]

    lam = mix[me]
    b["cc"][...] = jnp.zeros((8, D), BF)
    b["cc"][0:3] = cotg[0]
    s = deal_start(0, lambda r: tok.at[groups[r]])
    cot_ticket = dp_gather_start(b["cc"], b["ct"])
    t = deal_turn(0, s, partner)
    for i in range(3):
        row = lax.broadcasted_iota(jnp.int32, (SPANS[i], 1), 0)
        dz = jnp.where(row == 0, 0.0, cot[OFFS[i] : OFFS[i] + SPANS[i]].astype(F32))
        b["cz", i][...] = dz.astype(BF)
        b["dz", i][...] = dz.reshape(4, SLABS[i], D)
        share_rows("down", i, "fb", lambda t: b["cz", i])
    taken = deal_end(0, t)
    for r in range(7):
        value = lam * tok[groups[r]].astype(F32) + (1.0 - lam) * taken[r]
        if r < 4:
            b["x", 0][8 * r : 8 * r + 8] = value
        elif r < 6:
            b["x", 1][8 * (r - 4) : 8 * (r - 4) + 8] = value
        else:
            b["x", 2][...] = value

    def vec(ref, row):
        if len(ref.shape) == 3:
            return ref[row // 2, row % 2 : row % 2 + 1, :]
        return ref[row : row + 1, :]

    def norm(x, i, j):
        hat, _ = layer_stats(x)
        return hat * vec(gain, 2 * i + j) + vec(shift, 2 * i + j)

    def head_mask(h):
        lane = lax.broadcasted_iota(jnp.int32, (1, KD), 1)
        return (lane >= h * HD) & (lane < h * HD + HD)

    masks = [head_mask(h) for h in range(3)]
    zero = jnp.zeros((), BF)

    def stacked(a):
        return jnp.concatenate(
            [jnp.where(masks[h], a.astype(F32), 0.0) for h in range(3)], 0
        ).astype(BF)

    def folded(a, span):
        total = None
        for h in range(3):
            part = jnp.where(masks[h], a[h * span : (h + 1) * span], 0.0)
            total = part if total is None else total + part
        return total

    scale = HD ** (-0.5)

    def attend(i):
        span = SPANS[i]
        normed = rows_of(b["n1", i], i)
        wq = weight("wq", i)
        query = (nt(normed, wq[0:KD]) + vec(b_qv, 2 * i)).astype(BF)
        keys = nt(normed, wq[KD : 2 * KD]).astype(BF)
        values = (nt(normed, wq[2 * KD : 3 * KD]) + vec(b_qv, 2 * i + 1)).astype(BF)
        b["q", i][...] = query
        b["k", i][...] = keys
        b["v", i][...] = values
        scores = nt(stacked(query), keys) * scale
        if i < 3:
            col = lax.broadcasted_iota(jnp.int32, (1, span), 1)
            scores = jnp.where(col < lengths[0, i], scores, NEG)
        expo = jnp.exp(scores - jnp.max(scores, -1, keepdims=True))
        probs = expo / jnp.sum(expo, -1, keepdims=True)
        b["pr", i][...] = probs
        heads_out = folded(nn(probs.astype(BF), values), span).astype(BF)
        b["ho", i][...] = heads_out
        part = nn(heads_out, weight("wo", i)[...])
        b["s1", i][...] = part.astype(BF).reshape(4, SLABS[i], D) if SLABS[i] % 16 == 0 else (
            part.reshape(4, SLABS[i], D).astype(BF)
        )
        ticket = scatter_start(b["s1", i], b["r1", i])
        if i < 3:
            b["nr", i][...] = normed
            share_rows("qo", i, "fb", lambda t: b["nr", i])
        return ticket

    def put_slabs(name, i, value):
        b[name, i][...] = value.reshape(4, SLABS[i], D).astype(BF)

    def summed(send_name, recv_name, i, ticket):
        landed(*ticket)
        got = b[recv_name, i]
        total = b[send_name, i][m].astype(F32)
        for k in range(3):
            total = total + got[k].astype(F32)
        return total

    def middle(i, ticket):
        after = b["x", i][...] + summed("s1", "r1", i, ticket) + vec(b_out, i)
        b["af", i][...] = after
        b["n2", i][m] = norm(after, i, 1).astype(BF)
        return gather_start(b["n2", i])

    def feed(i, ticket):
        landed(*ticket)
        normed2 = rows_of(b["n2", i], i)
        if i < 3:
            b["n2r", i][...] = normed2
            share_rows("up", i, "fb", lambda t: b["n2r", i])
        inner = nn(normed2, weight("wu", i)[...]) + vec(b_up, i)
        active, b["dg", i][...] = gelu(inner)
        b["ac", i][...] = active
        part = nn(active, weight("wd", i)[...])
        put_slabs("s2", i, part)
        if i == 3:
            return scatter_start(b["s2", i], b["r2", i])
        for t in range(4):
            cols = slice(t * KD, t * KD + KD)
            b["ac4", i][t] = active[:, cols]
        return part[0:8][0:1]

    def feed_send(i):
        share_rows("down", i, "fa", lambda t: b["ac4", i].at[t])
        start_unit("down", i)
        return scatter_start(b["s2", i], b["r2", i])

    def finish(i, ticket):
        total = b["af", i][...] + summed("s2", "r2", i, ticket) + vec(b_down, i)
        b["zo", i][m] = total.astype(BF)
        return gather_start(b["zo", i])

    row8 = lax.broadcasted_iota(jnp.int32, (8, 1), 0)

    def rows8_at(buf, kinds):
        r_at = lax.broadcasted_iota(jnp.int32, (32 * kinds, 256), 0)
        k_at = lax.broadcasted_iota(jnp.int32, (32 * kinds, 256), 1)
        pick = (k_at == lax.rem(r_at, 32) * 8 + lax.div(r_at, 32)).astype(F32).astype(BF)
        return nn(pick, buf[...].astype(F32).reshape(256, D).astype(BF))

    def put_unit(name, row, value):
        value = value.astype(BF)
        chunks = value.shape[0] // 48
        lo = row // 48
        b["go"][OUT_OF[name], lo : lo + chunks] = value.reshape(chunks, 48, D)

    def back_feed(i):
        span = SPANS[i]
        dz = b["dz", i][...].reshape(span, D)
        dm = dz.astype(BF)
        dact = nt(dm, weight("wd", i)[...])
        dinner = (b["dg", i][...] * dact).astype(BF)
        put_slabs("s3", i, nt(dinner, weight("wu", i)[...]))
        if i < 3:
            for t in range(4):
                b["di4", i][t] = dinner[:, t * KD : t * KD + KD]
        else:
            ticket = scatter_start(b["s3", i], b["r3", i])
            for part in range(2):
                cols = slice(part * 384, part * 384 + 384)
                put_unit("down", part * 384, tn(b["ac", i][:, cols], dm))
            store_global("down")
            normed2 = rows_of(b["n2", i], i)
            for part in range(2):
                cols = slice(part * 384, part * 384 + 384)
                put_unit("up", part * 384, tn(dinner[:, cols], normed2))
            store_global("up")
        b["svb"][4 * i : 4 * i + 1] = jnp.sum(dz, 0, keepdims=True)
        b["svb"][4 * i + 2 : 4 * i + 3] = jnp.sum(dinner.astype(F32), 0, keepdims=True)
        return ticket if i == 3 else None

    def back_feed_send(i):
        share_rows("up", i, "fa", lambda t: b["di4", i].at[t])
        start_unit("up", i)
        return scatter_start(b["s3", i], b["r3", i])

    def norm_back(x, dy, i, j):
        hat, inv = layer_stats(x)
        b["sva"][4 * i + 2 * j : 4 * i + 2 * j + 1] = jnp.sum(dy * hat, 0, keepdims=True)
        b["sva"][4 * i + 2 * j + 1 : 4 * i + 2 * j + 2] = jnp.sum(dy, 0, keepdims=True)
        g = dy * vec(gain, 2 * i + j)
        return inv * (
            g - jnp.mean(g, -1, keepdims=True) - hat * jnp.mean(g * hat, -1, keepdims=True)
        )

    def back_middle(i, ticket):
        dn2 = summed("s3", "r3", i, ticket)
        dafter = b["dz", i][m] + norm_back(b["af", i][...], dn2, i, 1)
        b["daf", i][...] = dafter
        b["da", i][m] = dafter.astype(BF)
        return gather_start(b["da", i])

    def with_class_row(rows, first):
        row = lax.broadcasted_iota(jnp.int32, (rows.shape[0], 1), 0)
        return jnp.where(row == 0, first, rows.astype(F32)).astype(BF)

    def rows_send(i, ticket):
        landed(*ticket)
        b["dh", i][...] = rows_of(b["da", i], i)
        u = UNIT_OF["qo", i]
        one = UNITS[u][2][0]
        s = new("s")

        @pl.when(place[one] != 3)
        def _():
            half = pl.ds(lax.rem(m, 2) * (SPANS[i] // 2), SPANS[i] // 2)
            send(b["dh", i].at[half], b["fc", u].at[place[one], half], s, at(**{one: 3}))

        @pl.when(place[one] == 3)
        def _():
            b["fc", u][3] = b["dh", i][...]

        factors["fc", u] = s

    def rows_forward(i):
        u = UNIT_OF["qo", i]
        one, fc, n = UNITS[u][2][0], b["fc", u], SPANS[i] // 2
        s0, s = factors["fc", u], new("s")
        core = lax.rem(m, 2)

        @pl.when(place[one] == 3)
        def _():
            wait(fc.at[pl.ds(0, 3), pl.ds(0, n)], rsem.at[s0])
            part = fc.at[pl.ds(0, 3), pl.ds(core * n, n)]
            send(part, part, s, (me, m + 1 - 2 * core))

        factors["fc", u] = (s0, s)

    def class_rows_send():
        b["dcb"][...] = b["dac"][...].astype(BF)
        for axis in "yz":
            dst, p = b["dc", axis], place[axis]
            s = new("s")
            for k in (1, 3, 2):
                t = lax.rem(p + k, 4)
                send(b["dcb"], dst.at[p], s, at(**{axis: t}))
            dst[p] = b["dcb"][...]
            factors["dc", axis] = (dst.at[pl.ds(0, 3)], s)

    def back_attend(i, ticket):
        span = SPANS[i]
        if i < 3:
            da = with_class_row(b["dh", i][...], b["dac"][i : i + 1])
        else:
            landed(*ticket)
            da = rows_of(b["da", i], i)
        b["svb"][4 * i + 1 : 4 * i + 2] = jnp.sum(da.astype(F32), 0, keepdims=True)
        dheads = nt(da, weight("wo", i)[...]).astype(BF)
        query, keys, values = b["q", i][...], b["k", i][...], b["v", i][...]
        probs = b["pr", i][...]
        d3 = stacked(dheads)
        dprob = nt(d3, values)
        dscore = probs * (dprob - jnp.sum(dprob * probs, -1, keepdims=True))
        dscore = dscore.astype(BF)
        dquery = (folded(nn(dscore, keys), span) * scale).astype(BF)
        dkeys = (tn(dscore, stacked(query)) * scale).astype(BF)
        dvalues = tn(probs.astype(BF), d3).astype(BF)
        wq = weight("wq", i)
        part = nn(dquery, wq[0:KD]) + nn(dkeys, wq[KD : 2 * KD]) + nn(dvalues, wq[2 * KD : 3 * KD])
        put_slabs("s4", i, part)
        ticket = scatter_start(b["s4", i], b["r4", i])
        b["svb"][4 * i + 3 : 4 * i + 4, 0:KD] = jnp.sum(dquery.astype(F32), 0, keepdims=True)
        b["svb"][4 * i + 3 : 4 * i + 4, 256 : 256 + KD] = jnp.sum(
            dvalues.astype(F32), 0, keepdims=True
        )
        if i < 3:
            b["pj4", i][0] = dquery
            b["pj4", i][1] = dkeys
            b["pj4", i][2] = dvalues
            b["pj4", i][3] = b["ho", i][...]
            share_rows("qo", i, "fa", lambda t: b["pj4", i].at[t])
            start_unit("qo", i)
            return ticket
        normed = rows_of(b["n1", i], i)
        put_unit("qo", 0, tn(dquery, normed))
        put_unit("qo", KD, tn(dkeys, normed))
        put_unit("qo", 2 * KD, tn(dvalues, normed))
        put_unit("qo", 3 * KD, tn(b["ho", i][...], da))
        store_global("qo")
        return ticket

    def back_finish(i, ticket):
        dn1 = summed("s4", "r4", i, ticket)
        dafter = b["daf", i][...]
        if i < 3:
            row = lax.broadcasted_iota(jnp.int32, (SLABS[i], 1), 0)
            dafter = jnp.where((row == 0) & (m == 0), b["dac"][i : i + 1], dafter)
        return dafter + norm_back(b["x", i][...], dn1, i, 0)

    def class_feed(dgin):
        dz = jnp.zeros((8, D), F32)
        slope = jnp.zeros((8, D), F32)
        for i in range(3):
            first = cot[OFFS[i] : OFFS[i] + 16].astype(F32)[0:1]
            dz = jnp.where(row8 == i, first + dgin[i : i + 1], dz)
            slope = jnp.where(row8 == i, b["dg", i][0:8][0:1], slope)
        dm = dz.astype(BF)
        dact = jnp.zeros((8, D), F32)
        for i in range(3):
            dact = jnp.where(row8 == i, nt(dm, weight("wd", i)[...]), dact)
        dinner = (slope * dact).astype(BF)
        dn2 = jnp.zeros((8, D), F32)
        for i in range(3):
            dn2 = jnp.where(row8 == i, nt(dinner, weight("wu", i)[...]), dn2)
        b["pc"][m] = dn2.astype(BF)
        ticket = gather_start(b["pc"])
        both = dm.astype(F32)
        dinner = dinner.astype(F32)
        for i in range(3):
            both = jnp.where(row8 == 3 + i, dinner[i : i + 1], both)
            b["svb"][4 * i : 4 * i + 1] += dz[i : i + 1]
            b["svb"][4 * i + 2 : 4 * i + 3] += dinner[i : i + 1]
        b["bc"][...] = both.astype(BF)
        b["dac"][...] = dz
        return ticket

    def right_over_z():
        py, px, pz = place["y"], place["x"], place["z"]
        s = new("s")
        for k in (1, 3, 2):
            send(b["bc"], b["bg"].at[py, px, pz], s, at(z=lax.rem(pz + k, 4)))
        b["bg"][py, px, pz] = b["bc"][...]
        return b["bg"].at[0, 0, pl.ds(0, 3)], s

    def right_over_y(ticket):
        landed(*ticket)
        own = b["bg"].at[place["y"], place["x"]]
        s = new("s")
        for k in (1, 3, 2):
            send(own, own, s, at(y=lax.rem(place["y"] + k, 4)))
        return b["bg"].at[pl.ds(0, 3), 0], s

    def right_over_x(ticket):
        landed(*ticket)
        own = b["bg"].at[:, place["x"]]
        s = new("s")
        send(own, own, s, at(x=1 - place["x"]))
        return own, s

    def class_middle(ticket):
        landed(*ticket)
        dn2 = b["pc"][0].astype(F32)
        for k in range(1, 4):
            dn2 = dn2 + b["pc"][k].astype(F32)
        hat, inv = layer_stats(b["afc"][0])
        lead = jnp.where(m == 0, 1.0, 0.0)
        scales = jnp.zeros((8, D), F32)
        for i in range(3):
            scales = jnp.where(row8 == i, vec(gain, 2 * i + 1), scales)
            b["sva"][4 * i + 2 : 4 * i + 3] += lead * (dn2 * hat)[i : i + 1]
            b["sva"][4 * i + 3 : 4 * i + 4] += lead * dn2[i : i + 1]
        g = dn2 * scales
        b["dac"][...] += inv * (
            g - jnp.mean(g, -1, keepdims=True) - hat * jnp.mean(g * hat, -1, keepdims=True)
        )

    def halves(ref):
        n = ref.shape[0] // 2
        return ref.at[pl.ds(0, n)], ref.at[pl.ds(n, n)]

    def ring_spread(axis, slot, own, like):
        p = place[axis]
        up, down = lax.rem(p + 1, 4), lax.rem(p + 3, 4)
        to_up, to_down = at(**{axis: up}), at(**{axis: down})
        s0, s1, s2, s3 = new("s"), new("s"), new("s"), new("s")
        send(own, slot(p), s0, to_up)
        send(own, slot(p), s1, to_down)
        yield
        landed(like, s0)
        part = halves(slot(down))[0]
        send(part, part, s2, to_up)
        landed(like, s1)
        part = halves(slot(up))[1]
        send(part, part, s3, to_down)
        yield
        landed(halves(like)[0], s2)
        landed(halves(like)[1], s3)

    def sum_unit(u):
        name, view, (one, two) = UNITS[u]
        span = SPANS[view]
        g, near, gx, ga = b["g", u], b["near", u], b["gx", u], b["ga", u]
        p1, p2 = place[one], place[two]
        out = outs[name].at[view]
        yield
        landed(*factors["fa", u])
        landed(*factors["fb", u])

        def multiply(rows):
            left = b["fa", u][...].reshape(4 * span, KD)
            g[...] = tn(left, rows).astype(BF).reshape(4, 48, D)

        if name == "qo":
            s_da, s_core = factors["fc", u]
            n = span // 2
            fc = b["fc", u]
            if ("dc", one) in factors:
                landed(*factors.pop(("dc", one)))

            @pl.when(p1 == 3)
            def _():
                wait(fc.at[pl.ds(0, 3), pl.ds(0, n)], rsem.at[s_core])
                first = b["dc", one][...].astype(F32)
                multiply(
                    jnp.concatenate(
                        [with_class_row(fc[k], first[k, view : view + 1]) for k in range(4)], 0
                    )
                )

            @pl.when(p1 != 3)
            def _():
                multiply(b["fb", u][...].reshape(4 * span, D))

            def drain():
                @pl.when(p1 != 3)
                def _():
                    wait(fc.at[0, pl.ds(0, n)], ssem.at[s_da])

                @pl.when(p1 == 3)
                def _():
                    wait(fc.at[pl.ds(0, 3), pl.ds(0, n)], ssem.at[s_core])

            drains.append(drain)
        else:
            multiply(b["fb", u][...].reshape(4 * span, D))
        s = new("s")
        for k in (1, 3, 2):
            t = lax.rem(p2 + k, 4)
            send(g.at[t], near.at[k - 1], s, at(**{two: t}))
        yield
        landed(near, s)
        total = g[p2].astype(F32)
        for k in range(3):
            total = total + near[k].astype(F32)
        ga[p2] = total.astype(BF)
        s = new("s")
        send(ga.at[p2], gx, s, at(x=1 - place["x"]))
        yield
        landed(gx, s)
        wait(gx, ssem.at[s])
        drains.pop()
        ga[p2] = (ga[p2].astype(F32) + gx[...].astype(F32)).astype(BF)
        s = new("s")
        for k in (1, 3, 2):
            send(ga.at[p2], ga.at[p2], s, at(**{two: lax.rem(p2 + k, 4)}))
        yield
        landed(ga.at[pl.ds(0, 3)], s)
        own = out.at[pl.ds(p1 * 4, 4)]
        store(ga, own)
        yield from ring_spread(one, lambda t: out.at[pl.ds(t * 4, 4)], ga, out.at[pl.ds(0, 4)])

    stores = []

    def store(src, dst):
        copy = pltpu.make_async_copy(src, dst, lsem.at[new("l")])
        copy.start()
        stores.append(copy)

    running = []

    def store_global(name):
        store(b["go"].at[OUT_OF[name]], outs[name].at[3])

    def start_unit(name, i):
        unit = sum_unit(UNIT_OF[name, i])
        next(unit)
        running.append(unit)

    def tick(n):
        for _ in range(min(n, len(running))):
            unit = running.pop(0)
            if next(unit, "end") != "end":
                running.append(unit)

    tickets = [None] * 3
    back = [None] * 3
    for i in range(3):
        b["n1", i][m] = norm(b["x", i][...], i, 0).astype(BF)
        tickets[i] = gather_start(b["n1", i])
    for i in range(3):
        landed(*tickets[i])
        tickets[i] = attend(i)
    for i in range(3):
        tickets[i] = middle(i, tickets[i])
    firsts = jnp.zeros((8, D), F32)
    for i in range(3):
        firsts = jnp.where(row8 == i, b["af", i][0:8][0:1], firsts)
    b["afc"][m] = firsts
    after_ticket = gather_start(b["afc"])
    parts = jnp.zeros((8, D), F32)
    for i in range(3):
        parts = jnp.where(row8 == i, feed(i, tickets[i]), parts)
    b["zc"][m] = parts.astype(BF)
    ticket = gather_start(b["zc"])
    back_feed(0)
    landed(*after_ticket)
    classes = b["afc"][0]
    for i in range(3):
        classes = jnp.where(row8 == i, classes + vec(b_down, i), classes)
    landed(*ticket)
    for k in range(4):
        classes = classes + b["zc"][k].astype(F32)
    for i in range(3):
        classes = jnp.where(row8 == 3 + i, b["n2", i][0].astype(F32)[0:1], classes)
    b["cl"][...] = classes.astype(BF)
    class_ticket = dp_gather_start(b["cl"], b["cg"])
    for i in range(3):
        tickets[i] = feed_send(i)
    back[0] = back_feed_send(0)
    for i in (1, 2):
        back_feed(i)
        back[i] = back_feed_send(i)
    tick(TICKS[0])

    landed(*class_ticket)
    gathered = rows8_at(b["cg"], 6)
    gin = gathered[0:96]
    b["n20"][...] = gathered[96:192].astype(BF)
    b["gin"][...] = gin.reshape(4, 24, D)
    b["x", 3][...] = b["gin"][m]
    put_slabs("n1", 3, norm(gin, 3, 0))
    ticket = attend(3)
    landed(*cot_ticket)
    b["dz", 3][...] = rows8_at(b["ct"], 3).reshape(4, 24, D)
    tick(TICKS[1])
    ticket = middle(3, ticket)
    for i in range(3):
        tickets[i] = finish(i, tickets[i])
    tick(TICKS[2])
    glob_ticket = feed(3, ticket)
    ticket = back_feed(3)
    back[0] = back_middle(0, back[0])
    tick(TICKS[3])
    ticket = back_middle(3, ticket)
    for i in (1, 2):
        back[i] = back_middle(i, back[i])
    tick(TICKS[4])
    ticket = back_attend(3, ticket)
    for i in range(3):
        rows_send(i, back[i])
    tick(TICKS[5])
    dx = back_finish(3, ticket)
    o_at = lax.broadcasted_iota(jnp.int32, (8, 24), 0)
    w_at = lax.broadcasted_iota(jnp.int32, (8, 24), 1) + m * 24
    chosen = ((w_at == o_at * 32 + me) & (o_at < 3)).astype(F32).astype(BF)
    b["gdx"][m] = nn(chosen, dx.astype(BF)).astype(BF)
    ticket = gather_start(b["gdx"])
    glob_ticket = finish(3, glob_ticket)
    o_at = lax.broadcasted_iota(jnp.int32, (8, 96), 0)
    w_at = lax.broadcasted_iota(jnp.int32, (8, 96), 1)
    mine = ((w_at == o_at * 32 + me) & (o_at < 3)).astype(F32).astype(BF)
    tick(TICKS[6])
    landed(*ticket)
    dgin = b["gdx"][0].astype(F32)
    for k in range(1, 4):
        dgin = dgin + b["gdx"][k].astype(F32)

    ticket = class_feed(dgin)
    right_ticket = right_over_z()
    for i in range(3):
        rows_forward(i)
    for i in range(3):
        landed(*tickets[i])
        out_tok[OFFS[i] : OFFS[i] + SPANS[i]] = rows_of(b["zo", i], i)
    landed(*glob_ticket)
    out_glob[...] = nn(mine, rows_of(b["zo", 3], 3)).astype(BF)
    tick(TICKS[7])
    class_middle(ticket)
    class_rows_send()
    for i in range(3):
        tickets[i] = back_attend(i, None)
    right_ticket = right_over_y(right_ticket)
    tick(TICKS[8])
    for i in range(3):
        dx = back_finish(i, tickets[i])
        base = (0, 4, 6)[i]
        for r in range(SLABS[i] // 8):
            rows = dx[8 * r : 8 * r + 8]
            b["mx"][base + r] = lam * rows
            b["ts"][base + r] = ((1.0 - lam) * rows).astype(BF)
    right_ticket = right_over_x(right_ticket)
    def invert(d, _):
        found = jnp.int32(0)
        for c in range(CLIPS):
            found = jnp.where(partner[c] == d, c, found)
        b["inv"][d] = found
        return 0

    lax.fori_loop(0, CLIPS, invert, 0)
    s = deal_start(1, lambda r: b["ts"].at[r])

    s_mp = new("s")
    for k in (2, 1, 3):
        send(b["sva"], b["svr"].at[k - 1], s_mp, (me, lax.rem(m + k, 4)))
    tick(TICKS[9])
    t = deal_turn(1, s, b["inv"])
    tick(TICKS[10])
    landed(b["svr"], s_mp)
    sva = b["sva"][...] + b["svr"][0] + b["svr"][1] + b["svr"][2]
    svb = b["svb"][...]
    b["svs", 0][...] = jnp.concatenate([sva, svb], 0).astype(BF)

    def small_start(step, axis):
        s = new("s")
        far = (1, 3, 2) if axis != "x" else (1,)
        size = 4 if axis != "x" else 2
        for k in far:
            dev = at(**{axis: lax.rem(place[axis] + k, size)})
            send(b["svs", step], b["svt", step].at[k - 1], s, dev)
        return b["svt", step].at[pl.ds(0, len(far))], s

    def small_end(step, ticket, axis):
        landed(*ticket)
        total = b["svs", step][...].astype(F32)
        for k in range(3 if axis != "x" else 1):
            total = total + b["svt", step][k].astype(F32)
        return total

    ticket = small_start(0, "y")
    taken = deal_end(1, t)
    for i in range(3):
        base = (0, 4, 6)[i]
        for r in range(SLABS[i] // 8):
            rows = b["mx"][base + r] + taken[base + r]
            b["gt", i][m, 8 * r : 8 * r + 8] = rows.astype(BF)
        tickets[i] = gather_start(b["gt", i])
    tick(TICKS[11])
    b["svs", 1][...] = small_end(0, ticket, "y").astype(BF)
    ticket = small_start(1, "z")
    tick(TICKS[12])
    for i in range(3):
        landed(*tickets[i])
        out_grad[OFFS[i] : OFFS[i] + SPANS[i]] = rows_of(b["gt", i], i)
    b["svs", 2][...] = small_end(1, ticket, "z").astype(BF)
    ticket = small_start(2, "x")
    landed(*right_ticket)
    for i in range(3):
        rows = b["n20"][CLIPS * i : CLIPS * i + CLIPS]
        active, _ = gelu(nn(rows, weight("wu", i)[...]) + vec(b_up, i))
        out_left[CLIPS * i : CLIPS * i + CLIPS] = active
    out_left[3 * CLIPS : 6 * CLIPS] = b["n20"][...]
    out_right[...] = rows8_at(b["bg"], 6).astype(BF)
    tick(TICKS[13])
    total = small_end(2, ticket, "x")
    out_small[0:12] = total[0:12]
    out_small[12:16] = sva[12:16]
    out_small[16:28] = total[16:28]
    out_small[28:32] = svb[12:16]
    while running:
        tick(1)
    for drain in drains:
        drain()
    for copy in stores:
        copy.wait()


def shards(
    tokens,
    lengths,
    partner,
    mix_coef,
    norm_gain,
    norm_bias,
    w_qkv,
    b_qv,
    w_out,
    b_out,
    w_up,
    b_up,
    w_down,
    b_down,
    cot_tokens,
    cot_global,
):
    wq = jnp.transpose(w_qkv, (0, 2, 3, 1)).reshape(4, 3 * KD, D)
    plan = scratch_plan()
    names = list(plan)
    smem = pl.BlockSpec(memory_space=pltpu.SMEM)
    vmem = pl.BlockSpec(memory_space=pltpu.VMEM)
    hbm = pl.BlockSpec(memory_space=pl.ANY)
    unit = jax.ShapeDtypeStruct((4, 16, 48, D), BF)
    out_tok, out_glob, out_grad, small, left, right, qo, up, down = pl.pallas_call(
        functools.partial(kernel, names),
        out_shape=(
            jax.ShapeDtypeStruct((224, D), BF),
            jax.ShapeDtypeStruct((8, D), BF),
            jax.ShapeDtypeStruct((224, D), BF),
            jax.ShapeDtypeStruct((32, D), F32),
            jax.ShapeDtypeStruct((6 * CLIPS, D), BF),
            jax.ShapeDtypeStruct((6 * CLIPS, D), BF),
            unit,
            unit,
            unit,
        ),
        in_specs=[smem] * 3 + [vmem] * 9 + [hbm] * 4,
        out_specs=(vmem,) * 6 + (hbm,) * 3,
        scratch_shapes=list(plan.values()),
        compiler_params=pltpu.CompilerParams(
            collective_id=0, has_side_effects=True, vmem_limit_bytes=60 * 2**20
        ),
    )(
        partner,
        mix_coef,
        lengths,
        tokens.reshape(28, 8, D),
        cot_tokens[0],
        cot_global,
        norm_gain,
        norm_bias,
        b_out,
        b_down,
        b_up,
        b_qv,
        wq,
        w_out,
        w_up,
        w_down,
    )
    out_tok, out_glob, out_grad, gain, shift, qkv, qv, out, bout, ups, bup, downs, bdown = widen(
        out_tok,
        out_glob,
        out_grad,
        small,
        left,
        right,
        *(a.reshape(4, D, D) for a in (qo, up, down)),
    )
    return (
        out_tok,
        out_glob,
        out_grad,
        gain,
        shift,
        jnp.transpose(qkv.reshape(4, 3, KD, D), (0, 3, 1, 2)),
        qv,
        out,
        bout,
        ups,
        bup,
        downs,
        bdown,
    )


def widen_kernel(*refs):
    tok, glob, grad, small, left, right, qo, up, down = refs[:9]
    o_tok, o_glob, o_grad, o_gain, o_shift, o_qkv, o_qv, o_out, o_bout, o_up, o_bup, o_down, o_bdown = refs[9:22]
    held, wide, sem_in, sem_out = refs[22:]
    order = [(i, a) for i in (3, 0, 1, 2) for a in range(3)]
    fetches = []
    for n, (i, a) in enumerate(order):
        copy = pltpu.make_async_copy((qo, up, down)[a].at[i], held.at[n], sem_in.at[n])
        copy.start()
        fetches.append(copy)
    o_tok[0] = tok[...]
    o_grad[0] = grad[...]
    o_glob[0] = glob[0:3]
    m = lax.axis_index("mp")

    def share(row):
        value = small[row : row + 1]
        mine = value[:, 0:KD]
        for k in range(1, 4):
            mine = jnp.where(m == k, value[:, k * KD : (k + 1) * KD], mine)
        return mine

    for i in range(4):
        for j in range(2):
            o_gain[i, j : j + 1] = share(4 * i + 2 * j)
            o_shift[i, j : j + 1] = share(4 * i + 2 * j + 1)
        row = 16 + 4 * i
        o_bdown[i : i + 1] = share(row)
        o_bout[i : i + 1] = share(row + 1)
        o_bup[i : i + 1] = small[row + 2 : row + 3]
        o_qv[i, 0:1] = small[row + 3 : row + 4, 0:KD]
        o_qv[i, 1:2] = small[row + 3 : row + 4, 256 : 256 + KD]
    slots = wide.shape[0]
    busy = [[] for _ in range(slots)]
    for n, (i, a) in enumerate(order):
        slot = n % slots
        fetches[n].wait()
        for copy in busy[slot]:
            copy.wait()
        value = held[n].astype(F32)
        if a > 0 and i < 3:
            base = CLIPS * (3 * (a == 1) + i)
            rows, cols = (right, left) if a == 1 else (left, right)
            value = value + tn(rows[base : base + CLIPS], cols[base : base + CLIPS])
        wide[slot] = value.T if a == 1 else value
        src = wide.at[slot]
        if a == 0:
            pairs = (
                (src.at[pl.ds(0, 3 * KD)], o_qkv.at[i]),
                (src.at[pl.ds(3 * KD, KD)], o_out.at[i]),
            )
        else:
            pairs = ((src, (o_up, o_down)[a - 1].at[i]),)
        busy[slot] = []
        for k, (part, dst) in enumerate(pairs):
            copy = pltpu.make_async_copy(part, dst, sem_out.at[slot, k])
            copy.start()
            busy[slot].append(copy)
    for copies in busy:
        for copy in copies:
            copy.wait()


def widen(tok, glob, grad, small, left, right, qo, up, down):
    shape = jax.ShapeDtypeStruct
    vmem = pl.BlockSpec(memory_space=pltpu.VMEM)
    hbm = pl.BlockSpec(memory_space=pl.ANY)
    return pl.pallas_call(
        widen_kernel,
        in_specs=[vmem] * 6 + [hbm] * 3,
        out_specs=[vmem, vmem, vmem, vmem, vmem, hbm, vmem, hbm, vmem, hbm, vmem, hbm, vmem],
        out_shape=[shape((1, 224, D), BF), shape((1, 3, D), BF), shape((1, 224, D), BF)]
        + [shape((4, 2, KD), F32), shape((4, 2, KD), F32), shape((4, 3 * KD, D), F32)]
        + [shape((4, 2, KD), F32), shape((4, KD, D), F32), shape((4, KD), F32)]
        + [shape((4, D, D), F32), shape((4, D), F32), shape((4, D, D), F32), shape((4, KD), F32)],
        scratch_shapes=[
            pltpu.VMEM((12, D, D), BF),
            pltpu.VMEM((5, D, D), F32),
            pltpu.SemaphoreType.DMA((12,)),
            pltpu.SemaphoreType.DMA((5, 2)),
        ],
        compiler_params=pltpu.CompilerParams(vmem_limit_bytes=60 * 2**20),
    )(tok, glob, grad, small, left, right, qo, up, down)


def solution(mesh):
    placed = (
        P("dp", None, None),
        P("dp", None),
        P(),
        P(),
        P(),
        P(),
        P(None, None, None, "mp"),
        P(None, None, "mp"),
        P(None, "mp", None),
        P(),
        P(None, None, "mp"),
        P(None, "mp"),
        P(None, "mp", None),
        P(),
        P("dp", None, None),
        P("dp", None, None),
    )
    return jax.shard_map(
        shards,
        mesh=mesh,
        in_specs=placed,
        out_specs=(
            P("dp", None, None),
            P("dp", None, None),
            P("dp", None, None),
            P(None, None, "mp"),
            P(None, None, "mp"),
            P(None, None, None, "mp"),
            P(None, None, "mp"),
            P(None, "mp", None),
            P(None, "mp"),
            P(None, None, "mp"),
            P(None, "mp"),
            P(None, "mp", None),
            P(None, "mp"),
        ),
        check_vma=False,
    )
```

```python
import functools

import jax
import jax.numpy as jnp
from jax import lax
from jax.experimental import pallas as pl
from jax.experimental.pallas import tpu as pltpu
from jax.sharding import PartitionSpec as P

HD = 64
D = 768
KD = 192
SPANS = (128, 64, 32, 96)
SLABS = (32, 16, 8, 24)
OFFS = (0, 128, 192)
CLIPS = 32
PIECES = 21
EPS = 1e-06
NEG = -1000000000.0
MESH = pl.DeviceIdType.MESH
BF = jnp.bfloat16
F32 = jnp.float32
UNITS = (
    ("down", 0, "yz"),
    ("up", 0, "zy"),
    ("down", 1, "zy"),
    ("up", 1, "yz"),
    ("down", 2, "zy"),
    ("up", 2, "yz"),
    ("qo", 0, "yz"),
    ("qo", 1, "zy"),
    ("qo", 2, "zy"),
)
UNIT_OF = {(name, view): place for place, (name, view, _) in enumerate(UNITS)}
EASED = (("down", 0), ("up", 0))
TICKS = (0, 2, 1, 2, 2, 1, 6, 3, 2, 6, 6, 8, 8, 0)
OUT_OF = {"qo": 0, "up": 1, "down": 2}


def nn(a, b):
    return lax.dot_general(a, b, (((1,), (0,)), ((), ())), preferred_element_type=F32)


def nt(a, b):
    return lax.dot_general(a, b, (((1,), (1,)), ((), ())), preferred_element_type=F32)


def tn(a, b):
    return lax.dot_general(a, b, (((0,), (0,)), ((), ())), preferred_element_type=F32)


def gelu(inner):
    c0, c1 = 0.7978845608028654, 0.044715
    square = inner * inner
    th = jnp.tanh(c0 * inner * (1.0 + c1 * square))
    half = 0.5 * (1.0 + th)
    slope = half + 0.5 * inner * (1.0 - th * th) * c0 * (1.0 + 3.0 * c1 * square)
    return (inner * half).astype(BF), slope


def layer_stats(x):
    center = x - jnp.mean(x, -1, keepdims=True)
    spread = jnp.mean(center * center, -1, keepdims=True)
    inv = lax.rsqrt(spread + EPS)
    return center * inv, inv


def scratch_plan():
    plan = {}
    for i in range(4):
        span, slab = SPANS[i], SLABS[i]
        for name in ("n1", "s1", "n2", "s2", "zo", "s3", "da", "s4"):
            plan[name, i] = pltpu.VMEM((4, slab, D), BF)
        for name in ("r1", "r2", "r3", "r4"):
            plan[name, i] = pltpu.VMEM((3, slab, D), BF)
        for name in ("x", "af", "daf"):
            plan[name, i] = pltpu.VMEM((slab, D), F32)
        plan["dz", i] = pltpu.VMEM((4, slab, D), F32)
        for name in ("q", "k", "v", "ho"):
            plan[name, i] = pltpu.VMEM((span, KD), BF)
        plan["pr", i] = pltpu.VMEM((3 * span, span), F32)
        plan["dg", i] = pltpu.VMEM((span, D), F32)
        plan["ac", i] = pltpu.VMEM((span, D), BF)
        plan["wq", i] = pltpu.VMEM((3 * KD, D), BF)
        plan["wo", i] = pltpu.VMEM((KD, D), BF)
        plan["wu", i] = pltpu.VMEM((D, D), BF)
        plan["wd", i] = pltpu.VMEM((D, D), BF)
        if i < 3:
            plan["gt", i] = pltpu.VMEM((4, slab, D), BF)
            for name in ("ac4", "di4", "pj4"):
                plan[name, i] = pltpu.VMEM((4, span, KD), BF)
            for name in ("cz", "nr", "n2r", "dh"):
                plan[name, i] = pltpu.VMEM((span, D), BF)
    for turn in range(2):
        plan["pa", turn] = pltpu.VMEM((CLIPS, 8, 256), BF)
        plan["pb", turn] = pltpu.VMEM((CLIPS, 8, 256), BF)
        plan["pc", turn] = pltpu.VMEM((PIECES, 8, 256), BF)
    plan["ts"] = pltpu.VMEM((7, 8, D), BF)
    plan["mx"] = pltpu.VMEM((7, 8, D), F32)
    plan["cc"] = pltpu.VMEM((8, D), BF)
    plan["inv"] = pltpu.SMEM((CLIPS,), jnp.int32)
    plan["cl"] = pltpu.VMEM((8, D), BF)
    plan["cg"] = pltpu.VMEM((CLIPS, 8, D), BF)
    plan["ct"] = pltpu.VMEM((CLIPS, 8, D), BF)
    for name in ("bc", "dcb"):
        plan[name] = pltpu.VMEM((8, D), BF)
    for axis in "yz":
        plan["dc", axis] = pltpu.VMEM((4, 8, D), BF)
    plan["bg"] = pltpu.VMEM((4, 2, 4, 8, D), BF)
    plan["n20"] = pltpu.VMEM((3 * CLIPS, D), BF)
    plan["zc"] = pltpu.VMEM((4, 8, D), BF)
    plan["afc"] = pltpu.VMEM((4, 8, D), F32)
    plan["pc"] = pltpu.VMEM((4, 8, D), BF)
    plan["dac"] = pltpu.VMEM((8, D), F32)
    plan["gin"] = pltpu.VMEM((4, 24, D), F32)
    plan["gdx"] = pltpu.VMEM((4, 8, D), BF)
    plan["go"] = pltpu.VMEM((3, 16, 48, D), BF)
    for u, (name, view, _) in enumerate(UNITS):
        plan["fa", u] = pltpu.VMEM((4, SPANS[view], KD), BF)
        plan["fb", u] = pltpu.VMEM((4, SPANS[view], D), BF)
        if name == "qo":
            plan["fc", u] = pltpu.VMEM((4, SPANS[view], D), BF)
        plan["g", u] = pltpu.VMEM((4, 48, D), BF)
        plan["near", u] = pltpu.VMEM((3, 48, D), BF)
        plan["gx", u] = pltpu.VMEM((48, D), BF)
        plan["ga", u] = pltpu.VMEM((4, 48, D), BF)
    plan["sva"] = pltpu.VMEM((16, D), F32)
    plan["svb"] = pltpu.VMEM((16, D), F32)
    plan["svr"] = pltpu.VMEM((3, 16, D), F32)
    for step in range(3):
        plan["svs", step] = pltpu.VMEM((32, D), BF)
        plan["svt", step] = pltpu.VMEM((3, 32, D), BF)
    plan["ssem"] = pltpu.SemaphoreType.DMA((256,))
    plan["rsem"] = pltpu.SemaphoreType.DMA((256,))
    plan["lsem"] = pltpu.SemaphoreType.DMA((48,))
    return plan


def kernel(names, *refs):
    (
        partner,
        mix,
        lengths,
        tok,
        cot,
        cotg,
        gain,
        shift,
        b_out,
        b_down,
        b_up,
        b_qv,
        wq_all,
        wo_all,
        wu_all,
        wd_all,
        out_tok,
        out_glob,
        out_grad,
        out_small,
        out_left,
        out_right,
        out_qo,
        out_up,
        out_down,
    ) = refs[:25]
    b = dict(zip(names, refs[25:]))
    ssem, rsem, lsem = b["ssem"], b["rsem"], b["lsem"]
    outs = {"qo": out_qo, "up": out_up, "down": out_down}
    me = lax.axis_index("dp")
    m = lax.axis_index("mp")
    place = {"y": lax.div(me, 8), "x": lax.rem(lax.div(me, 4), 2), "z": lax.rem(me, 4)}

    def at(**moved):
        p = dict(place)
        p.update(moved)
        return ((p["y"] * 2 + p["x"]) * 4 + p["z"], m)

    count = {"s": 0, "l": 0}
    drains = []

    def new(kind):
        count[kind] += 1
        return count[kind] - 1

    def send(src, dst, s, dev):
        pltpu.make_async_remote_copy(
            src_ref=src,
            dst_ref=dst,
            send_sem=ssem.at[s],
            recv_sem=rsem.at[s],
            device_id=dev,
            device_id_type=MESH,
        ).start()

    def wait(like, sem):
        pltpu.make_async_copy(like, like, sem).wait()

    def landed(like, s):
        wait(like, rsem.at[s])
        drains.append(lambda: wait(like, ssem.at[s]))

    barrier = pltpu.get_barrier_semaphore()

    def greet(k, _):
        pl.semaphore_signal(
            barrier, inc=1, device_id=(lax.rem(me + k, CLIPS), m), device_id_type=MESH
        )
        return 0

    lax.fori_loop(1, CLIPS, greet, 0)
    for k in (1, 2, 3):
        pl.semaphore_signal(barrier, inc=1, device_id=(me, lax.rem(m + k, 4)), device_id_type=MESH)

    fetch = {}
    for i in range(4):
        for name, src in (("wq", wq_all), ("wo", wo_all), ("wu", wu_all), ("wd", wd_all)):
            copy = pltpu.make_async_copy(src.at[i], b[name, i], lsem.at[new("l")])
            copy.start()
            fetch[name, i] = copy

    def weight(name, i):
        if (name, i) in fetch:
            fetch.pop((name, i)).wait()
        return b[name, i]

    pl.semaphore_wait(barrier, CLIPS - 1 + 3)

    def gather_start(buf):
        s = new("s")
        for k in (2, 1, 3):
            send(buf.at[m], buf.at[m], s, (me, lax.rem(m + k, 4)))
        return buf.at[pl.ds(0, 3)], s

    def scatter_start(src, dst):
        s = new("s")
        for k in (2, 1, 3):
            t = lax.rem(m + k, 4)
            send(src.at[t], dst.at[k - 1], s, (me, t))
        return dst, s

    def dp_gather_start(src, dst):
        s = new("s")

        def step(k, _):
            send(src, dst.at[me], s, (lax.rem(me + k, CLIPS), m))
            return 0

        lax.fori_loop(1, CLIPS, step, 0)
        dst[me] = src[...]
        return dst.at[pl.ds(0, CLIPS - 1)], s

    factors = {}

    def share_rows(name, i, part, src_of):
        u = UNIT_OF[name, i]
        one = UNITS[u][2][0]
        p = place[one]
        dst = b[part, u]
        s = new("s")
        for k in (1, 3, 2):
            t = lax.rem(p + k, 4)
            send(src_of(t), dst.at[p], s, at(**{one: t}))
        dst[p] = src_of(p)[...]
        factors[part, u] = (dst.at[pl.ds(0, 3)], s)

    def rows_of(buf, i):
        span, slab = SPANS[i], SLABS[i]
        if slab % 16 == 0:
            return buf[...].reshape(span, D)
        return buf[...].astype(F32).reshape(span, D).astype(BF)

    groups = [m * 4 + r for r in range(4)] + [16 + m * 2 + r for r in range(2)] + [24 + m]

    def deal_start(turn, src_at):
        keep = b["pa", turn]
        s = new("s")
        for j in range(PIECES):

            @pl.when(me != j)
            def _():
                send(src_at(j // 3).at[:, pl.ds((j % 3) * 256, 256)], keep.at[me], s, (j, m))

            @pl.when(me == j)
            def _():
                keep[me] = src_at(j // 3)[:, (j % 3) * 256 : (j % 3) * 256 + 256]

        return s

    def few_or_all(buf, sem):
        @pl.when(me < PIECES)
        def _():
            wait(buf.at[pl.ds(0, PIECES - 1)], sem)

        @pl.when(me >= PIECES)
        def _():
            wait(buf, sem)

    def deal_turn(turn, s, index):
        keep, stage, got = b["pa", turn], b["pb", turn], b["pc", turn]
        t = new("s")

        @pl.when(me < PIECES)
        def _():
            wait(keep.at[pl.ds(0, CLIPS - 1)], rsem.at[s])
            for d in range(CLIPS):
                stage[d] = keep[index[d]]
            got[me] = stage[me]

            def step(k, _):
                d = lax.rem(me + k, CLIPS)
                send(stage.at[d], got.at[me], t, (d, m))
                return 0

            lax.fori_loop(1, CLIPS, step, 0)

        few_or_all(got, ssem.at[s])
        return t

    def deal_end(turn, t):
        stage, got = b["pb", turn], b["pc", turn]
        few_or_all(got, rsem.at[t])

        @pl.when(me < PIECES)
        def _():
            wait(stage.at[pl.ds(0, CLIPS - 1)], ssem.at[t])

        return [
            jnp.concatenate([got[3 * r + c].astype(F32) for c in range(3)], 1) for r in range(7)
        ]

    lam = mix[me]
    b["cc"][...] = jnp.zeros((8, D), BF)
    b["cc"][0:3] = cotg[0]
    s = deal_start(0, lambda r: tok.at[groups[r]])
    cot_ticket = dp_gather_start(b["cc"], b["ct"])
    t = deal_turn(0, s, partner)
    for i in range(3):
        row = lax.broadcasted_iota(jnp.int32, (SPANS[i], 1), 0)
        dz = jnp.where(row == 0, 0.0, cot[OFFS[i] : OFFS[i] + SPANS[i]].astype(F32))
        b["cz", i][...] = dz.astype(BF)
        b["dz", i][...] = dz.reshape(4, SLABS[i], D)
        share_rows("down", i, "fb", lambda t: b["cz", i])
    taken = deal_end(0, t)
    for r in range(7):
        value = lam * tok[groups[r]].astype(F32) + (1.0 - lam) * taken[r]
        if r < 4:
            b["x", 0][8 * r : 8 * r + 8] = value
        elif r < 6:
            b["x", 1][8 * (r - 4) : 8 * (r - 4) + 8] = value
        else:
            b["x", 2][...] = value

    def vec(ref, row):
        if len(ref.shape) == 3:
            return ref[row // 2, row % 2 : row % 2 + 1, :]
        return ref[row : row + 1, :]

    def norm(x, i, j):
        hat, _ = layer_stats(x)
        return hat * vec(gain, 2 * i + j) + vec(shift, 2 * i + j)

    def head_mask(h):
        lane = lax.broadcasted_iota(jnp.int32, (1, KD), 1)
        return (lane >= h * HD) & (lane < h * HD + HD)

    masks = [head_mask(h) for h in range(3)]
    zero = jnp.zeros((), BF)

    def stacked(a):
        return jnp.concatenate(
            [jnp.where(masks[h], a.astype(F32), 0.0) for h in range(3)], 0
        ).astype(BF)

    def folded(a, span):
        total = None
        for h in range(3):
            part = jnp.where(masks[h], a[h * span : (h + 1) * span], 0.0)
            total = part if total is None else total + part
        return total

    scale = HD ** (-0.5)

    def attend(i):
        span = SPANS[i]
        normed = rows_of(b["n1", i], i)
        wq = weight("wq", i)
        query = (nt(normed, wq[0:KD]) + vec(b_qv, 2 * i)).astype(BF)
        keys = nt(normed, wq[KD : 2 * KD]).astype(BF)
        values = (nt(normed, wq[2 * KD : 3 * KD]) + vec(b_qv, 2 * i + 1)).astype(BF)
        b["q", i][...] = query
        b["k", i][...] = keys
        b["v", i][...] = values
        scores = nt(stacked(query), keys) * scale
        if i < 3:
            col = lax.broadcasted_iota(jnp.int32, (1, span), 1)
            scores = jnp.where(col < lengths[0, i], scores, NEG)
        expo = jnp.exp(scores - jnp.max(scores, -1, keepdims=True))
        probs = expo / jnp.sum(expo, -1, keepdims=True)
        b["pr", i][...] = probs
        heads_out = folded(nn(probs.astype(BF), values), span).astype(BF)
        b["ho", i][...] = heads_out
        part = nn(heads_out, weight("wo", i)[...])
        b["s1", i][...] = part.astype(BF).reshape(4, SLABS[i], D) if SLABS[i] % 16 == 0 else (
            part.reshape(4, SLABS[i], D).astype(BF)
        )
        ticket = scatter_start(b["s1", i], b["r1", i])
        if i < 3:
            b["nr", i][...] = normed
            share_rows("qo", i, "fb", lambda t: b["nr", i])
        return ticket

    def put_slabs(name, i, value):
        b[name, i][...] = value.reshape(4, SLABS[i], D).astype(BF)

    def summed(send_name, recv_name, i, ticket):
        landed(*ticket)
        got = b[recv_name, i]
        total = b[send_name, i][m].astype(F32)
        for k in range(3):
            total = total + got[k].astype(F32)
        return total

    def middle(i, ticket):
        after = b["x", i][...] + summed("s1", "r1", i, ticket) + vec(b_out, i)
        b["af", i][...] = after
        b["n2", i][m] = norm(after, i, 1).astype(BF)
        return gather_start(b["n2", i])

    def feed(i, ticket):
        landed(*ticket)
        normed2 = rows_of(b["n2", i], i)
        if i < 3:
            b["n2r", i][...] = normed2
            share_rows("up", i, "fb", lambda t: b["n2r", i])
        inner = nn(normed2, weight("wu", i)[...]) + vec(b_up, i)
        active, b["dg", i][...] = gelu(inner)
        b["ac", i][...] = active
        part = nn(active, weight("wd", i)[...])
        put_slabs("s2", i, part)
        if i == 3:
            return scatter_start(b["s2", i], b["r2", i])
        for t in range(4):
            cols = slice(t * KD, t * KD + KD)
            b["ac4", i][t] = active[:, cols]
        return part[0:8][0:1]

    def feed_send(i):
        share_rows("down", i, "fa", lambda t: b["ac4", i].at[t])
        start_unit("down", i)
        return scatter_start(b["s2", i], b["r2", i])

    def finish(i, ticket):
        total = b["af", i][...] + summed("s2", "r2", i, ticket) + vec(b_down, i)
        b["zo", i][m] = total.astype(BF)
        return gather_start(b["zo", i])

    row8 = lax.broadcasted_iota(jnp.int32, (8, 1), 0)

    def rows8_at(buf, kinds):
        r_at = lax.broadcasted_iota(jnp.int32, (32 * kinds, 256), 0)
        k_at = lax.broadcasted_iota(jnp.int32, (32 * kinds, 256), 1)
        pick = (k_at == lax.rem(r_at, 32) * 8 + lax.div(r_at, 32)).astype(F32).astype(BF)
        return nn(pick, buf[...].astype(F32).reshape(256, D).astype(BF))

    def put_unit(name, row, value):
        value = value.astype(BF)
        chunks = value.shape[0] // 48
        lo = row // 48
        b["go"][OUT_OF[name], lo : lo + chunks] = value.reshape(chunks, 48, D)

    def back_feed(i):
        span = SPANS[i]
        dz = b["dz", i][...].reshape(span, D)
        dm = dz.astype(BF)
        dact = nt(dm, weight("wd", i)[...])
        dinner = (b["dg", i][...] * dact).astype(BF)
        put_slabs("s3", i, nt(dinner, weight("wu", i)[...]))
        if i < 3:
            for t in range(4):
                b["di4", i][t] = dinner[:, t * KD : t * KD + KD]
        else:
            ticket = scatter_start(b["s3", i], b["r3", i])
            for part in range(2):
                cols = slice(part * 384, part * 384 + 384)
                put_unit("down", part * 384, tn(b["ac", i][:, cols], dm))
            store_global("down")
            normed2 = rows_of(b["n2", i], i)
            for part in range(2):
                cols = slice(part * 384, part * 384 + 384)
                put_unit("up", part * 384, tn(dinner[:, cols], normed2))
            store_global("up")
        b["svb"][4 * i : 4 * i + 1] = jnp.sum(dz, 0, keepdims=True)
        b["svb"][4 * i + 2 : 4 * i + 3] = jnp.sum(dinner.astype(F32), 0, keepdims=True)
        return ticket if i == 3 else None

    def back_feed_send(i):
        share_rows("up", i, "fa", lambda t: b["di4", i].at[t])
        start_unit("up", i)
        return scatter_start(b["s3", i], b["r3", i])

    def norm_back(x, dy, i, j):
        hat, inv = layer_stats(x)
        b["sva"][4 * i + 2 * j : 4 * i + 2 * j + 1] = jnp.sum(dy * hat, 0, keepdims=True)
        b["sva"][4 * i + 2 * j + 1 : 4 * i + 2 * j + 2] = jnp.sum(dy, 0, keepdims=True)
        g = dy * vec(gain, 2 * i + j)
        return inv * (
            g - jnp.mean(g, -1, keepdims=True) - hat * jnp.mean(g * hat, -1, keepdims=True)
        )

    def back_middle(i, ticket):
        dn2 = summed("s3", "r3", i, ticket)
        dafter = b["dz", i][m] + norm_back(b["af", i][...], dn2, i, 1)
        b["daf", i][...] = dafter
        b["da", i][m] = dafter.astype(BF)
        return gather_start(b["da", i])

    def with_class_row(rows, first):
        row = lax.broadcasted_iota(jnp.int32, (rows.shape[0], 1), 0)
        return jnp.where(row == 0, first, rows.astype(F32)).astype(BF)

    def rows_send(i, ticket):
        landed(*ticket)
        b["dh", i][...] = rows_of(b["da", i], i)
        u = UNIT_OF["qo", i]
        one = UNITS[u][2][0]
        s = new("s")

        @pl.when(place[one] != 3)
        def _():
            half = pl.ds(lax.rem(m, 2) * (SPANS[i] // 2), SPANS[i] // 2)
            send(b["dh", i].at[half], b["fc", u].at[place[one], half], s, at(**{one: 3}))

        @pl.when(place[one] == 3)
        def _():
            b["fc", u][3] = b["dh", i][...]

        factors["fc", u] = s

    def rows_forward(i):
        u = UNIT_OF["qo", i]
        one, fc, n = UNITS[u][2][0], b["fc", u], SPANS[i] // 2
        s0, s = factors["fc", u], new("s")
        core = lax.rem(m, 2)

        @pl.when(place[one] == 3)
        def _():
            wait(fc.at[pl.ds(0, 3), pl.ds(0, n)], rsem.at[s0])
            part = fc.at[pl.ds(0, 3), pl.ds(core * n, n)]
            send(part, part, s, (me, m + 1 - 2 * core))

        factors["fc", u] = (s0, s)

    def class_rows_send():
        b["dcb"][...] = b["dac"][...].astype(BF)
        for axis in "yz":
            dst, p = b["dc", axis], place[axis]
            s = new("s")
            for k in (1, 3, 2):
                t = lax.rem(p + k, 4)
                send(b["dcb"], dst.at[p], s, at(**{axis: t}))
            dst[p] = b["dcb"][...]
            factors["dc", axis] = (dst.at[pl.ds(0, 3)], s)

    def back_attend(i, ticket):
        span = SPANS[i]
        if i < 3:
            da = with_class_row(b["dh", i][...], b["dac"][i : i + 1])
        else:
            landed(*ticket)
            da = rows_of(b["da", i], i)
        b["svb"][4 * i + 1 : 4 * i + 2] = jnp.sum(da.astype(F32), 0, keepdims=True)
        dheads = nt(da, weight("wo", i)[...]).astype(BF)
        query, keys, values = b["q", i][...], b["k", i][...], b["v", i][...]
        probs = b["pr", i][...]
        d3 = stacked(dheads)
        dprob = nt(d3, values)
        dscore = probs * (dprob - jnp.sum(dprob * probs, -1, keepdims=True))
        dscore = dscore.astype(BF)
        dquery = (folded(nn(dscore, keys), span) * scale).astype(BF)
        dkeys = (tn(dscore, stacked(query)) * scale).astype(BF)
        dvalues = tn(probs.astype(BF), d3).astype(BF)
        wq = weight("wq", i)
        part = nn(dquery, wq[0:KD]) + nn(dkeys, wq[KD : 2 * KD]) + nn(dvalues, wq[2 * KD : 3 * KD])
        put_slabs("s4", i, part)
        ticket = scatter_start(b["s4", i], b["r4", i])
        b["svb"][4 * i + 3 : 4 * i + 4, 0:KD] = jnp.sum(dquery.astype(F32), 0, keepdims=True)
        b["svb"][4 * i + 3 : 4 * i + 4, 256 : 256 + KD] = jnp.sum(
            dvalues.astype(F32), 0, keepdims=True
        )
        if i < 3:
            b["pj4", i][0] = dquery
            b["pj4", i][1] = dkeys
            b["pj4", i][2] = dvalues
            b["pj4", i][3] = b["ho", i][...]
            share_rows("qo", i, "fa", lambda t: b["pj4", i].at[t])
            start_unit("qo", i)
            return ticket
        normed = rows_of(b["n1", i], i)
        put_unit("qo", 0, tn(dquery, normed))
        put_unit("qo", KD, tn(dkeys, normed))
        put_unit("qo", 2 * KD, tn(dvalues, normed))
        put_unit("qo", 3 * KD, tn(b["ho", i][...], da))
        store_global("qo")
        return ticket

    def back_finish(i, ticket):
        dn1 = summed("s4", "r4", i, ticket)
        dafter = b["daf", i][...]
        if i < 3:
            row = lax.broadcasted_iota(jnp.int32, (SLABS[i], 1), 0)
            dafter = jnp.where((row == 0) & (m == 0), b["dac"][i : i + 1], dafter)
        return dafter + norm_back(b["x", i][...], dn1, i, 0)

    def class_feed(dgin):
        dz = jnp.zeros((8, D), F32)
        slope = jnp.zeros((8, D), F32)
        for i in range(3):
            first = cot[OFFS[i] : OFFS[i] + 16].astype(F32)[0:1]
            dz = jnp.where(row8 == i, first + dgin[i : i + 1], dz)
            slope = jnp.where(row8 == i, b["dg", i][0:8][0:1], slope)
        dm = dz.astype(BF)
        dact = jnp.zeros((8, D), F32)
        for i in range(3):
            dact = jnp.where(row8 == i, nt(dm, weight("wd", i)[...]), dact)
        dinner = (slope * dact).astype(BF)
        dn2 = jnp.zeros((8, D), F32)
        for i in range(3):
            dn2 = jnp.where(row8 == i, nt(dinner, weight("wu", i)[...]), dn2)
        b["pc"][m] = dn2.astype(BF)
        ticket = gather_start(b["pc"])
        both = dm.astype(F32)
        dinner = dinner.astype(F32)
        for i in range(3):
            both = jnp.where(row8 == 3 + i, dinner[i : i + 1], both)
            b["svb"][4 * i : 4 * i + 1] += dz[i : i + 1]
            b["svb"][4 * i + 2 : 4 * i + 3] += dinner[i : i + 1]
        b["bc"][...] = both.astype(BF)
        b["dac"][...] = dz
        return ticket

    def right_over_z():
        py, px, pz = place["y"], place["x"], place["z"]
        s = new("s")
        for k in (1, 3, 2):
            send(b["bc"], b["bg"].at[py, px, pz], s, at(z=lax.rem(pz + k, 4)))
        b["bg"][py, px, pz] = b["bc"][...]
        return b["bg"].at[0, 0, pl.ds(0, 3)], s

    def right_over_y(ticket):
        landed(*ticket)
        own = b["bg"].at[place["y"], place["x"]]
        s = new("s")
        for k in (1, 3, 2):
            send(own, own, s, at(y=lax.rem(place["y"] + k, 4)))
        return b["bg"].at[pl.ds(0, 3), 0], s

    def right_over_x(ticket):
        landed(*ticket)
        own = b["bg"].at[:, place["x"]]
        s = new("s")
        send(own, own, s, at(x=1 - place["x"]))
        return own, s

    def class_middle(ticket):
        landed(*ticket)
        dn2 = b["pc"][0].astype(F32)
        for k in range(1, 4):
            dn2 = dn2 + b["pc"][k].astype(F32)
        hat, inv = layer_stats(b["afc"][0])
        lead = jnp.where(m == 0, 1.0, 0.0)
        scales = jnp.zeros((8, D), F32)
        for i in range(3):
            scales = jnp.where(row8 == i, vec(gain, 2 * i + 1), scales)
            b["sva"][4 * i + 2 : 4 * i + 3] += lead * (dn2 * hat)[i : i + 1]
            b["sva"][4 * i + 3 : 4 * i + 4] += lead * dn2[i : i + 1]
        g = dn2 * scales
        b["dac"][...] += inv * (
            g - jnp.mean(g, -1, keepdims=True) - hat * jnp.mean(g * hat, -1, keepdims=True)
        )

    def half_spread(axis, out, own):
        p, px = place[axis], place["x"]
        up, down, far = lax.rem(p + 1, 4), lax.rem(p + 3, 4), lax.rem(p + 2, 4)
        to_up, to_down, to_x = at(**{axis: up}), at(**{axis: down}), at(x=1 - px)
        half = pl.ds(px * 384, 384)
        s = [new("s") for _ in range(7)]

        def slot(t):
            return out.at[pl.ds(t * 4, 4), :, half]

        like = slot(0)
        send(own.at[:, :, half], slot(p), s[0], to_up)
        send(own.at[:, :, half], slot(p), s[1], to_down)
        yield
        landed(like, s[0])
        part = slot(down).at[pl.ds(0, 2)]
        send(part, part, s[2], to_up)
        send(slot(down), slot(down), s[4], to_x)
        landed(like, s[1])
        part = slot(up).at[pl.ds(2, 2)]
        send(part, part, s[3], to_down)
        send(slot(up), slot(up), s[5], to_x)
        yield
        landed(like.at[pl.ds(0, 2)], s[2])
        landed(like.at[pl.ds(0, 2)], s[3])
        send(slot(far), slot(far), s[6], to_x)
        yield
        for k in (4, 5, 6):
            landed(like, s[k])

    def halves(ref):
        n = ref.shape[0] // 2
        return ref.at[pl.ds(0, n)], ref.at[pl.ds(n, n)]

    def ring_spread(axis, slot, own, like):
        p = place[axis]
        up, down = lax.rem(p + 1, 4), lax.rem(p + 3, 4)
        to_up, to_down = at(**{axis: up}), at(**{axis: down})
        s0, s1, s2, s3 = new("s"), new("s"), new("s"), new("s")
        send(own, slot(p), s0, to_up)
        send(own, slot(p), s1, to_down)
        yield
        landed(like, s0)
        part = halves(slot(down))[0]
        send(part, part, s2, to_up)
        landed(like, s1)
        part = halves(slot(up))[1]
        send(part, part, s3, to_down)
        yield
        landed(halves(like)[0], s2)
        landed(halves(like)[1], s3)

    def sum_unit(u):
        name, view, (one, two) = UNITS[u]
        span = SPANS[view]
        g, near, gx, ga = b["g", u], b["near", u], b["gx", u], b["ga", u]
        p1, p2 = place[one], place[two]
        out = outs[name].at[view]
        yield
        landed(*factors["fa", u])
        landed(*factors["fb", u])

        def multiply(rows):
            left = b["fa", u][...].reshape(4 * span, KD)
            g[...] = tn(left, rows).astype(BF).reshape(4, 48, D)

        if name == "qo":
            s_da, s_core = factors["fc", u]
            n = span // 2
            fc = b["fc", u]
            if ("dc", one) in factors:
                landed(*factors.pop(("dc", one)))

            @pl.when(p1 == 3)
            def _():
                wait(fc.at[pl.ds(0, 3), pl.ds(0, n)], rsem.at[s_core])
                first = b["dc", one][...].astype(F32)
                multiply(
                    jnp.concatenate(
                        [with_class_row(fc[k], first[k, view : view + 1]) for k in range(4)], 0
                    )
                )

            @pl.when(p1 != 3)
            def _():
                multiply(b["fb", u][...].reshape(4 * span, D))

            def drain():
                @pl.when(p1 != 3)
                def _():
                    wait(fc.at[0, pl.ds(0, n)], ssem.at[s_da])

                @pl.when(p1 == 3)
                def _():
                    wait(fc.at[pl.ds(0, 3), pl.ds(0, n)], ssem.at[s_core])

            drains.append(drain)
        else:
            multiply(b["fb", u][...].reshape(4 * span, D))
        s = new("s")
        for k in (1, 3, 2):
            t = lax.rem(p2 + k, 4)
            send(g.at[t], near.at[k - 1], s, at(**{two: t}))
        yield
        landed(near, s)
        total = g[p2].astype(F32)
        for k in range(3):
            total = total + near[k].astype(F32)
        ga[p2] = total.astype(BF)
        s = new("s")
        send(ga.at[p2], gx, s, at(x=1 - place["x"]))
        yield
        landed(gx, s)
        wait(gx, ssem.at[s])
        drains.pop()
        ga[p2] = (ga[p2].astype(F32) + gx[...].astype(F32)).astype(BF)
        s = new("s")
        for k in (1, 3, 2):
            send(ga.at[p2], ga.at[p2], s, at(**{two: lax.rem(p2 + k, 4)}))
        yield
        landed(ga.at[pl.ds(0, 3)], s)
        own = out.at[pl.ds(p1 * 4, 4)]
        store(ga, own)
        if (name, view) in EASED:
            yield from half_spread(one, out, ga)
            return
        yield from ring_spread(one, lambda t: out.at[pl.ds(t * 4, 4)], ga, out.at[pl.ds(0, 4)])

    stores = []

    def store(src, dst):
        copy = pltpu.make_async_copy(src, dst, lsem.at[new("l")])
        copy.start()
        stores.append(copy)

    running = []

    def store_global(name):
        store(b["go"].at[OUT_OF[name]], outs[name].at[3])

    def start_unit(name, i):
        unit = sum_unit(UNIT_OF[name, i])
        next(unit)
        running.append(unit)

    def tick(n):
        for _ in range(min(n, len(running))):
            unit = running.pop(0)
            if next(unit, "end") != "end":
                running.append(unit)

    tickets = [None] * 3
    back = [None] * 3
    for i in range(3):
        b["n1", i][m] = norm(b["x", i][...], i, 0).astype(BF)
        tickets[i] = gather_start(b["n1", i])
    for i in range(3):
        landed(*tickets[i])
        tickets[i] = attend(i)
    for i in range(3):
        tickets[i] = middle(i, tickets[i])
    firsts = jnp.zeros((8, D), F32)
    for i in range(3):
        firsts = jnp.where(row8 == i, b["af", i][0:8][0:1], firsts)
    b["afc"][m] = firsts
    after_ticket = gather_start(b["afc"])
    parts = jnp.zeros((8, D), F32)
    for i in range(3):
        parts = jnp.where(row8 == i, feed(i, tickets[i]), parts)
    b["zc"][m] = parts.astype(BF)
    ticket = gather_start(b["zc"])
    back_feed(0)
    landed(*after_ticket)
    classes = b["afc"][0]
    for i in range(3):
        classes = jnp.where(row8 == i, classes + vec(b_down, i), classes)
    landed(*ticket)
    for k in range(4):
        classes = classes + b["zc"][k].astype(F32)
    for i in range(3):
        classes = jnp.where(row8 == 3 + i, b["n2", i][0].astype(F32)[0:1], classes)
    b["cl"][...] = classes.astype(BF)
    class_ticket = dp_gather_start(b["cl"], b["cg"])
    for i in range(3):
        tickets[i] = feed_send(i)
    back[0] = back_feed_send(0)
    for i in (1, 2):
        back_feed(i)
        back[i] = back_feed_send(i)
    tick(TICKS[0])

    landed(*class_ticket)
    gathered = rows8_at(b["cg"], 6)
    gin = gathered[0:96]
    b["n20"][...] = gathered[96:192].astype(BF)
    b["gin"][...] = gin.reshape(4, 24, D)
    b["x", 3][...] = b["gin"][m]
    put_slabs("n1", 3, norm(gin, 3, 0))
    ticket = attend(3)
    landed(*cot_ticket)
    b["dz", 3][...] = rows8_at(b["ct"], 3).reshape(4, 24, D)
    tick(TICKS[1])
    ticket = middle(3, ticket)
    for i in range(3):
        tickets[i] = finish(i, tickets[i])
    tick(TICKS[2])
    glob_ticket = feed(3, ticket)
    ticket = back_feed(3)
    back[0] = back_middle(0, back[0])
    tick(TICKS[3])
    ticket = back_middle(3, ticket)
    for i in (1, 2):
        back[i] = back_middle(i, back[i])
    tick(TICKS[4])
    ticket = back_attend(3, ticket)
    for i in range(3):
        rows_send(i, back[i])
    tick(TICKS[5])
    dx = back_finish(3, ticket)
    o_at = lax.broadcasted_iota(jnp.int32, (8, 24), 0)
    w_at = lax.broadcasted_iota(jnp.int32, (8, 24), 1) + m * 24
    chosen = ((w_at == o_at * 32 + me) & (o_at < 3)).astype(F32).astype(BF)
    b["gdx"][m] = nn(chosen, dx.astype(BF)).astype(BF)
    ticket = gather_start(b["gdx"])
    glob_ticket = finish(3, glob_ticket)
    o_at = lax.broadcasted_iota(jnp.int32, (8, 96), 0)
    w_at = lax.broadcasted_iota(jnp.int32, (8, 96), 1)
    mine = ((w_at == o_at * 32 + me) & (o_at < 3)).astype(F32).astype(BF)
    tick(TICKS[6])
    landed(*ticket)
    dgin = b["gdx"][0].astype(F32)
    for k in range(1, 4):
        dgin = dgin + b["gdx"][k].astype(F32)

    ticket = class_feed(dgin)
    right_ticket = right_over_z()
    for i in range(3):
        rows_forward(i)
    for i in range(3):
        landed(*tickets[i])
        out_tok[OFFS[i] : OFFS[i] + SPANS[i]] = rows_of(b["zo", i], i)
    landed(*glob_ticket)
    out_glob[...] = nn(mine, rows_of(b["zo", 3], 3)).astype(BF)
    tick(TICKS[7])
    class_middle(ticket)
    class_rows_send()
    for i in range(3):
        tickets[i] = back_attend(i, None)
    right_ticket = right_over_y(right_ticket)
    tick(TICKS[8])
    for i in range(3):
        dx = back_finish(i, tickets[i])
        base = (0, 4, 6)[i]
        for r in range(SLABS[i] // 8):
            rows = dx[8 * r : 8 * r + 8]
            b["mx"][base + r] = lam * rows
            b["ts"][base + r] = ((1.0 - lam) * rows).astype(BF)
    right_ticket = right_over_x(right_ticket)
    def invert(d, _):
        found = jnp.int32(0)
        for c in range(CLIPS):
            found = jnp.where(partner[c] == d, c, found)
        b["inv"][d] = found
        return 0

    lax.fori_loop(0, CLIPS, invert, 0)
    s = deal_start(1, lambda r: b["ts"].at[r])

    s_mp = new("s")
    for k in (2, 1, 3):
        send(b["sva"], b["svr"].at[k - 1], s_mp, (me, lax.rem(m + k, 4)))
    tick(TICKS[9])
    t = deal_turn(1, s, b["inv"])
    tick(TICKS[10])
    landed(b["svr"], s_mp)
    sva = b["sva"][...] + b["svr"][0] + b["svr"][1] + b["svr"][2]
    svb = b["svb"][...]
    b["svs", 0][...] = jnp.concatenate([sva, svb], 0).astype(BF)

    def small_start(step, axis):
        s = new("s")
        far = (1, 3, 2) if axis != "x" else (1,)
        size = 4 if axis != "x" else 2
        for k in far:
            dev = at(**{axis: lax.rem(place[axis] + k, size)})
            send(b["svs", step], b["svt", step].at[k - 1], s, dev)
        return b["svt", step].at[pl.ds(0, len(far))], s

    def small_end(step, ticket, axis):
        landed(*ticket)
        total = b["svs", step][...].astype(F32)
        for k in range(3 if axis != "x" else 1):
            total = total + b["svt", step][k].astype(F32)
        return total

    ticket = small_start(0, "y")
    taken = deal_end(1, t)
    for i in range(3):
        base = (0, 4, 6)[i]
        for r in range(SLABS[i] // 8):
            rows = b["mx"][base + r] + taken[base + r]
            b["gt", i][m, 8 * r : 8 * r + 8] = rows.astype(BF)
        tickets[i] = gather_start(b["gt", i])
    tick(TICKS[11])
    b["svs", 1][...] = small_end(0, ticket, "y").astype(BF)
    ticket = small_start(1, "z")
    tick(TICKS[12])
    for i in range(3):
        landed(*tickets[i])
        out_grad[OFFS[i] : OFFS[i] + SPANS[i]] = rows_of(b["gt", i], i)
    b["svs", 2][...] = small_end(1, ticket, "z").astype(BF)
    ticket = small_start(2, "x")
    landed(*right_ticket)
    for i in range(3):
        rows = b["n20"][CLIPS * i : CLIPS * i + CLIPS]
        active, _ = gelu(nn(rows, weight("wu", i)[...]) + vec(b_up, i))
        out_left[CLIPS * i : CLIPS * i + CLIPS] = active
    out_left[3 * CLIPS : 6 * CLIPS] = b["n20"][...]
    out_right[...] = rows8_at(b["bg"], 6).astype(BF)
    tick(TICKS[13])
    total = small_end(2, ticket, "x")
    out_small[0:12] = total[0:12]
    out_small[12:16] = sva[12:16]
    out_small[16:28] = total[16:28]
    out_small[28:32] = svb[12:16]
    while running:
        tick(1)
    for drain in drains:
        drain()
    for copy in stores:
        copy.wait()


def shards(
    tokens,
    lengths,
    partner,
    mix_coef,
    norm_gain,
    norm_bias,
    w_qkv,
    b_qv,
    w_out,
    b_out,
    w_up,
    b_up,
    w_down,
    b_down,
    cot_tokens,
    cot_global,
):
    wq = jnp.transpose(w_qkv, (0, 2, 3, 1)).reshape(4, 3 * KD, D)
    plan = scratch_plan()
    names = list(plan)
    smem = pl.BlockSpec(memory_space=pltpu.SMEM)
    vmem = pl.BlockSpec(memory_space=pltpu.VMEM)
    hbm = pl.BlockSpec(memory_space=pl.ANY)
    unit = jax.ShapeDtypeStruct((4, 16, 48, D), BF)
    out_tok, out_glob, out_grad, small, left, right, qo, up, down = pl.pallas_call(
        functools.partial(kernel, names),
        out_shape=(
            jax.ShapeDtypeStruct((224, D), BF),
            jax.ShapeDtypeStruct((8, D), BF),
            jax.ShapeDtypeStruct((224, D), BF),
            jax.ShapeDtypeStruct((32, D), F32),
            jax.ShapeDtypeStruct((6 * CLIPS, D), BF),
            jax.ShapeDtypeStruct((6 * CLIPS, D), BF),
            unit,
            unit,
            unit,
        ),
        in_specs=[smem] * 3 + [vmem] * 9 + [hbm] * 4,
        out_specs=(vmem,) * 6 + (hbm,) * 3,
        scratch_shapes=list(plan.values()),
        compiler_params=pltpu.CompilerParams(
            collective_id=0, has_side_effects=True, vmem_limit_bytes=60 * 2**20
        ),
    )(
        partner,
        mix_coef,
        lengths,
        tokens.reshape(28, 8, D),
        cot_tokens[0],
        cot_global,
        norm_gain,
        norm_bias,
        b_out,
        b_down,
        b_up,
        b_qv,
        wq,
        w_out,
        w_up,
        w_down,
    )
    out_tok, out_glob, out_grad, gain, shift, qkv, qv, out, bout, ups, bup, downs, bdown = widen(
        out_tok,
        out_glob,
        out_grad,
        small,
        left,
        right,
        *(a.reshape(4, D, D) for a in (qo, up, down)),
    )
    return (
        out_tok,
        out_glob,
        out_grad,
        gain,
        shift,
        jnp.transpose(qkv.reshape(4, 3, KD, D), (0, 3, 1, 2)),
        qv,
        out,
        bout,
        ups,
        bup,
        downs,
        bdown,
    )


def widen_kernel(*refs):
    tok, glob, grad, small, left, right, qo, up, down = refs[:9]
    o_tok, o_glob, o_grad, o_gain, o_shift, o_qkv, o_qv, o_out, o_bout, o_up, o_bup, o_down, o_bdown = refs[9:22]
    held, wide, sem_in, sem_out = refs[22:]
    order = [(i, a) for i in (3, 0, 1, 2) for a in range(3)]
    fetches = []
    for n, (i, a) in enumerate(order):
        copy = pltpu.make_async_copy((qo, up, down)[a].at[i], held.at[n], sem_in.at[n])
        copy.start()
        fetches.append(copy)
    o_tok[0] = tok[...]
    o_grad[0] = grad[...]
    o_glob[0] = glob[0:3]
    m = lax.axis_index("mp")

    def share(row):
        value = small[row : row + 1]
        mine = value[:, 0:KD]
        for k in range(1, 4):
            mine = jnp.where(m == k, value[:, k * KD : (k + 1) * KD], mine)
        return mine

    for i in range(4):
        for j in range(2):
            o_gain[i, j : j + 1] = share(4 * i + 2 * j)
            o_shift[i, j : j + 1] = share(4 * i + 2 * j + 1)
        row = 16 + 4 * i
        o_bdown[i : i + 1] = share(row)
        o_bout[i : i + 1] = share(row + 1)
        o_bup[i : i + 1] = small[row + 2 : row + 3]
        o_qv[i, 0:1] = small[row + 3 : row + 4, 0:KD]
        o_qv[i, 1:2] = small[row + 3 : row + 4, 256 : 256 + KD]
    slots = wide.shape[0]
    busy = [[] for _ in range(slots)]
    for n, (i, a) in enumerate(order):
        slot = n % slots
        fetches[n].wait()
        for copy in busy[slot]:
            copy.wait()
        value = held[n].astype(F32)
        if a > 0 and i < 3:
            base = CLIPS * (3 * (a == 1) + i)
            rows, cols = (right, left) if a == 1 else (left, right)
            value = value + tn(rows[base : base + CLIPS], cols[base : base + CLIPS])
        wide[slot] = value.T if a == 1 else value
        src = wide.at[slot]
        if a == 0:
            pairs = (
                (src.at[pl.ds(0, 3 * KD)], o_qkv.at[i]),
                (src.at[pl.ds(3 * KD, KD)], o_out.at[i]),
            )
        else:
            pairs = ((src, (o_up, o_down)[a - 1].at[i]),)
        busy[slot] = []
        for k, (part, dst) in enumerate(pairs):
            copy = pltpu.make_async_copy(part, dst, sem_out.at[slot, k])
            copy.start()
            busy[slot].append(copy)
    for copies in busy:
        for copy in copies:
            copy.wait()


def widen(tok, glob, grad, small, left, right, qo, up, down):
    shape = jax.ShapeDtypeStruct
    vmem = pl.BlockSpec(memory_space=pltpu.VMEM)
    hbm = pl.BlockSpec(memory_space=pl.ANY)
    return pl.pallas_call(
        widen_kernel,
        in_specs=[vmem] * 6 + [hbm] * 3,
        out_specs=[vmem, vmem, vmem, vmem, vmem, hbm, vmem, hbm, vmem, hbm, vmem, hbm, vmem],
        out_shape=[shape((1, 224, D), BF), shape((1, 3, D), BF), shape((1, 224, D), BF)]
        + [shape((4, 2, KD), F32), shape((4, 2, KD), F32), shape((4, 3 * KD, D), F32)]
        + [shape((4, 2, KD), F32), shape((4, KD, D), F32), shape((4, KD), F32)]
        + [shape((4, D, D), F32), shape((4, D), F32), shape((4, D, D), F32), shape((4, KD), F32)],
        scratch_shapes=[
            pltpu.VMEM((12, D, D), BF),
            pltpu.VMEM((5, D, D), F32),
            pltpu.SemaphoreType.DMA((12,)),
            pltpu.SemaphoreType.DMA((5, 2)),
        ],
        compiler_params=pltpu.CompilerParams(vmem_limit_bytes=60 * 2**20),
    )(tok, glob, grad, small, left, right, qo, up, down)


def solution(mesh):
    placed = (
        P("dp", None, None),
        P("dp", None),
        P(),
        P(),
        P(),
        P(),
        P(None, None, None, "mp"),
        P(None, None, "mp"),
        P(None, "mp", None),
        P(),
        P(None, None, "mp"),
        P(None, "mp"),
        P(None, "mp", None),
        P(),
        P("dp", None, None),
        P("dp", None, None),
    )
    return jax.shard_map(
        shards,
        mesh=mesh,
        in_specs=placed,
        out_specs=(
            P("dp", None, None),
            P("dp", None, None),
            P("dp", None, None),
            P(None, None, "mp"),
            P(None, None, "mp"),
            P(None, None, None, "mp"),
            P(None, None, "mp"),
            P(None, "mp", None),
            P(None, "mp"),
            P(None, None, "mp"),
            P(None, "mp"),
            P(None, "mp", None),
            P(None, "mp"),
        ),
        check_vma=False,
    )
```

```python
import functools

import jax
import jax.numpy as jnp
from jax import lax
from jax.experimental import pallas as pl
from jax.experimental.pallas import tpu as pltpu
from jax.sharding import PartitionSpec as P

HD = 64
D = 768
KD = 192
SPANS = (128, 64, 32, 96)
SLABS = (32, 16, 8, 24)
OFFS = (0, 128, 192)
CLIPS = 32
PIECES = 21
EPS = 1e-06
NEG = -1000000000.0
MESH = pl.DeviceIdType.MESH
BF = jnp.bfloat16
F32 = jnp.float32
UNITS = (
    ("down", 0, "yz"),
    ("up", 0, "zy"),
    ("down", 1, "zy"),
    ("up", 1, "yz"),
    ("down", 2, "zy"),
    ("up", 2, "yz"),
    ("qo", 0, "yz"),
    ("qo", 1, "zy"),
    ("qo", 2, "zy"),
)
UNIT_OF = {(name, view): place for place, (name, view, _) in enumerate(UNITS)}
TICKS = (0, 2, 1, 2, 2, 1, 6, 3, 2, 6, 6, 8, 8, 0)
OUT_OF = {"qo": 0, "up": 1, "down": 2}


def nn(a, b):
    return lax.dot_general(a, b, (((1,), (0,)), ((), ())), preferred_element_type=F32)


def nt(a, b):
    return lax.dot_general(a, b, (((1,), (1,)), ((), ())), preferred_element_type=F32)


def tn(a, b):
    return lax.dot_general(a, b, (((0,), (0,)), ((), ())), preferred_element_type=F32)


def gelu(inner):
    c0, c1 = 0.7978845608028654, 0.044715
    square = inner * inner
    th = jnp.tanh(c0 * inner * (1.0 + c1 * square))
    half = 0.5 * (1.0 + th)
    slope = half + 0.5 * inner * (1.0 - th * th) * c0 * (1.0 + 3.0 * c1 * square)
    return (inner * half).astype(BF), slope


def layer_stats(x):
    center = x - jnp.mean(x, -1, keepdims=True)
    spread = jnp.mean(center * center, -1, keepdims=True)
    inv = lax.rsqrt(spread + EPS)
    return center * inv, inv


def scratch_plan():
    plan = {}
    for i in range(4):
        span, slab = SPANS[i], SLABS[i]
        for name in ("n1", "s1", "n2", "s2", "zo", "s3", "da", "s4"):
            plan[name, i] = pltpu.VMEM((4, slab, D), BF)
        for name in ("r1", "r2", "r3", "r4"):
            plan[name, i] = pltpu.VMEM((3, slab, D), BF)
        for name in ("x", "af", "daf"):
            plan[name, i] = pltpu.VMEM((slab, D), F32)
        plan["dz", i] = pltpu.VMEM((4, slab, D), F32)
        for name in ("q", "k", "v", "ho"):
            plan[name, i] = pltpu.VMEM((span, KD), BF)
        plan["pr", i] = pltpu.VMEM((3 * span, span), F32)
        plan["dg", i] = pltpu.VMEM((span, D), F32)
        plan["ac", i] = pltpu.VMEM((span, D), BF)
        plan["wq", i] = pltpu.VMEM((3 * KD, D), BF)
        plan["wo", i] = pltpu.VMEM((KD, D), BF)
        plan["wu", i] = pltpu.VMEM((D, D), BF)
        plan["wd", i] = pltpu.VMEM((D, D), BF)
        plan["ut", i] = pltpu.VMEM((D, D), BF)
        plan["dt", i] = pltpu.VMEM((D, D), BF)
        if i < 3:
            plan["gt", i] = pltpu.VMEM((4, slab, D), BF)
            for name in ("ac4", "di4", "pj4"):
                plan[name, i] = pltpu.VMEM((4, span, KD), BF)
            for name in ("cz", "nr", "n2r", "dh"):
                plan[name, i] = pltpu.VMEM((span, D), BF)
    for turn in range(2):
        plan["pa", turn] = pltpu.VMEM((CLIPS, 8, 256), BF)
        plan["pb", turn] = pltpu.VMEM((CLIPS, 8, 256), BF)
        plan["pc", turn] = pltpu.VMEM((PIECES, 8, 256), BF)
    plan["ts"] = pltpu.VMEM((7, 8, D), BF)
    plan["mx"] = pltpu.VMEM((7, 8, D), F32)
    plan["cc"] = pltpu.VMEM((8, D), BF)
    plan["inv"] = pltpu.SMEM((CLIPS,), jnp.int32)
    plan["cl"] = pltpu.VMEM((8, D), BF)
    plan["cg"] = pltpu.VMEM((CLIPS, 8, D), BF)
    plan["ct"] = pltpu.VMEM((CLIPS, 8, D), BF)
    for name in ("bc", "dcb"):
        plan[name] = pltpu.VMEM((8, D), BF)
    for axis in "yz":
        plan["dc", axis] = pltpu.VMEM((4, 8, D), BF)
    plan["bg"] = pltpu.VMEM((4, 2, 4, 8, D), BF)
    plan["n20"] = pltpu.VMEM((3 * CLIPS, D), BF)
    plan["zc"] = pltpu.VMEM((4, 8, D), BF)
    plan["afc"] = pltpu.VMEM((4, 8, D), F32)
    plan["pc"] = pltpu.VMEM((4, 8, D), BF)
    plan["dac"] = pltpu.VMEM((8, D), F32)
    plan["gin"] = pltpu.VMEM((4, 24, D), F32)
    plan["gdx"] = pltpu.VMEM((4, 8, D), BF)
    plan["go"] = pltpu.VMEM((3, 16, 48, D), BF)
    for u, (name, view, _) in enumerate(UNITS):
        plan["fa", u] = pltpu.VMEM((4, SPANS[view], KD), BF)
        plan["fb", u] = pltpu.VMEM((4, SPANS[view], D), BF)
        if name == "qo":
            plan["fc", u] = pltpu.VMEM((4, SPANS[view], D), BF)
        plan["g", u] = pltpu.VMEM((4, 48, D), BF)
        plan["near", u] = pltpu.VMEM((3, 48, D), BF)
        plan["gx", u] = pltpu.VMEM((48, D), BF)
        plan["ga", u] = pltpu.VMEM((4, 48, D), BF)
    plan["sva"] = pltpu.VMEM((16, D), F32)
    plan["svb"] = pltpu.VMEM((16, D), F32)
    plan["svr"] = pltpu.VMEM((3, 16, D), F32)
    for step in range(3):
        plan["svs", step] = pltpu.VMEM((32, D), BF)
        plan["svt", step] = pltpu.VMEM((3, 32, D), BF)
    plan["ssem"] = pltpu.SemaphoreType.DMA((256,))
    plan["rsem"] = pltpu.SemaphoreType.DMA((256,))
    plan["lsem"] = pltpu.SemaphoreType.DMA((48,))
    return plan


def kernel(names, *refs):
    (
        partner,
        mix,
        lengths,
        tok,
        cot,
        cotg,
        gain,
        shift,
        b_out,
        b_down,
        b_up,
        b_qv,
        wq_all,
        wo_all,
        wu_all,
        wd_all,
        out_tok,
        out_glob,
        out_grad,
        out_small,
        out_left,
        out_right,
        out_qo,
        out_up,
        out_down,
    ) = refs[:25]
    b = dict(zip(names, refs[25:]))
    ssem, rsem, lsem = b["ssem"], b["rsem"], b["lsem"]
    outs = {"qo": out_qo, "up": out_up, "down": out_down}
    me = lax.axis_index("dp")
    m = lax.axis_index("mp")
    place = {"y": lax.div(me, 8), "x": lax.rem(lax.div(me, 4), 2), "z": lax.rem(me, 4)}

    def at(**moved):
        p = dict(place)
        p.update(moved)
        return ((p["y"] * 2 + p["x"]) * 4 + p["z"], m)

    count = {"s": 0, "l": 0}
    drains = []

    def new(kind):
        count[kind] += 1
        return count[kind] - 1

    def send(src, dst, s, dev):
        pltpu.make_async_remote_copy(
            src_ref=src,
            dst_ref=dst,
            send_sem=ssem.at[s],
            recv_sem=rsem.at[s],
            device_id=dev,
            device_id_type=MESH,
        ).start()

    def wait(like, sem):
        pltpu.make_async_copy(like, like, sem).wait()

    def landed(like, s):
        wait(like, rsem.at[s])
        drains.append(lambda: wait(like, ssem.at[s]))

    barrier = pltpu.get_barrier_semaphore()

    def greet(k, _):
        pl.semaphore_signal(
            barrier, inc=1, device_id=(lax.rem(me + k, CLIPS), m), device_id_type=MESH
        )
        return 0

    lax.fori_loop(1, CLIPS, greet, 0)
    for k in (1, 2, 3):
        pl.semaphore_signal(barrier, inc=1, device_id=(me, lax.rem(m + k, 4)), device_id_type=MESH)

    fetch = {}
    for i in range(4):
        for name, src in (("wq", wq_all), ("wo", wo_all), ("wu", wu_all), ("wd", wd_all)):
            copy = pltpu.make_async_copy(src.at[i], b[name, i], lsem.at[new("l")])
            copy.start()
            fetch[name, i] = copy

    def weight(name, i):
        if (name, i) in fetch:
            fetch.pop((name, i)).wait()
        return b[name, i]

    pl.semaphore_wait(barrier, CLIPS - 1 + 3)

    def gather_start(buf):
        s = new("s")
        for k in (2, 1, 3):
            send(buf.at[m], buf.at[m], s, (me, lax.rem(m + k, 4)))
        return buf.at[pl.ds(0, 3)], s

    def scatter_start(src, dst):
        s = new("s")
        for k in (2, 1, 3):
            t = lax.rem(m + k, 4)
            send(src.at[t], dst.at[k - 1], s, (me, t))
        return dst, s

    def dp_gather_start(src, dst):
        s = new("s")

        def step(k, _):
            send(src, dst.at[me], s, (lax.rem(me + k, CLIPS), m))
            return 0

        lax.fori_loop(1, CLIPS, step, 0)
        dst[me] = src[...]
        return dst.at[pl.ds(0, CLIPS - 1)], s

    factors = {}

    def share_rows(name, i, part, src_of):
        u = UNIT_OF[name, i]
        one = UNITS[u][2][0]
        p = place[one]
        dst = b[part, u]
        s = new("s")
        for k in (1, 3, 2):
            t = lax.rem(p + k, 4)
            send(src_of(t), dst.at[p], s, at(**{one: t}))
        dst[p] = src_of(p)[...]
        factors[part, u] = (dst.at[pl.ds(0, 3)], s)

    def rows_of(buf, i):
        span, slab = SPANS[i], SLABS[i]
        if slab % 16 == 0:
            return buf[...].reshape(span, D)
        return buf[...].astype(F32).reshape(span, D).astype(BF)

    groups = [m * 4 + r for r in range(4)] + [16 + m * 2 + r for r in range(2)] + [24 + m]

    def deal_start(turn, src_at):
        keep = b["pa", turn]
        s = new("s")
        for j in range(PIECES):

            @pl.when(me != j)
            def _():
                send(src_at(j // 3).at[:, pl.ds((j % 3) * 256, 256)], keep.at[me], s, (j, m))

            @pl.when(me == j)
            def _():
                keep[me] = src_at(j // 3)[:, (j % 3) * 256 : (j % 3) * 256 + 256]

        return s

    def few_or_all(buf, sem):
        @pl.when(me < PIECES)
        def _():
            wait(buf.at[pl.ds(0, PIECES - 1)], sem)

        @pl.when(me >= PIECES)
        def _():
            wait(buf, sem)

    def deal_turn(turn, s, index):
        keep, stage, got = b["pa", turn], b["pb", turn], b["pc", turn]
        t = new("s")

        @pl.when(me < PIECES)
        def _():
            wait(keep.at[pl.ds(0, CLIPS - 1)], rsem.at[s])
            for d in range(CLIPS):
                stage[d] = keep[index[d]]
            got[me] = stage[me]

            def step(k, _):
                d = lax.rem(me + k, CLIPS)
                send(stage.at[d], got.at[me], t, (d, m))
                return 0

            lax.fori_loop(1, CLIPS, step, 0)

        few_or_all(got, ssem.at[s])
        return t

    def deal_end(turn, t):
        stage, got = b["pb", turn], b["pc", turn]
        few_or_all(got, rsem.at[t])

        @pl.when(me < PIECES)
        def _():
            wait(stage.at[pl.ds(0, CLIPS - 1)], ssem.at[t])

        return [
            jnp.concatenate([got[3 * r + c].astype(F32) for c in range(3)], 1) for r in range(7)
        ]

    lam = mix[me]
    b["cc"][...] = jnp.zeros((8, D), BF)
    b["cc"][0:3] = cotg[0]
    s = deal_start(0, lambda r: tok.at[groups[r]])
    cot_ticket = dp_gather_start(b["cc"], b["ct"])
    for i in range(4):
        b["dt", i][...] = weight("wd", i)[...].T
    t = deal_turn(0, s, partner)
    for i in range(4):
        b["ut", i][...] = weight("wu", i)[...].T
    for i in range(3):
        row = lax.broadcasted_iota(jnp.int32, (SPANS[i], 1), 0)
        dz = jnp.where(row == 0, 0.0, cot[OFFS[i] : OFFS[i] + SPANS[i]].astype(F32))
        b["cz", i][...] = dz.astype(BF)
        b["dz", i][...] = dz.reshape(4, SLABS[i], D)
        share_rows("down", i, "fb", lambda t: b["cz", i])
    taken = deal_end(0, t)
    for r in range(7):
        value = lam * tok[groups[r]].astype(F32) + (1.0 - lam) * taken[r]
        if r < 4:
            b["x", 0][8 * r : 8 * r + 8] = value
        elif r < 6:
            b["x", 1][8 * (r - 4) : 8 * (r - 4) + 8] = value
        else:
            b["x", 2][...] = value

    def vec(ref, row):
        if len(ref.shape) == 3:
            return ref[row // 2, row % 2 : row % 2 + 1, :]
        return ref[row : row + 1, :]

    def norm(x, i, j):
        hat, _ = layer_stats(x)
        return hat * vec(gain, 2 * i + j) + vec(shift, 2 * i + j)

    def head_mask(h):
        lane = lax.broadcasted_iota(jnp.int32, (1, KD), 1)
        return (lane >= h * HD) & (lane < h * HD + HD)

    masks = [head_mask(h) for h in range(3)]
    zero = jnp.zeros((), BF)

    def stacked(a):
        return jnp.concatenate(
            [jnp.where(masks[h], a.astype(F32), 0.0) for h in range(3)], 0
        ).astype(BF)

    def folded(a, span):
        total = None
        for h in range(3):
            part = jnp.where(masks[h], a[h * span : (h + 1) * span], 0.0)
            total = part if total is None else total + part
        return total

    scale = HD ** (-0.5)

    def attend(i):
        span = SPANS[i]
        normed = rows_of(b["n1", i], i)
        wq = weight("wq", i)
        query = (nt(normed, wq[0:KD]) + vec(b_qv, 2 * i)).astype(BF)
        keys = nt(normed, wq[KD : 2 * KD]).astype(BF)
        values = (nt(normed, wq[2 * KD : 3 * KD]) + vec(b_qv, 2 * i + 1)).astype(BF)
        b["q", i][...] = query
        b["k", i][...] = keys
        b["v", i][...] = values
        scores = nt(stacked(query), keys) * scale
        if i < 3:
            col = lax.broadcasted_iota(jnp.int32, (1, span), 1)
            scores = jnp.where(col < lengths[0, i], scores, NEG)
        expo = jnp.exp(scores - jnp.max(scores, -1, keepdims=True))
        probs = expo / jnp.sum(expo, -1, keepdims=True)
        b["pr", i][...] = probs
        heads_out = folded(nn(probs.astype(BF), values), span).astype(BF)
        b["ho", i][...] = heads_out
        part = nn(heads_out, weight("wo", i)[...])
        b["s1", i][...] = part.astype(BF).reshape(4, SLABS[i], D) if SLABS[i] % 16 == 0 else (
            part.reshape(4, SLABS[i], D).astype(BF)
        )
        ticket = scatter_start(b["s1", i], b["r1", i])
        if i < 3:
            b["nr", i][...] = normed
            share_rows("qo", i, "fb", lambda t: b["nr", i])
        return ticket

    def put_slabs(name, i, value):
        b[name, i][...] = value.reshape(4, SLABS[i], D).astype(BF)

    def summed(send_name, recv_name, i, ticket):
        landed(*ticket)
        got = b[recv_name, i]
        total = b[send_name, i][m].astype(F32)
        for k in range(3):
            total = total + got[k].astype(F32)
        return total

    def middle(i, ticket):
        after = b["x", i][...] + summed("s1", "r1", i, ticket) + vec(b_out, i)
        b["af", i][...] = after
        b["n2", i][m] = norm(after, i, 1).astype(BF)
        return gather_start(b["n2", i])

    def feed(i, ticket):
        landed(*ticket)
        normed2 = rows_of(b["n2", i], i)
        if i < 3:
            b["n2r", i][...] = normed2
            share_rows("up", i, "fb", lambda t: b["n2r", i])
        inner = nn(normed2, weight("wu", i)[...]) + vec(b_up, i)
        active, b["dg", i][...] = gelu(inner)
        b["ac", i][...] = active
        part = nn(active, weight("wd", i)[...])
        put_slabs("s2", i, part)
        if i == 3:
            return scatter_start(b["s2", i], b["r2", i])
        for t in range(4):
            cols = slice(t * KD, t * KD + KD)
            b["ac4", i][t] = active[:, cols]
        return part[0:8][0:1]

    def feed_send(i):
        share_rows("down", i, "fa", lambda t: b["ac4", i].at[t])
        start_unit("down", i)
        return scatter_start(b["s2", i], b["r2", i])

    def finish(i, ticket):
        total = b["af", i][...] + summed("s2", "r2", i, ticket) + vec(b_down, i)
        b["zo", i][m] = total.astype(BF)
        return gather_start(b["zo", i])

    row8 = lax.broadcasted_iota(jnp.int32, (8, 1), 0)

    def rows8_at(buf, kinds):
        r_at = lax.broadcasted_iota(jnp.int32, (32 * kinds, 256), 0)
        k_at = lax.broadcasted_iota(jnp.int32, (32 * kinds, 256), 1)
        pick = (k_at == lax.rem(r_at, 32) * 8 + lax.div(r_at, 32)).astype(F32).astype(BF)
        return nn(pick, buf[...].astype(F32).reshape(256, D).astype(BF))

    def put_unit(name, row, value):
        value = value.astype(BF)
        chunks = value.shape[0] // 48
        lo = row // 48
        b["go"][OUT_OF[name], lo : lo + chunks] = value.reshape(chunks, 48, D)

    def back_feed(i):
        span = SPANS[i]
        dz = b["dz", i][...].reshape(span, D)
        dm = dz.astype(BF)
        dact = nn(dm, b["dt", i][...])
        dinner = (b["dg", i][...] * dact).astype(BF)
        put_slabs("s3", i, nn(dinner, b["ut", i][...]))
        if i < 3:
            for t in range(4):
                b["di4", i][t] = dinner[:, t * KD : t * KD + KD]
        else:
            ticket = scatter_start(b["s3", i], b["r3", i])
            for part in range(2):
                cols = slice(part * 384, part * 384 + 384)
                put_unit("down", part * 384, tn(b["ac", i][:, cols], dm))
            store_global("down")
            normed2 = rows_of(b["n2", i], i)
            for part in range(2):
                cols = slice(part * 384, part * 384 + 384)
                put_unit("up", part * 384, tn(dinner[:, cols], normed2))
            store_global("up")
        b["svb"][4 * i : 4 * i + 1] = jnp.sum(dz, 0, keepdims=True)
        b["svb"][4 * i + 2 : 4 * i + 3] = jnp.sum(dinner.astype(F32), 0, keepdims=True)
        return ticket if i == 3 else None

    def back_feed_send(i):
        share_rows("up", i, "fa", lambda t: b["di4", i].at[t])
        start_unit("up", i)
        return scatter_start(b["s3", i], b["r3", i])

    def norm_back(x, dy, i, j):
        hat, inv = layer_stats(x)
        b["sva"][4 * i + 2 * j : 4 * i + 2 * j + 1] = jnp.sum(dy * hat, 0, keepdims=True)
        b["sva"][4 * i + 2 * j + 1 : 4 * i + 2 * j + 2] = jnp.sum(dy, 0, keepdims=True)
        g = dy * vec(gain, 2 * i + j)
        return inv * (
            g - jnp.mean(g, -1, keepdims=True) - hat * jnp.mean(g * hat, -1, keepdims=True)
        )

    def back_middle(i, ticket):
        dn2 = summed("s3", "r3", i, ticket)
        dafter = b["dz", i][m] + norm_back(b["af", i][...], dn2, i, 1)
        b["daf", i][...] = dafter
        b["da", i][m] = dafter.astype(BF)
        return gather_start(b["da", i])

    def with_class_row(rows, first):
        row = lax.broadcasted_iota(jnp.int32, (rows.shape[0], 1), 0)
        return jnp.where(row == 0, first, rows.astype(F32)).astype(BF)

    def rows_send(i, ticket):
        landed(*ticket)
        b["dh", i][...] = rows_of(b["da", i], i)
        u = UNIT_OF["qo", i]
        one = UNITS[u][2][0]
        s = new("s")

        @pl.when(place[one] != 3)
        def _():
            half = pl.ds(lax.rem(m, 2) * (SPANS[i] // 2), SPANS[i] // 2)
            send(b["dh", i].at[half], b["fc", u].at[place[one], half], s, at(**{one: 3}))

        @pl.when(place[one] == 3)
        def _():
            b["fc", u][3] = b["dh", i][...]

        factors["fc", u] = s

    def rows_forward(i):
        u = UNIT_OF["qo", i]
        one, fc, n = UNITS[u][2][0], b["fc", u], SPANS[i] // 2
        s0, s = factors["fc", u], new("s")
        core = lax.rem(m, 2)

        @pl.when(place[one] == 3)
        def _():
            wait(fc.at[pl.ds(0, 3), pl.ds(0, n)], rsem.at[s0])
            part = fc.at[pl.ds(0, 3), pl.ds(core * n, n)]
            send(part, part, s, (me, m + 1 - 2 * core))

        factors["fc", u] = (s0, s)

    def class_rows_send():
        b["dcb"][...] = b["dac"][...].astype(BF)
        for axis in "yz":
            dst, p = b["dc", axis], place[axis]
            s = new("s")
            for k in (1, 3, 2):
                t = lax.rem(p + k, 4)
                send(b["dcb"], dst.at[p], s, at(**{axis: t}))
            dst[p] = b["dcb"][...]
            factors["dc", axis] = (dst.at[pl.ds(0, 3)], s)

    def back_attend(i, ticket):
        span = SPANS[i]
        if i < 3:
            da = with_class_row(b["dh", i][...], b["dac"][i : i + 1])
        else:
            landed(*ticket)
            da = rows_of(b["da", i], i)
        b["svb"][4 * i + 1 : 4 * i + 2] = jnp.sum(da.astype(F32), 0, keepdims=True)
        dheads = nt(da, weight("wo", i)[...]).astype(BF)
        query, keys, values = b["q", i][...], b["k", i][...], b["v", i][...]
        probs = b["pr", i][...]
        d3 = stacked(dheads)
        dprob = nt(d3, values)
        dscore = probs * (dprob - jnp.sum(dprob * probs, -1, keepdims=True))
        dscore = dscore.astype(BF)
        dquery = (folded(nn(dscore, keys), span) * scale).astype(BF)
        dkeys = (tn(dscore, stacked(query)) * scale).astype(BF)
        dvalues = tn(probs.astype(BF), d3).astype(BF)
        wq = weight("wq", i)
        part = nn(dquery, wq[0:KD]) + nn(dkeys, wq[KD : 2 * KD]) + nn(dvalues, wq[2 * KD : 3 * KD])
        put_slabs("s4", i, part)
        ticket = scatter_start(b["s4", i], b["r4", i])
        b["svb"][4 * i + 3 : 4 * i + 4, 0:KD] = jnp.sum(dquery.astype(F32), 0, keepdims=True)
        b["svb"][4 * i + 3 : 4 * i + 4, 256 : 256 + KD] = jnp.sum(
            dvalues.astype(F32), 0, keepdims=True
        )
        if i < 3:
            b["pj4", i][0] = dquery
            b["pj4", i][1] = dkeys
            b["pj4", i][2] = dvalues
            b["pj4", i][3] = b["ho", i][...]
            share_rows("qo", i, "fa", lambda t: b["pj4", i].at[t])
            start_unit("qo", i)
            return ticket
        normed = rows_of(b["n1", i], i)
        put_unit("qo", 0, tn(dquery, normed))
        put_unit("qo", KD, tn(dkeys, normed))
        put_unit("qo", 2 * KD, tn(dvalues, normed))
        put_unit("qo", 3 * KD, tn(b["ho", i][...], da))
        store_global("qo")
        return ticket

    def back_finish(i, ticket):
        dn1 = summed("s4", "r4", i, ticket)
        dafter = b["daf", i][...]
        if i < 3:
            row = lax.broadcasted_iota(jnp.int32, (SLABS[i], 1), 0)
            dafter = jnp.where((row == 0) & (m == 0), b["dac"][i : i + 1], dafter)
        return dafter + norm_back(b["x", i][...], dn1, i, 0)

    def class_feed(dgin):
        dz = jnp.zeros((8, D), F32)
        slope = jnp.zeros((8, D), F32)
        for i in range(3):
            first = cot[OFFS[i] : OFFS[i] + 16].astype(F32)[0:1]
            dz = jnp.where(row8 == i, first + dgin[i : i + 1], dz)
            slope = jnp.where(row8 == i, b["dg", i][0:8][0:1], slope)
        dm = dz.astype(BF)
        dact = jnp.zeros((8, D), F32)
        for i in range(3):
            dact = jnp.where(row8 == i, nn(dm, b["dt", i][...]), dact)
        dinner = (slope * dact).astype(BF)
        dn2 = jnp.zeros((8, D), F32)
        for i in range(3):
            dn2 = jnp.where(row8 == i, nn(dinner, b["ut", i][...]), dn2)
        b["pc"][m] = dn2.astype(BF)
        ticket = gather_start(b["pc"])
        both = dm.astype(F32)
        dinner = dinner.astype(F32)
        for i in range(3):
            both = jnp.where(row8 == 3 + i, dinner[i : i + 1], both)
            b["svb"][4 * i : 4 * i + 1] += dz[i : i + 1]
            b["svb"][4 * i + 2 : 4 * i + 3] += dinner[i : i + 1]
        b["bc"][...] = both.astype(BF)
        b["dac"][...] = dz
        return ticket

    def right_over_z():
        py, px, pz = place["y"], place["x"], place["z"]
        s = new("s")
        for k in (1, 3, 2):
            send(b["bc"], b["bg"].at[py, px, pz], s, at(z=lax.rem(pz + k, 4)))
        b["bg"][py, px, pz] = b["bc"][...]
        return b["bg"].at[0, 0, pl.ds(0, 3)], s

    def right_over_y(ticket):
        landed(*ticket)
        own = b["bg"].at[place["y"], place["x"]]
        s = new("s")
        for k in (1, 3, 2):
            send(own, own, s, at(y=lax.rem(place["y"] + k, 4)))
        return b["bg"].at[pl.ds(0, 3), 0], s

    def right_over_x(ticket):
        landed(*ticket)
        own = b["bg"].at[:, place["x"]]
        s = new("s")
        send(own, own, s, at(x=1 - place["x"]))
        return own, s

    def class_middle(ticket):
        landed(*ticket)
        dn2 = b["pc"][0].astype(F32)
        for k in range(1, 4):
            dn2 = dn2 + b["pc"][k].astype(F32)
        hat, inv = layer_stats(b["afc"][0])
        lead = jnp.where(m == 0, 1.0, 0.0)
        scales = jnp.zeros((8, D), F32)
        for i in range(3):
            scales = jnp.where(row8 == i, vec(gain, 2 * i + 1), scales)
            b["sva"][4 * i + 2 : 4 * i + 3] += lead * (dn2 * hat)[i : i + 1]
            b["sva"][4 * i + 3 : 4 * i + 4] += lead * dn2[i : i + 1]
        g = dn2 * scales
        b["dac"][...] += inv * (
            g - jnp.mean(g, -1, keepdims=True) - hat * jnp.mean(g * hat, -1, keepdims=True)
        )

    def halves(ref):
        n = ref.shape[0] // 2
        return ref.at[pl.ds(0, n)], ref.at[pl.ds(n, n)]

    def ring_spread(axis, slot, own, like):
        p = place[axis]
        up, down = lax.rem(p + 1, 4), lax.rem(p + 3, 4)
        to_up, to_down = at(**{axis: up}), at(**{axis: down})
        s0, s1, s2, s3 = new("s"), new("s"), new("s"), new("s")
        send(own, slot(p), s0, to_up)
        send(own, slot(p), s1, to_down)
        yield
        landed(like, s0)
        part = halves(slot(down))[0]
        send(part, part, s2, to_up)
        landed(like, s1)
        part = halves(slot(up))[1]
        send(part, part, s3, to_down)
        yield
        landed(halves(like)[0], s2)
        landed(halves(like)[1], s3)

    def sum_unit(u):
        name, view, (one, two) = UNITS[u]
        span = SPANS[view]
        g, near, gx, ga = b["g", u], b["near", u], b["gx", u], b["ga", u]
        p1, p2 = place[one], place[two]
        out = outs[name].at[view]
        yield
        landed(*factors["fa", u])
        landed(*factors["fb", u])

        def multiply(rows):
            left = b["fa", u][...].reshape(4 * span, KD)
            g[...] = tn(left, rows).astype(BF).reshape(4, 48, D)

        if name == "qo":
            s_da, s_core = factors["fc", u]
            n = span // 2
            fc = b["fc", u]
            if ("dc", one) in factors:
                landed(*factors.pop(("dc", one)))

            @pl.when(p1 == 3)
            def _():
                wait(fc.at[pl.ds(0, 3), pl.ds(0, n)], rsem.at[s_core])
                first = b["dc", one][...].astype(F32)
                multiply(
                    jnp.concatenate(
                        [with_class_row(fc[k], first[k, view : view + 1]) for k in range(4)], 0
                    )
                )

            @pl.when(p1 != 3)
            def _():
                multiply(b["fb", u][...].reshape(4 * span, D))

            def drain():
                @pl.when(p1 != 3)
                def _():
                    wait(fc.at[0, pl.ds(0, n)], ssem.at[s_da])

                @pl.when(p1 == 3)
                def _():
                    wait(fc.at[pl.ds(0, 3), pl.ds(0, n)], ssem.at[s_core])

            drains.append(drain)
        else:
            multiply(b["fb", u][...].reshape(4 * span, D))
        s = new("s")
        for k in (1, 3, 2):
            t = lax.rem(p2 + k, 4)
            send(g.at[t], near.at[k - 1], s, at(**{two: t}))
        yield
        landed(near, s)
        total = g[p2].astype(F32)
        for k in range(3):
            total = total + near[k].astype(F32)
        ga[p2] = total.astype(BF)
        s = new("s")
        send(ga.at[p2], gx, s, at(x=1 - place["x"]))
        yield
        landed(gx, s)
        wait(gx, ssem.at[s])
        drains.pop()
        ga[p2] = (ga[p2].astype(F32) + gx[...].astype(F32)).astype(BF)
        s = new("s")
        for k in (1, 3, 2):
            send(ga.at[p2], ga.at[p2], s, at(**{two: lax.rem(p2 + k, 4)}))
        yield
        landed(ga.at[pl.ds(0, 3)], s)
        own = out.at[pl.ds(p1 * 4, 4)]
        store(ga, own)
        yield from ring_spread(one, lambda t: out.at[pl.ds(t * 4, 4)], ga, out.at[pl.ds(0, 4)])

    stores = []

    def store(src, dst):
        copy = pltpu.make_async_copy(src, dst, lsem.at[new("l")])
        copy.start()
        stores.append(copy)

    running = []

    def store_global(name):
        store(b["go"].at[OUT_OF[name]], outs[name].at[3])

    def start_unit(name, i):
        unit = sum_unit(UNIT_OF[name, i])
        next(unit)
        running.append(unit)

    def tick(n):
        for _ in range(min(n, len(running))):
            unit = running.pop(0)
            if next(unit, "end") != "end":
                running.append(unit)

    tickets = [None] * 3
    back = [None] * 3
    for i in range(3):
        b["n1", i][m] = norm(b["x", i][...], i, 0).astype(BF)
        tickets[i] = gather_start(b["n1", i])
    for i in range(3):
        landed(*tickets[i])
        tickets[i] = attend(i)
    for i in range(3):
        tickets[i] = middle(i, tickets[i])
    firsts = jnp.zeros((8, D), F32)
    for i in range(3):
        firsts = jnp.where(row8 == i, b["af", i][0:8][0:1], firsts)
    b["afc"][m] = firsts
    after_ticket = gather_start(b["afc"])
    parts = jnp.zeros((8, D), F32)
    for i in range(3):
        parts = jnp.where(row8 == i, feed(i, tickets[i]), parts)
    b["zc"][m] = parts.astype(BF)
    ticket = gather_start(b["zc"])
    back_feed(0)
    landed(*after_ticket)
    classes = b["afc"][0]
    for i in range(3):
        classes = jnp.where(row8 == i, classes + vec(b_down, i), classes)
    landed(*ticket)
    for k in range(4):
        classes = classes + b["zc"][k].astype(F32)
    for i in range(3):
        classes = jnp.where(row8 == 3 + i, b["n2", i][0].astype(F32)[0:1], classes)
    b["cl"][...] = classes.astype(BF)
    class_ticket = dp_gather_start(b["cl"], b["cg"])
    for i in range(3):
        tickets[i] = feed_send(i)
    back[0] = back_feed_send(0)
    for i in (1, 2):
        back_feed(i)
        back[i] = back_feed_send(i)
    tick(TICKS[0])

    landed(*class_ticket)
    gathered = rows8_at(b["cg"], 6)
    gin = gathered[0:96]
    b["n20"][...] = gathered[96:192].astype(BF)
    b["gin"][...] = gin.reshape(4, 24, D)
    b["x", 3][...] = b["gin"][m]
    put_slabs("n1", 3, norm(gin, 3, 0))
    ticket = attend(3)
    landed(*cot_ticket)
    b["dz", 3][...] = rows8_at(b["ct"], 3).reshape(4, 24, D)
    tick(TICKS[1])
    ticket = middle(3, ticket)
    for i in range(3):
        tickets[i] = finish(i, tickets[i])
    tick(TICKS[2])
    glob_ticket = feed(3, ticket)
    ticket = back_feed(3)
    back[0] = back_middle(0, back[0])
    tick(TICKS[3])
    ticket = back_middle(3, ticket)
    for i in (1, 2):
        back[i] = back_middle(i, back[i])
    tick(TICKS[4])
    ticket = back_attend(3, ticket)
    for i in range(3):
        rows_send(i, back[i])
    tick(TICKS[5])
    dx = back_finish(3, ticket)
    o_at = lax.broadcasted_iota(jnp.int32, (8, 24), 0)
    w_at = lax.broadcasted_iota(jnp.int32, (8, 24), 1) + m * 24
    chosen = ((w_at == o_at * 32 + me) & (o_at < 3)).astype(F32).astype(BF)
    b["gdx"][m] = nn(chosen, dx.astype(BF)).astype(BF)
    ticket = gather_start(b["gdx"])
    glob_ticket = finish(3, glob_ticket)
    o_at = lax.broadcasted_iota(jnp.int32, (8, 96), 0)
    w_at = lax.broadcasted_iota(jnp.int32, (8, 96), 1)
    mine = ((w_at == o_at * 32 + me) & (o_at < 3)).astype(F32).astype(BF)
    tick(TICKS[6])
    landed(*ticket)
    dgin = b["gdx"][0].astype(F32)
    for k in range(1, 4):
        dgin = dgin + b["gdx"][k].astype(F32)

    ticket = class_feed(dgin)
    right_ticket = right_over_z()
    for i in range(3):
        rows_forward(i)
    for i in range(3):
        landed(*tickets[i])
        out_tok[OFFS[i] : OFFS[i] + SPANS[i]] = rows_of(b["zo", i], i)
    landed(*glob_ticket)
    out_glob[...] = nn(mine, rows_of(b["zo", 3], 3)).astype(BF)
    tick(TICKS[7])
    class_middle(ticket)
    class_rows_send()
    for i in range(3):
        tickets[i] = back_attend(i, None)
    right_ticket = right_over_y(right_ticket)
    tick(TICKS[8])
    for i in range(3):
        dx = back_finish(i, tickets[i])
        base = (0, 4, 6)[i]
        for r in range(SLABS[i] // 8):
            rows = dx[8 * r : 8 * r + 8]
            b["mx"][base + r] = lam * rows
            b["ts"][base + r] = ((1.0 - lam) * rows).astype(BF)
    right_ticket = right_over_x(right_ticket)
    def invert(d, _):
        found = jnp.int32(0)
        for c in range(CLIPS):
            found = jnp.where(partner[c] == d, c, found)
        b["inv"][d] = found
        return 0

    lax.fori_loop(0, CLIPS, invert, 0)
    s = deal_start(1, lambda r: b["ts"].at[r])

    s_mp = new("s")
    for k in (2, 1, 3):
        send(b["sva"], b["svr"].at[k - 1], s_mp, (me, lax.rem(m + k, 4)))
    tick(TICKS[9])
    t = deal_turn(1, s, b["inv"])
    tick(TICKS[10])
    landed(b["svr"], s_mp)
    sva = b["sva"][...] + b["svr"][0] + b["svr"][1] + b["svr"][2]
    svb = b["svb"][...]
    b["svs", 0][...] = jnp.concatenate([sva, svb], 0).astype(BF)

    def small_start(step, axis):
        s = new("s")
        far = (1, 3, 2) if axis != "x" else (1,)
        size = 4 if axis != "x" else 2
        for k in far:
            dev = at(**{axis: lax.rem(place[axis] + k, size)})
            send(b["svs", step], b["svt", step].at[k - 1], s, dev)
        return b["svt", step].at[pl.ds(0, len(far))], s

    def small_end(step, ticket, axis):
        landed(*ticket)
        total = b["svs", step][...].astype(F32)
        for k in range(3 if axis != "x" else 1):
            total = total + b["svt", step][k].astype(F32)
        return total

    ticket = small_start(0, "y")
    taken = deal_end(1, t)
    for i in range(3):
        base = (0, 4, 6)[i]
        for r in range(SLABS[i] // 8):
            rows = b["mx"][base + r] + taken[base + r]
            b["gt", i][m, 8 * r : 8 * r + 8] = rows.astype(BF)
        tickets[i] = gather_start(b["gt", i])
    tick(TICKS[11])
    b["svs", 1][...] = small_end(0, ticket, "y").astype(BF)
    ticket = small_start(1, "z")
    tick(TICKS[12])
    for i in range(3):
        landed(*tickets[i])
        out_grad[OFFS[i] : OFFS[i] + SPANS[i]] = rows_of(b["gt", i], i)
    b["svs", 2][...] = small_end(1, ticket, "z").astype(BF)
    ticket = small_start(2, "x")
    landed(*right_ticket)
    for i in range(3):
        rows = b["n20"][CLIPS * i : CLIPS * i + CLIPS]
        active, _ = gelu(nn(rows, weight("wu", i)[...]) + vec(b_up, i))
        out_left[CLIPS * i : CLIPS * i + CLIPS] = active
    out_left[3 * CLIPS : 6 * CLIPS] = b["n20"][...]
    out_right[...] = rows8_at(b["bg"], 6).astype(BF)
    tick(TICKS[13])
    total = small_end(2, ticket, "x")
    out_small[0:12] = total[0:12]
    out_small[12:16] = sva[12:16]
    out_small[16:28] = total[16:28]
    out_small[28:32] = svb[12:16]
    while running:
        tick(1)
    for drain in drains:
        drain()
    for copy in stores:
        copy.wait()


def shards(
    tokens,
    lengths,
    partner,
    mix_coef,
    norm_gain,
    norm_bias,
    w_qkv,
    b_qv,
    w_out,
    b_out,
    w_up,
    b_up,
    w_down,
    b_down,
    cot_tokens,
    cot_global,
):
    wq = jnp.transpose(w_qkv, (0, 2, 3, 1)).reshape(4, 3 * KD, D)
    plan = scratch_plan()
    names = list(plan)
    smem = pl.BlockSpec(memory_space=pltpu.SMEM)
    vmem = pl.BlockSpec(memory_space=pltpu.VMEM)
    hbm = pl.BlockSpec(memory_space=pl.ANY)
    unit = jax.ShapeDtypeStruct((4, 16, 48, D), BF)
    out_tok, out_glob, out_grad, small, left, right, qo, up, down = pl.pallas_call(
        functools.partial(kernel, names),
        out_shape=(
            jax.ShapeDtypeStruct((224, D), BF),
            jax.ShapeDtypeStruct((8, D), BF),
            jax.ShapeDtypeStruct((224, D), BF),
            jax.ShapeDtypeStruct((32, D), F32),
            jax.ShapeDtypeStruct((6 * CLIPS, D), BF),
            jax.ShapeDtypeStruct((6 * CLIPS, D), BF),
            unit,
            unit,
            unit,
        ),
        in_specs=[smem] * 3 + [vmem] * 9 + [hbm] * 4,
        out_specs=(vmem,) * 6 + (hbm,) * 3,
        scratch_shapes=list(plan.values()),
        compiler_params=pltpu.CompilerParams(
            collective_id=0, has_side_effects=True, vmem_limit_bytes=60 * 2**20
        ),
    )(
        partner,
        mix_coef,
        lengths,
        tokens.reshape(28, 8, D),
        cot_tokens[0],
        cot_global,
        norm_gain,
        norm_bias,
        b_out,
        b_down,
        b_up,
        b_qv,
        wq,
        w_out,
        w_up,
        w_down,
    )
    out_tok, out_glob, out_grad, gain, shift, qkv, qv, out, bout, ups, bup, downs, bdown = widen(
        out_tok,
        out_glob,
        out_grad,
        small,
        left,
        right,
        *(a.reshape(4, D, D) for a in (qo, up, down)),
    )
    return (
        out_tok,
        out_glob,
        out_grad,
        gain,
        shift,
        jnp.transpose(qkv.reshape(4, 3, KD, D), (0, 3, 1, 2)),
        qv,
        out,
        bout,
        ups,
        bup,
        downs,
        bdown,
    )


def widen_kernel(*refs):
    tok, glob, grad, small, left, right, qo, up, down = refs[:9]
    o_tok, o_glob, o_grad, o_gain, o_shift, o_qkv, o_qv, o_out, o_bout, o_up, o_bup, o_down, o_bdown = refs[9:22]
    held, wide, sem_in, sem_out = refs[22:]
    order = [(i, a) for i in (3, 0, 1, 2) for a in range(3)]
    fetches = []
    for n, (i, a) in enumerate(order):
        copy = pltpu.make_async_copy((qo, up, down)[a].at[i], held.at[n], sem_in.at[n])
        copy.start()
        fetches.append(copy)
    o_tok[0] = tok[...]
    o_grad[0] = grad[...]
    o_glob[0] = glob[0:3]
    m = lax.axis_index("mp")

    def share(row):
        value = small[row : row + 1]
        mine = value[:, 0:KD]
        for k in range(1, 4):
            mine = jnp.where(m == k, value[:, k * KD : (k + 1) * KD], mine)
        return mine

    for i in range(4):
        for j in range(2):
            o_gain[i, j : j + 1] = share(4 * i + 2 * j)
            o_shift[i, j : j + 1] = share(4 * i + 2 * j + 1)
        row = 16 + 4 * i
        o_bdown[i : i + 1] = share(row)
        o_bout[i : i + 1] = share(row + 1)
        o_bup[i : i + 1] = small[row + 2 : row + 3]
        o_qv[i, 0:1] = small[row + 3 : row + 4, 0:KD]
        o_qv[i, 1:2] = small[row + 3 : row + 4, 256 : 256 + KD]
    slots = wide.shape[0]
    busy = [[] for _ in range(slots)]
    for n, (i, a) in enumerate(order):
        slot = n % slots
        fetches[n].wait()
        for copy in busy[slot]:
            copy.wait()
        value = held[n].astype(F32)
        if a > 0 and i < 3:
            base = CLIPS * (3 * (a == 1) + i)
            rows, cols = (right, left) if a == 1 else (left, right)
            value = value + tn(rows[base : base + CLIPS], cols[base : base + CLIPS])
        wide[slot] = value.T if a == 1 else value
        src = wide.at[slot]
        if a == 0:
            pairs = (
                (src.at[pl.ds(0, 3 * KD)], o_qkv.at[i]),
                (src.at[pl.ds(3 * KD, KD)], o_out.at[i]),
            )
        else:
            pairs = ((src, (o_up, o_down)[a - 1].at[i]),)
        busy[slot] = []
        for k, (part, dst) in enumerate(pairs):
            copy = pltpu.make_async_copy(part, dst, sem_out.at[slot, k])
            copy.start()
            busy[slot].append(copy)
    for copies in busy:
        for copy in copies:
            copy.wait()


def widen(tok, glob, grad, small, left, right, qo, up, down):
    shape = jax.ShapeDtypeStruct
    vmem = pl.BlockSpec(memory_space=pltpu.VMEM)
    hbm = pl.BlockSpec(memory_space=pl.ANY)
    return pl.pallas_call(
        widen_kernel,
        in_specs=[vmem] * 6 + [hbm] * 3,
        out_specs=[vmem, vmem, vmem, vmem, vmem, hbm, vmem, hbm, vmem, hbm, vmem, hbm, vmem],
        out_shape=[shape((1, 224, D), BF), shape((1, 3, D), BF), shape((1, 224, D), BF)]
        + [shape((4, 2, KD), F32), shape((4, 2, KD), F32), shape((4, 3 * KD, D), F32)]
        + [shape((4, 2, KD), F32), shape((4, KD, D), F32), shape((4, KD), F32)]
        + [shape((4, D, D), F32), shape((4, D), F32), shape((4, D, D), F32), shape((4, KD), F32)],
        scratch_shapes=[
            pltpu.VMEM((12, D, D), BF),
            pltpu.VMEM((5, D, D), F32),
            pltpu.SemaphoreType.DMA((12,)),
            pltpu.SemaphoreType.DMA((5, 2)),
        ],
        compiler_params=pltpu.CompilerParams(vmem_limit_bytes=60 * 2**20),
    )(tok, glob, grad, small, left, right, qo, up, down)


def solution(mesh):
    placed = (
        P("dp", None, None),
        P("dp", None),
        P(),
        P(),
        P(),
        P(),
        P(None, None, None, "mp"),
        P(None, None, "mp"),
        P(None, "mp", None),
        P(),
        P(None, None, "mp"),
        P(None, "mp"),
        P(None, "mp", None),
        P(),
        P("dp", None, None),
        P("dp", None, None),
    )
    return jax.shard_map(
        shards,
        mesh=mesh,
        in_specs=placed,
        out_specs=(
            P("dp", None, None),
            P("dp", None, None),
            P("dp", None, None),
            P(None, None, "mp"),
            P(None, None, "mp"),
            P(None, None, None, "mp"),
            P(None, None, "mp"),
            P(None, "mp", None),
            P(None, "mp"),
            P(None, None, "mp"),
            P(None, "mp"),
            P(None, "mp", None),
            P(None, "mp"),
        ),
        check_vma=False,
    )
```
